32 devices in a mesh: batch: 8 (over y, x, core), blk: 4 (over z).
Axes of the slice: x: 2, y: 2, z: 4, core: 2. Of those that a mesh axis runs over, the one named last changes fastest.
Arguments:
- decoder_input: bfloat16 [16, 1024, 512], P('batch', 'blk'), may hold values from -6 to 6
- encoder_output: bfloat16 [16, 1024, 512], P('batch', 'blk'), may hold values from -6 to 6
- sequence_lengths: int32 [16], P('batch'), may hold values from 256 to 1024, as said below
- chain_breaks: int32 [16, 4], P('batch'), may hold values from 1 to 1022, as said below
- self_inward: bfloat16 [512, 1536], replicated, may hold values from -0.25 to 0.25
- self_outward: bfloat16 [512, 512], replicated, may hold values from -2 to 2
- cross_query: bfloat16 [512, 512], replicated, may hold values from -0.25 to 0.25
- cross_memory: bfloat16 [512, 1024], replicated, may hold values from -0.25 to 0.25
- cross_outward: bfloat16 [512, 512], replicated, may hold values from -4 to 4
- feed_up: bfloat16 [512, 2048], replicated, may hold values from -0.25 to 0.25
- feed_up_bias: bfloat16 [2048], replicated, may hold values from -4 to 4
- feed_down: bfloat16 [2048, 512], replicated, may hold values from -0.125 to 0.125
- feed_down_bias: bfloat16 [512], replicated, may hold values from -4 to 4
- norm_gains: float32 [3, 512], replicated, may hold values from 0.5 to 1.5
- norm_shifts: float32 [3, 512], replicated, may hold values from -3 to 3
- output_cotangent: bfloat16 [16, 1024, 512], P('batch', 'blk'), may hold values from -6 to 6
Outputs:
- layer_output: bfloat16 [16, 1024, 512], P('batch', 'blk')
- input_gradient: float32 [16, 1024, 512], P('batch', 'blk')
- encoder_gradient: float32 [16, 1024, 512], P('batch', 'blk')
- self_inward_gradient: float32 [512, 1536], replicated
- self_outward_gradient: float32 [512, 512], replicated
- cross_query_gradient: float32 [512, 512], replicated
- cross_memory_gradient: float32 [512, 1024], replicated
- cross_outward_gradient: float32 [512, 512], replicated
- feed_up_gradient: float32 [512, 2048], replicated
- feed_up_bias_gradient: float32 [2048], replicated
- feed_down_gradient: float32 [2048, 512], replicated
- feed_down_bias_gradient: float32 [512], replicated
- norm_gains_gradient: float32 [3, 512], replicated
- norm_shifts_gradient: float32 [3, 512], replicated
The draws below stay inside these ranges and needn't reach their ends.
Inputs may be any that keep to these rules, and one draw needn't show every extreme that they name: `sequence_lengths`: in each group of 2 sequences that share an index of batch, one has length 1024; the others have a quarter of 1024 or more, and one of them exactly that. `chain_breaks`: each position lies from 1 to its sequence's length minus 2; positions may repeat.
All inputs are finite; a program needn't handle non-finite values.
Results may differ from the reference program's by a relative error of at most 0.019.
Values may be sent and summed in bfloat16 or wider, within the bound.
No kernel may reach another device: no remote copies, remote signals or barrier semaphores. Data moves between devices by JAX's collectives and lax.ppermute only.
A program may use at most 384 MiB of HBM per device.

```python
import jax
import jax.numpy as jnp
from jax import lax

D = 512
HEADS = 8
HEAD = 64
FF = 2048
SEQS_DEV = 2
BREAKS = 4
LENGTH = 1024
SEQS = 16


def length_law(key):
    groups = SEQS // SEQS_DEV
    spread = jax.random.randint(jax.random.fold_in(key, 1), (groups, SEQS_DEV), LENGTH // 4, LENGTH + 1)
    longest = jax.random.randint(jax.random.fold_in(key, 2), (groups, 1), 0, SEQS_DEV)
    places = jnp.arange(SEQS_DEV, dtype=jnp.int32)[None, :]
    shortest = (longest + 1) % SEQS_DEV
    spread = jnp.where(places == shortest, LENGTH // 4, spread)
    spread = jnp.where(places == longest, LENGTH, spread)
    return spread.reshape(SEQS).astype(jnp.int32)


def draw_sequence_lengths(key, part):
    return length_law(key)


def draw_chain_breaks(key, part):
    lengths = length_law(key)
    key = jax.random.fold_in(key, 5)
    raw = jax.random.randint(key, (SEQS, BREAKS), 0, 1 << 20)
    breaks = 1 + raw % (lengths[:, None] - 2)
    column = jnp.arange(BREAKS, dtype=jnp.int32)[None, :]
    full = lengths[:, None] == LENGTH
    breaks = jnp.where(full & (column == 0), 1, breaks)
    breaks = jnp.where(full & (column == 1), LENGTH - 2, breaks)
    return breaks.astype(jnp.int32)


def block_scale(own_key, dims, split, least, high):
    factor_of = 1.0
    for dim, shards_of in split:
        heights = jax.random.uniform(jax.random.fold_in(jax.random.fold_in(own_key, 6), dim), (shards_of,), jnp.float32, least / len(split), high / len(split))
        factor_of = factor_of * jnp.repeat(jnp.exp(heights), dims[dim] // shards_of).reshape((-1,) + (1,) * (len(dims) - 1 - dim))
    return factor_of


def bell_draw(stream_key, dims, scale, reach, shards=(), held_as=jnp.bfloat16):
    level = block_scale(stream_key, dims, shards, -0.22, 0.18) if shards else 1.0
    array = jax.random.normal(stream_key, dims, jnp.float32) * scale * level
    return jnp.minimum(jnp.maximum(array, -reach), reach).astype(held_as)


def setup_inputs(seed: int = 0) -> dict:
    streams_of = jax.random.split(jax.random.key(seed), 17)
    return {
        "decoder_input": bell_draw(streams_of[0], (SEQS, LENGTH, D), 1.0, 6.0, ((0, 8), (1, 4))),
        "encoder_output": bell_draw(streams_of[1], (SEQS, LENGTH, D), 1.0, 6.0, ((0, 8), (1, 4))),
        "sequence_lengths": draw_sequence_lengths(jax.random.fold_in(streams_of[16], 71), 0),
        "chain_breaks": draw_chain_breaks(jax.random.fold_in(streams_of[16], 71), 0),
        "self_inward": bell_draw(streams_of[4], (D, 3 * D), D ** -0.5, 0.25),
        "self_outward": bell_draw(streams_of[5], (D, D), (max(1, D // 64)) ** -0.5, 2.0),
        "cross_query": bell_draw(streams_of[6], (D, D), D ** -0.5, 0.25),
        "cross_memory": bell_draw(streams_of[7], (D, 2 * D), D ** -0.5, 0.25),
        "cross_outward": bell_draw(streams_of[8], (D, D), (max(2, D // 256)) ** -0.5, 4.0),
        "feed_up": bell_draw(streams_of[9], (D, FF), D ** -0.5, 0.25),
        "feed_up_bias": bell_draw(streams_of[10], (FF,), 0.3, 4.0),
        "feed_down": bell_draw(streams_of[11], (FF, D), FF ** -0.5, 0.125),
        "feed_down_bias": bell_draw(streams_of[12], (D,), 0.3, 4.0),
        "norm_gains": jnp.clip(1.0 + 0.1 * jax.random.normal(streams_of[13], (3, D), jnp.float32), 0.5, 1.5),
        "norm_shifts": bell_draw(streams_of[14], (3, D), 0.2, 3.0, (), jnp.float32),
        "output_cotangent": bell_draw(streams_of[15], (SEQS, LENGTH, D), 1.0, 6.0, ((0, 8), (1, 4))),
    }


@jax.custom_vjp
def low(v):
    return lax.optimization_barrier(v.astype(jnp.bfloat16)).astype(jnp.float32)

@jax.custom_vjp
def low_back(v):
    return v

def low_keep(v):
    return (low(v), None)

def low_pass(kept, grad):
    return (grad,)

def back_keep(v):
    return (v, None)

def back_low(kept, grad):
    return (low(grad),)
low.defvjp(low_keep, low_pass)
low_back.defvjp(back_keep, back_low)
EPSILON = 1e-05

def layer_norm(values, gain, shift):
    center = values - lax.optimization_barrier(jnp.mean(values, axis=-1, keepdims=True))
    spread = lax.optimization_barrier(jnp.mean(center * center, axis=-1, keepdims=True))
    return center * lax.rsqrt(spread + EPSILON) * gain + shift

def product(left, right):
    return jnp.dot(left, right, precision=lax.Precision.HIGHEST, preferred_element_type=jnp.float32)

def attend(queries, keys, values, allowed, causal):
    block = min(512, LENGTH)
    blocks = LENGTH // block
    scale = HEAD ** (-0.5)
    split_queries = queries.reshape(blocks, block, HEADS, HEAD)
    keys = keys.reshape(LENGTH, HEADS, HEAD)
    values = values.reshape(LENGTH, HEADS, HEAD)
    places = jnp.arange(LENGTH, dtype=jnp.int32)

    def one_block(inputs):
        rows, first = inputs
        scores = low_back(jnp.einsum('qhe,khe->hqk', rows, keys, precision=lax.Precision.HIGHEST) * scale)
        usable = jnp.broadcast_to(allowed[None, :], (block, LENGTH))
        if causal:
            usable = usable & (places[None, :] <= first + jnp.arange(block, dtype=jnp.int32)[:, None])
        scores = jnp.where(usable[None], scores, -jnp.inf)
        weights = jax.nn.softmax(scores, axis=-1)
        return jnp.einsum('hqk,khe->qhe', weights, values, precision=lax.Precision.HIGHEST)
    firsts = jnp.arange(blocks, dtype=jnp.int32) * block
    return lax.map(jax.checkpoint(one_block), (split_queries, firsts)).reshape(LENGTH, HEADS * HEAD)

def decoder_layer(hidden, memory, allowed_self, allowed_cross, weights):
    self_inward, self_outward, cross_query, cross_memory, cross_outward, feed_up, feed_up_bias, feed_down, feed_down_bias, norm_gains, norm_shifts = weights
    first_norm = layer_norm(hidden, norm_gains[0], norm_shifts[0])
    triple = product(low(first_norm), self_inward)
    self_asking = low(low_back(triple[:, :D]))
    self_pairs = low(triple[:, D:])
    self_mix = attend(self_asking, self_pairs[:, :D], self_pairs[:, D:], allowed_self, True)
    after_self = hidden + low_back(product(low(low_back(self_mix)), self_outward))
    second_norm = layer_norm(after_self, norm_gains[1], norm_shifts[1])
    asking = low(low_back(product(low(second_norm), cross_query)))
    pairs = low(product(low(memory), cross_memory))
    cross_mix = attend(asking, pairs[:, :D], pairs[:, D:], allowed_cross, False)
    after_cross = after_self + low_back(product(low(low_back(cross_mix)), cross_outward))
    third_norm = layer_norm(after_cross, norm_gains[2], norm_shifts[2])
    rising = low_back(product(low(third_norm), feed_up)) + feed_up_bias
    active = jax.nn.gelu(rising, approximate=False)
    return after_cross + low_back(product(low(active), feed_down)) + feed_down_bias

def reference(decoder_input, encoder_output, sequence_lengths, chain_breaks, self_inward, self_outward, cross_query, cross_memory, cross_outward, feed_up, feed_up_bias, feed_down, feed_down_bias, norm_gains, norm_shifts, output_cotangent):
    weights = tuple((w.astype(jnp.float32) for w in (self_inward, self_outward, cross_query, cross_memory, cross_outward, feed_up, feed_up_bias, feed_down, feed_down_bias, norm_gains, norm_shifts)))
    places = jnp.arange(LENGTH, dtype=jnp.int32)

    def one_sequence(totals, inputs):
        hidden, memory, length, breaks, cotangent = inputs
        inside = places < length
        linker = jnp.any(places[:, None] == breaks[None, :], axis=1)

        def layer(hidden, memory, *parameters):
            return decoder_layer(hidden, memory, inside, inside & jnp.logical_not(linker), parameters)
        output, pullback = jax.vjp(layer, hidden, memory, *weights)
        gradients = pullback(cotangent)
        totals = tuple((t + g for t, g in zip(totals, gradients[2:])))
        return (totals, (output.astype(jnp.bfloat16), gradients[0], gradients[1]))
    start = tuple((jnp.zeros_like(w) for w in weights))
    totals, (outputs, input_grads, encoder_grads) = lax.scan(one_sequence, start, (decoder_input.astype(jnp.float32), encoder_output.astype(jnp.float32), sequence_lengths, chain_breaks, output_cotangent.astype(jnp.float32)))
    return (outputs, input_grads, encoder_grads, totals[0], totals[1], totals[2], totals[3], totals[4], totals[5], totals[6], totals[7], totals[8], totals[9], totals[10])
```

```python
import functools

import jax
import jax.numpy as jnp
from jax import lax
from jax.experimental import pallas as pl
from jax.experimental.pallas import tpu as pltpu
from jax.sharding import PartitionSpec as P

HEAD = 64
PAIR = 2 * HEAD
EPSILON = 1e-05
FAR = 1e30
LOW = jnp.bfloat16
WIDE = jnp.float32


def contract(left, right, a, b):
    return lax.dot_general(left, right, (((a,), (b,)), ((), ())), preferred_element_type=WIDE)


def nn(left, right):
    return contract(left, right, 1, 0)


def nt(left, right):
    return contract(left, right, 1, 1)


def tn(left, right):
    return contract(left, right, 0, 0)


def standard(values):
    center = values - jnp.mean(values, axis=-1, keepdims=True)
    spread = jnp.mean(center * center, axis=-1, keepdims=True)
    inverse = lax.rsqrt(spread + EPSILON)
    return center * inverse, inverse


def norm_back(values, gain, upstream):
    unit, inverse = standard(values)
    m = upstream * gain
    grad = inverse * (
        m
        - jnp.mean(m, axis=-1, keepdims=True)
        - unit * jnp.mean(m * unit, axis=-1, keepdims=True)
    )
    return grad, jnp.sum(upstream * unit, axis=0), jnp.sum(upstream, axis=0)


def gelu_pair(x):
    z = jnp.abs(x) * 0.7071067811865476
    t = 1.0 / (1.0 + 0.5 * z)
    poly = 0.17087277
    for c in (
        -0.82215223,
        1.48851587,
        -1.13520398,
        0.27886807,
        -0.18628806,
        0.09678418,
        0.37409196,
        1.00002368,
        -1.26551223,
    ):
        poly = poly * t + c
    bell = jnp.exp(-z * z)
    tail = 0.5 * t * jnp.exp(poly) * bell
    share = jnp.where(x >= 0, 1.0 - tail, tail)
    return x * share, share + x * bell * 0.3989422804014327


def by_head(pair_rows):
    lane = lax.broadcasted_iota(jnp.int32, pair_rows.shape, 1)
    zero = jnp.zeros_like(pair_rows)
    return jnp.concatenate(
        [jnp.where(lane < HEAD, pair_rows, zero), jnp.where(lane >= HEAD, pair_rows, zero)], axis=0
    )


def own_parts(both):
    rows = both.shape[1] // 2
    return jnp.concatenate([both[:HEAD, :rows], both[HEAD:, rows:]], axis=0)


def attend(q_ref, kv_ref, p_ref, mixed_ref, inverse_ref, plan, mask):
    rows = q_ref.shape[0] // 2
    width = q_ref.shape[1]
    for pair in range(width // PAIR):
        lanes = slice(pair * PAIR, (pair + 1) * PAIR)
        values = slice(width + pair * PAIR, width + (pair + 1) * PAIR)
        spot = slice(pair * 2 * rows, (pair + 1) * 2 * rows)
        for seq, blocks in enumerate(plan):
            mine = slice(seq * rows, (seq + 1) * rows)
            queries = by_head(q_ref[mine, lanes])
            scores, tops = [], []
            for block in blocks:
                s = nt(kv_ref[block * rows : (block + 1) * rows, lanes], queries)
                s, far = mask(block, s)
                scores.append((s, far))
                tops.append(jnp.max(s, axis=0, keepdims=True) - far)
            top = functools.reduce(jnp.maximum, tops)
            total = jnp.zeros_like(top)
            mixed = jnp.zeros((PAIR, 2 * rows), WIDE)
            for block, (s, far) in zip(blocks, scores):
                at = slice(block * rows, (block + 1) * rows)
                p = jnp.exp(s - (top + far))
                total = total + jnp.sum(p, axis=0, keepdims=True)
                p = p.astype(LOW)
                p_ref[at, spot] = p
                mixed = mixed + tn(kv_ref[at, values], p)
            inverse = 1.0 / total
            mixed_ref[mine, lanes] = own_parts(mixed * inverse).T
            inverse_ref[mine, lanes] = own_parts(jnp.broadcast_to(inverse, mixed.shape)).T


def attend_back(up, mixed_ref, inverse_ref, q_ref, kv_ref, p_ref, dq_ref, dkv_ref, plan):
    rows = q_ref.shape[0] // 2
    width = q_ref.shape[1]
    scale = HEAD ** (-0.5)
    for pair in range(width // PAIR):
        lanes = slice(pair * PAIR, (pair + 1) * PAIR)
        values = slice(width + pair * PAIR, width + (pair + 1) * PAIR)
        spot = slice(pair * 2 * rows, (pair + 1) * 2 * rows)
        for seq, blocks in enumerate(plan):
            mine = slice(seq * rows, (seq + 1) * rows)
            queries = by_head(q_ref[mine, lanes])
            scaled = up[mine, lanes] * inverse_ref[mine, lanes]
            inner = (scaled * mixed_ref[mine, lanes]).T
            offset = jnp.concatenate(
                [
                    jnp.sum(inner[:HEAD], axis=0, keepdims=True),
                    jnp.sum(inner[HEAD:], axis=0, keepdims=True),
                ],
                axis=1,
            )
            upper = by_head(scaled.astype(LOW))
            dq = jnp.zeros((PAIR, 2 * rows), WIDE)
            for block in blocks:
                at = slice(block * rows, (block + 1) * rows)
                p = p_ref[at, spot]
                dp = nt(kv_ref[at, values], upper)
                ds = (p.astype(WIDE) * (dp - offset)).astype(LOW)
                dkv_ref[at, values] = nn(p, upper).astype(LOW)
                dkv_ref[at, lanes] = nn(ds, queries).astype(LOW)
                dq = dq + tn(kv_ref[at, lanes], ds)
            dq_ref[mine, lanes] = (own_parts(dq).T * scale).astype(LOW)


def plan_of(n):
    return (tuple(range(n)), tuple(range(n, n + n // 4)))


def self_kernel(
    n, order, rank, x, xl, xs, w_in, w_out, w_cq, gains, shifts,
    q, kv, p, mixed, inverse, after, cq, n1,
):
    rows, width = x.shape[1:]
    r = rank[0]

    def first_norm(v):
        return (standard(v.astype(WIDE))[0] * gains[0:1] + shifts[0:1]).astype(LOW)

    def keys(v, block):
        kv[block * rows : (block + 1) * rows, :] = nn(first_norm(v), w_in[:, width:]).astype(LOW)

    mine = jnp.concatenate([x[order[0]], x[order[1]]], axis=0)
    normed = first_norm(mine)
    kv[0:rows, :] = nn(normed[:rows], w_in[:, width:]).astype(LOW)
    for d in range(1, n):
        keys(xl[d - 1], d)
    for j in range(n // 4):
        keys(xs[j], n + j)
    q[...] = nn(normed, w_in[:, :width]).astype(LOW) * HEAD ** (-0.5)

    def mask(block, s):
        if 0 < block < n:
            return s, jnp.where(r >= block, 0.0, FAR)
        key = lax.broadcasted_iota(jnp.int32, s.shape, 0)
        query = lax.broadcasted_iota(jnp.int32, s.shape, 1)
        query = jnp.where(query >= rows, query - rows, query)
        if block >= n:
            query = query + (r - (block - n)) * rows
        return jnp.where(key <= query, s, -FAR), 0.0

    attend(q, kv, p, mixed, inverse, plan_of(n), mask)
    total = mine.astype(WIDE) + nn(mixed[...].astype(LOW), w_out[...])
    after[...] = total
    second = (standard(total)[0] * gains[1:2] + shifts[1:2]).astype(LOW)
    n1[...] = second
    cq[...] = nn(second, w_cq[...]).astype(LOW) * HEAD ** (-0.5)


def cross_kernel(
    n, order, rank, breaks, enc, el, es, cq, after, w_cm, w_out,
    kv, p, mixed, inverse, crossed,
):
    rows, width = enc.shape[1:]
    r = rank[0]
    kv[0:rows, :] = nn(enc[order[0]], w_cm[...]).astype(LOW)
    for d in range(1, n):
        kv[d * rows : (d + 1) * rows, :] = nn(el[d - 1], w_cm[...]).astype(LOW)
    for j in range(n // 4):
        kv[(n + j) * rows : (n + j + 1) * rows, :] = nn(es[j], w_cm[...]).astype(LOW)

    def mask(block, s):
        key = lax.broadcasted_iota(jnp.int32, s.shape, 0)
        if block < n:
            first = lax.rem(r - block + n, n) * rows
            which = order[0]
        else:
            first = (block - n) * rows
            which = order[1]
        shut = key == breaks[which, 0] - first
        for i in range(1, breaks.shape[1]):
            shut = shut | (key == breaks[which, i] - first)
        return jnp.where(shut, -FAR, s), 0.0

    attend(cq, kv, p, mixed, inverse, plan_of(n), mask)
    crossed[...] = after[...] + nn(mixed[...].astype(LOW), w_out[...])


def feed_kernel(
    order, crossed, cot, w_up, b_up, w_down, b_down, gains, shifts,
    out, grad, g_up, g_down, g_bias, g_small,
):
    rows, width = cot.shape[1:]
    hidden = w_up.shape[1]
    base = crossed[...]
    third = (standard(base)[0] * gains[2:3] + shifts[2:3]).astype(LOW)
    up_low = jnp.concatenate([cot[order[0]], cot[order[1]]], axis=0)
    upward = up_low.astype(WIDE)
    total = base + b_down[...].astype(WIDE)
    back = jnp.zeros_like(base)
    step = width
    for c in range(hidden // step):
        at = slice(c * step, (c + 1) * step)
        rising = nn(third, w_up[:, at]) + b_up[:, at].astype(WIDE)
        active, slope = gelu_pair(rising)
        active = active.astype(LOW)
        total = total + nn(active, w_down[at, :])
        rising_grad = nt(up_low, w_down[at, :]) * slope
        g_bias[:, at] = jnp.sum(rising_grad, axis=0, keepdims=True)
        rising_grad = rising_grad.astype(LOW)
        back = back + nt(rising_grad, w_up[:, at])
        g_down[at, :] = tn(active, up_low).astype(LOW)
        g_up[:, at] = tn(third, rising_grad).astype(LOW)
    total = total.astype(LOW)
    out[order[0]] = total[:rows]
    out[order[1]] = total[rows:]
    inner, gain, shift = norm_back(base, gains[2:3], back)
    grad[...] = upward + inner
    g_small[0, :] = jnp.sum(upward, axis=0)
    g_small[1, :] = gain
    g_small[2, :] = shift


def cross_back_kernel(
    n, order, enc, el, es, grad, mixed, inverse, cq, kv, p, after, n1,
    w_cm, w_cout, w_cq, gains,
    part, self_grad, g_cout, g_cm, g_cq, g_small, dq, dkv,
):
    rows, width = enc.shape[1:]
    low = grad[...].astype(LOW)
    g_cout[...] = tn(mixed[...].astype(LOW), low).astype(LOW)
    up = nt(low, w_cout[...]).astype(LOW).astype(WIDE)
    attend_back(up, mixed, inverse, cq, kv, p, dq, dkv, plan_of(n))
    dq_low = dq[...]
    g_cq[...] = tn(n1[...], dq_low).astype(LOW)
    total = tn(enc[order[0]], dkv[0:rows, :])
    for d in range(1, n):
        total = total + tn(el[d - 1], dkv[d * rows : (d + 1) * rows, :])
    for j in range(n // 4):
        total = total + tn(es[j], dkv[(n + j) * rows : (n + j + 1) * rows, :])
    g_cm[...] = total.astype(LOW)
    for b in range(n + n // 4):
        part[b] = nt(dkv[b * rows : (b + 1) * rows, :], w_cm[...]).astype(LOW)
    inner, gain, shift = norm_back(after[...], gains[1:2], nt(dq_low, w_cq[...]))
    self_grad[...] = grad[...] + inner
    g_small[0, :] = gain
    g_small[1, :] = shift


def self_back_kernel(
    n, order, x, xl, xs, self_grad, mixed, inverse, q, kv, p, w_in, w_out, gains, shifts,
    part, own, g_in, g_out, g_small, dq, dkv,
):
    rows, width = x.shape[1:]
    low = self_grad[...].astype(LOW)
    g_out[...] = tn(mixed[...].astype(LOW), low).astype(LOW)
    up = nt(low, w_out[...]).astype(LOW).astype(WIDE)
    attend_back(up, mixed, inverse, q, kv, p, dq, dkv, plan_of(n))
    mine = jnp.concatenate([x[order[0]], x[order[1]]], axis=0).astype(WIDE)
    unit = standard(mine)[0]
    low = (unit * gains[0:1] + shifts[0:1]).astype(LOW)
    g_in[:, :width] = tn(low, dq[...]).astype(LOW)
    mine = nt(dq[...], w_in[:, :width])
    own[...] = mine
    gain = jnp.sum(mine * unit, axis=0)
    shift = jnp.sum(mine, axis=0)
    total = None
    for b in range(n + n // 4):
        if b == 0:
            key_unit, key_low = unit[:rows], low[:rows]
        else:
            v = xl[b - 1] if b < n else xs[b - n]
            key_unit = standard(v.astype(WIDE))[0]
            key_low = (key_unit * gains[0:1] + shifts[0:1]).astype(LOW)
        pairs = dkv[b * rows : (b + 1) * rows, :]
        term = tn(key_low, pairs)
        total = term if total is None else total + term
        back = nt(pairs, w_in[:, width:])
        part[b] = back.astype(LOW)
        gain = gain + jnp.sum(back * key_unit, axis=0)
        shift = shift + jnp.sum(back, axis=0)
    g_in[:, width:] = total.astype(LOW)
    g_small[0, :] = gain
    g_small[1, :] = shift


def last_kernel(n, order, rank, x, self_grad, own, part, taken, short, e_part, e_taken, e_short,
                gains, grad, e_grad):
    rows, width = x.shape[1:]
    long_up = own[:rows] + part[0].astype(WIDE)
    e_long = e_part[0].astype(WIDE)
    for d in range(n - 1):
        long_up = long_up + taken[d].astype(WIDE)
        e_long = e_long + e_taken[d].astype(WIDE)
    short_up = own[rows:] + short[...].astype(WIDE)
    for which, up, at in ((order[0], long_up, 0), (order[1], short_up, rows)):
        inner, _, _ = norm_back(x[which].astype(WIDE), gains[0:1], up)
        grad[which] = self_grad[at : at + rows] + inner
    e_grad[order[0]] = e_long
    e_grad[order[1]] = e_short[...].astype(WIDE)


def call(kernel, ins, outs, scratch=(), smem=0):
    return pl.pallas_call(
        kernel,
        out_shape=[jax.ShapeDtypeStruct(s, t) for s, t in outs],
        in_specs=[pl.BlockSpec(memory_space=pltpu.SMEM)] * smem
        + [pl.BlockSpec(memory_space=pltpu.VMEM)] * (len(ins) - smem),
        out_specs=[pl.BlockSpec(memory_space=pltpu.VMEM)] * len(outs),
        scratch_shapes=[pltpu.VMEM(s, t) for s, t in scratch],
        compiler_params=pltpu.CompilerParams(vmem_limit_bytes=62 << 20),
    )(*ins)


def send_long(block, n, wrap):
    got = []
    for d in range(1, n):
        pairs = [(i, (i + d) % n) for i in range(n) if wrap or i + d < n]
        got.append(lax.ppermute(block, "blk", pairs))
    return got


def send_short(block, n, rank):
    got = []
    for root in range(n // 4):
        held = jnp.where(rank == root, block, jnp.zeros_like(block))
        d = n // 2
        while d:
            pairs = [((root + k) % n, (root + k + d) % n) for k in range(0, n, 2 * d)]
            held = held + lax.ppermute(held, "blk", pairs)
            d //= 2
        got.append(held)
    return got


def return_long(part, n, wrap):
    got = []
    for d in range(1, n):
        pairs = [(i, (i - d) % n) for i in range(n) if wrap or i - d >= 0]
        got.append(lax.ppermute(part[d], "blk", pairs))
    return jnp.stack(got)


def return_short(part, n, rank):
    got = jnp.zeros_like(part[0])
    for root in range(n // 4):
        held = part[n + root]
        d = 1
        while d < n:
            pairs = [((root + k + d) % n, (root + k) % n) for k in range(0, n, 2 * d)]
            held = held + lax.ppermute(held, "blk", pairs)
            d *= 2
        got = jnp.where(rank == root, held, got)
    return got


def on_device(
    decoder_input, encoder_output, sequence_lengths, chain_breaks,
    self_inward, self_outward, cross_query, cross_memory, cross_outward,
    feed_up, feed_up_bias, feed_down, feed_down_bias, norm_gains, norm_shifts,
    output_cotangent,
):
    sequences, rows, width = decoder_input.shape
    hidden = feed_up.shape[1]
    n = lax.axis_size("blk")
    rank = lax.axis_index("blk")
    ranks = rank.astype(jnp.int32)[None]
    longest = (sequence_lengths[1] > sequence_lengths[0]).astype(jnp.int32)
    order = jnp.stack([longest, 1 - longest])
    both = 2 * rows
    nk = (n + n // 4) * rows
    pairs = width // PAIR

    def pick(v, i):
        return jnp.where(order[i] == 0, v[0], v[1])

    xl = jnp.stack(send_long(pick(decoder_input, 0), n, False))
    xs = jnp.stack(send_short(pick(decoder_input, 1), n, rank))
    el = jnp.stack(send_long(pick(encoder_output, 0), n, True))
    es = jnp.stack(send_short(pick(encoder_output, 1), n, rank))

    q, kv, p, mixed, inverse, after, cq, n1 = call(
        functools.partial(self_kernel, n),
        (order, ranks, decoder_input, xl, xs, self_inward, self_outward, cross_query,
         norm_gains, norm_shifts),
        [((both, width), LOW), ((nk, 2 * width), LOW), ((nk, pairs * both), LOW),
         ((both, width), WIDE), ((both, width), WIDE), ((both, width), WIDE),
         ((both, width), LOW), ((both, width), LOW)],
        smem=2,
    )
    ckv, cp, cmixed, cinverse, crossed = call(
        functools.partial(cross_kernel, n),
        (order, ranks, chain_breaks, encoder_output, el, es, cq, after, cross_memory,
         cross_outward),
        [((nk, 2 * width), LOW), ((nk, pairs * both), LOW),
         ((both, width), WIDE), ((both, width), WIDE), ((both, width), WIDE)],
        smem=3,
    )
    layer_output, cross_grad, g_up, g_down, g_bias, small_feed = call(
        feed_kernel,
        (order, crossed, output_cotangent, feed_up, feed_up_bias[None], feed_down,
         feed_down_bias[None], norm_gains, norm_shifts),
        [(decoder_input.shape, LOW), ((both, width), WIDE), (feed_up.shape, LOW),
         (feed_down.shape, LOW), ((1, hidden), WIDE), ((3, width), WIDE)],
        smem=1,
    )
    e_part, self_grad, g_cout, g_cm, g_cq, small_cross = call(
        functools.partial(cross_back_kernel, n),
        (order, encoder_output, el, es, cross_grad, cmixed, cinverse, cq, ckv, cp, after,
         n1, cross_memory, cross_outward, cross_query, norm_gains),
        [((nk // rows, rows, width), LOW), ((both, width), WIDE), (cross_outward.shape, LOW),
         (cross_memory.shape, LOW), (cross_query.shape, LOW), ((2, width), WIDE)],
        scratch=[((both, width), LOW), ((nk, 2 * width), LOW)],
        smem=1,
    )
    e_taken = return_long(e_part, n, True)
    e_short = return_short(e_part, n, rank)
    part, own, g_in, g_out, small_self = call(
        functools.partial(self_back_kernel, n),
        (order, decoder_input, xl, xs, self_grad, mixed, inverse, q, kv, p, self_inward,
         self_outward, norm_gains, norm_shifts),
        [((nk // rows, rows, width), LOW), ((both, width), WIDE), (self_inward.shape, LOW),
         (self_outward.shape, LOW), ((2, width), WIDE)],
        scratch=[((both, width), LOW), ((nk, 2 * width), LOW)],
        smem=1,
    )
    taken = return_long(part, n, False)
    short = return_short(part, n, rank)
    input_gradient, encoder_gradient = call(
        functools.partial(last_kernel, n),
        (order, ranks, decoder_input, self_grad, own, part, taken, short, e_part, e_taken,
         e_short, norm_gains),
        [(decoder_input.shape, WIDE), (decoder_input.shape, WIDE)],
        smem=2,
    )
    small = jnp.concatenate(
        [small_feed[0], small_self[0], small_cross[0], small_feed[1],
         small_self[1], small_cross[1], small_feed[2], g_bias[0]]
    )
    small = small.reshape(-1, width).astype(LOW)
    flat = jnp.concatenate(
        [v.reshape(-1, width) for v in (g_up, g_down, g_in, g_out, g_cq, g_cm, g_cout)] + [small]
    )
    flat = lax.psum(flat, ("batch", "blk")).astype(WIDE)
    sums, at = [], 0
    for v in (g_up, g_down, g_in, g_out, g_cq, g_cm, g_cout):
        size = v.size // width
        sums.append(flat[at : at + size].reshape(v.shape))
        at += size
    s_up, s_down, s_in, s_out, s_cq, s_cm, s_cout = sums
    small = flat[at:].reshape(-1)
    vec = [small[i * width : (i + 1) * width] for i in range(7)]
    return (
        layer_output, input_gradient, encoder_gradient, s_in, s_out, s_cq, s_cm, s_cout,
        s_up, small[7 * width :], s_down, vec[0],
        jnp.stack(vec[1:4]), jnp.stack(vec[4:7]),
    )


def solution(mesh):
    blocked = P("batch", "blk", None)
    placed = (blocked, blocked, P("batch"), P("batch", None)) + (P(),) * 11 + (blocked,)
    return jax.shard_map(
        on_device,
        mesh=mesh,
        in_specs=placed,
        out_specs=(blocked,) * 3 + (P(),) * 11,
        check_vma=False,
    )
```

```python
import functools

import jax
import jax.numpy as jnp
from jax import lax
from jax.experimental import pallas as pl
from jax.experimental.pallas import tpu as pltpu
from jax.sharding import PartitionSpec as P

HEAD = 64
PAIR = 2 * HEAD
EPSILON = 1e-05
FAR = 1e30
LOW = jnp.bfloat16
WIDE = jnp.float32


def contract(left, right, a, b):
    return lax.dot_general(left, right, (((a,), (b,)), ((), ())), preferred_element_type=WIDE)


def nn(left, right):
    return contract(left, right, 1, 0)


def nt(left, right):
    return contract(left, right, 1, 1)


def tn(left, right):
    return contract(left, right, 0, 0)


def standard(values):
    center = values - jnp.mean(values, axis=-1, keepdims=True)
    spread = jnp.mean(center * center, axis=-1, keepdims=True)
    inverse = lax.rsqrt(spread + EPSILON)
    return center * inverse, inverse


def norm_back(values, gain, upstream):
    unit, inverse = standard(values)
    m = upstream * gain
    grad = inverse * (
        m
        - jnp.mean(m, axis=-1, keepdims=True)
        - unit * jnp.mean(m * unit, axis=-1, keepdims=True)
    )
    return grad, jnp.sum(upstream * unit, axis=0), jnp.sum(upstream, axis=0)


def gelu_pair(x):
    z = jnp.abs(x) * 0.7071067811865476
    t = 1.0 / (1.0 + 0.5 * z)
    poly = 0.17087277
    for c in (
        -0.82215223,
        1.48851587,
        -1.13520398,
        0.27886807,
        -0.18628806,
        0.09678418,
        0.37409196,
        1.00002368,
        -1.26551223,
    ):
        poly = poly * t + c
    bell = jnp.exp(-z * z)
    tail = 0.5 * t * jnp.exp(poly) * bell
    share = jnp.where(x >= 0, 1.0 - tail, tail)
    return x * share, share + x * bell * 0.3989422804014327


def by_head(pair_rows):
    lane = lax.broadcasted_iota(jnp.int32, pair_rows.shape, 1)
    zero = jnp.zeros_like(pair_rows)
    return jnp.concatenate(
        [jnp.where(lane < HEAD, pair_rows, zero), jnp.where(lane >= HEAD, pair_rows, zero)], axis=0
    )


def own_parts(both):
    rows = both.shape[1] // 2
    return jnp.concatenate([both[:HEAD, :rows], both[HEAD:, rows:]], axis=0)


def attend(q_ref, kv_ref, p_ref, mixed_ref, inverse_ref, plan, mask):
    rows = q_ref.shape[0] // 2
    width = q_ref.shape[1]
    for pair in range(width // PAIR):
        lanes = slice(pair * PAIR, (pair + 1) * PAIR)
        values = slice(width + pair * PAIR, width + (pair + 1) * PAIR)
        spot = slice(pair * 2 * rows, (pair + 1) * 2 * rows)
        for seq, blocks in enumerate(plan):
            mine = slice(seq * rows, (seq + 1) * rows)
            queries = by_head(q_ref[mine, lanes])
            scores, tops = [], []
            for block in blocks:
                s = nt(kv_ref[block * rows : (block + 1) * rows, lanes], queries)
                s, far = mask(block, s)
                scores.append((s, far))
                tops.append(jnp.max(s, axis=0, keepdims=True) - far)
            top = functools.reduce(jnp.maximum, tops)
            total = jnp.zeros_like(top)
            mixed = jnp.zeros((PAIR, 2 * rows), WIDE)
            for block, (s, far) in zip(blocks, scores):
                at = slice(block * rows, (block + 1) * rows)
                p = jnp.exp(s - (top + far))
                total = total + jnp.sum(p, axis=0, keepdims=True)
                p = p.astype(LOW)
                p_ref[at, spot] = p
                mixed = mixed + tn(kv_ref[at, values], p)
            inverse = 1.0 / total
            mixed_ref[mine, lanes] = own_parts(mixed * inverse).T
            inverse_ref[mine, lanes] = own_parts(jnp.broadcast_to(inverse, mixed.shape)).T


def attend_back(up, mixed_ref, inverse_ref, q_ref, kv_ref, p_ref, dq_ref, dkv_ref, plan):
    rows = q_ref.shape[0] // 2
    width = q_ref.shape[1]
    scale = HEAD ** (-0.5)
    for pair in range(width // PAIR):
        lanes = slice(pair * PAIR, (pair + 1) * PAIR)
        values = slice(width + pair * PAIR, width + (pair + 1) * PAIR)
        spot = slice(pair * 2 * rows, (pair + 1) * 2 * rows)
        for seq, blocks in enumerate(plan):
            mine = slice(seq * rows, (seq + 1) * rows)
            queries = by_head(q_ref[mine, lanes])
            scaled = up[mine, lanes] * inverse_ref[mine, lanes]
            inner = (scaled * mixed_ref[mine, lanes]).T
            offset = jnp.concatenate(
                [
                    jnp.sum(inner[:HEAD], axis=0, keepdims=True),
                    jnp.sum(inner[HEAD:], axis=0, keepdims=True),
                ],
                axis=1,
            )
            upper = by_head(scaled.astype(LOW))
            dq = jnp.zeros((PAIR, 2 * rows), WIDE)
            for block in blocks:
                at = slice(block * rows, (block + 1) * rows)
                p = p_ref[at, spot]
                dp = nt(kv_ref[at, values], upper)
                ds = (p.astype(WIDE) * (dp - offset)).astype(LOW)
                dkv_ref[at, values] = nn(p, upper).astype(LOW)
                dkv_ref[at, lanes] = nn(ds, queries).astype(LOW)
                dq = dq + tn(kv_ref[at, lanes], ds)
            dq_ref[mine, lanes] = (own_parts(dq).T * scale).astype(LOW)


def plan_of(n):
    return (tuple(range(n)), tuple(range(n, n + n // 4)))


def add_terms(out, refs, terms):
    for j in range(out.shape[0]):
        total = refs[j * terms][...]
        for ref in refs[j * terms + 1 : (j + 1) * terms]:
            total = total + ref[...]
        out[j] = total


def self_kernel(n, terms, order, rank, x, *refs):
    xl, refs = refs[: n - 1], refs[n - 1 :]
    shorts, refs = refs[: terms * (n // 4)], refs[terms * (n // 4) :]
    (w_in, w_out, w_cq, gains, shifts, q, kv, p, mixed, inverse, after, cq, n1, xs) = refs
    add_terms(xs, shorts, terms)
    rows, width = x.shape[1:]
    r = rank[0]

    def first_norm(v):
        return (standard(v.astype(WIDE))[0] * gains[0:1] + shifts[0:1]).astype(LOW)

    def keys(v, block):
        kv[block * rows : (block + 1) * rows, :] = nn(first_norm(v), w_in[:, width:]).astype(LOW)

    mine = jnp.concatenate([x[order[0]], x[order[1]]], axis=0)
    normed = first_norm(mine)
    kv[0:rows, :] = nn(normed[:rows], w_in[:, width:]).astype(LOW)
    for d in range(1, n):
        keys(xl[d - 1][...], d)
    for j in range(n // 4):
        keys(xs[j], n + j)
    q[...] = nn(normed, w_in[:, :width]).astype(LOW) * HEAD ** (-0.5)

    def mask(block, s):
        if 0 < block < n:
            return s, jnp.where(r >= block, 0.0, FAR)
        key = lax.broadcasted_iota(jnp.int32, s.shape, 0)
        query = lax.broadcasted_iota(jnp.int32, s.shape, 1)
        query = jnp.where(query >= rows, query - rows, query)
        if block >= n:
            query = query + (r - (block - n)) * rows
        return jnp.where(key <= query, s, -FAR), 0.0

    attend(q, kv, p, mixed, inverse, plan_of(n), mask)
    total = mine.astype(WIDE) + nn(mixed[...].astype(LOW), w_out[...])
    after[...] = total
    second = (standard(total)[0] * gains[1:2] + shifts[1:2]).astype(LOW)
    n1[...] = second
    cq[...] = nn(second, w_cq[...]).astype(LOW) * HEAD ** (-0.5)


def cross_kernel(n, terms, order, rank, breaks, enc, *refs):
    el, refs = refs[: n - 1], refs[n - 1 :]
    shorts, refs = refs[: terms * (n // 4)], refs[terms * (n // 4) :]
    cq, after, w_cm, w_out, kv, p, mixed, inverse, crossed, es = refs
    add_terms(es, shorts, terms)
    rows, width = enc.shape[1:]
    r = rank[0]
    kv[0:rows, :] = nn(enc[order[0]], w_cm[...]).astype(LOW)
    for d in range(1, n):
        kv[d * rows : (d + 1) * rows, :] = nn(el[d - 1][...], w_cm[...]).astype(LOW)
    for j in range(n // 4):
        kv[(n + j) * rows : (n + j + 1) * rows, :] = nn(es[j], w_cm[...]).astype(LOW)

    def mask(block, s):
        key = lax.broadcasted_iota(jnp.int32, s.shape, 0)
        if block < n:
            first = lax.rem(r - block + n, n) * rows
            which = order[0]
        else:
            first = (block - n) * rows
            which = order[1]
        shut = key == breaks[which, 0] - first
        for i in range(1, breaks.shape[1]):
            shut = shut | (key == breaks[which, i] - first)
        return jnp.where(shut, -FAR, s), 0.0

    attend(cq, kv, p, mixed, inverse, plan_of(n), mask)
    crossed[...] = after[...] + nn(mixed[...].astype(LOW), w_out[...])


def spread(near, far, code, value, first, lanes, deep=None):
    half, tall = near.shape[:2]
    deep = deep or tall
    wide = value.shape[1]

    def put(low, high):
        for k in range(value.shape[0] // deep):
            ref = low if first + k < half else high
            for i in range(deep // tall):
                at = slice(lanes.start + i * wide, lanes.start + (i + 1) * wide)
                part = value[k * deep + i * tall : k * deep + (i + 1) * tall]
                ref[((first + k) ^ code) & (half - 1), :, at] = part

    @pl.when(code < half)
    def _():
        put(near, far)

    @pl.when(code >= half)
    def _():
        put(far, near)


def feed_kernel(
    order, codes, crossed, cot, w_up, b_up, w_down, b_down, gains, shifts,
    out, grad, near, far, g_bias, g_small,
):
    rows, width = cot.shape[1:]
    hidden = w_up.shape[1]
    base = crossed[...]
    third = (standard(base)[0] * gains[2:3] + shifts[2:3]).astype(LOW)
    up_low = jnp.concatenate([cot[order[0]], cot[order[1]]], axis=0)
    upward = up_low.astype(WIDE)
    total = base + b_down[...].astype(WIDE)
    back = jnp.zeros_like(base)
    step = width
    for c in range(hidden // step):
        at = slice(c * step, (c + 1) * step)
        rising = nn(third, w_up[:, at]) + b_up[:, at].astype(WIDE)
        active, slope = gelu_pair(rising)
        active = active.astype(LOW)
        total = total + nn(active, w_down[at, :])
        rising_grad = nt(up_low, w_down[at, :]) * slope
        g_bias[:, at] = jnp.sum(rising_grad, axis=0, keepdims=True)
        rising_grad = rising_grad.astype(LOW)
        back = back + nt(rising_grad, w_up[:, at])
        deep = hidden // (2 * near.shape[0])
        spread(near, far, codes[0], tn(third, rising_grad).astype(LOW), 0, at)
        spread(near, far, codes[1], tn(active, up_low).astype(LOW), c * step // deep,
               slice(hidden, 2 * hidden), deep)
    total = total.astype(LOW)
    out[order[0]] = total[:rows]
    out[order[1]] = total[rows:]
    inner, gain, shift = norm_back(base, gains[2:3], back)
    grad[...] = upward + inner
    g_small[0, :] = jnp.sum(upward, axis=0)
    g_small[1, :] = gain
    g_small[2, :] = shift


def cross_back_kernel(n, order, enc, *refs):
    el, es, refs = refs[: n - 1], refs[n - 1], refs[n:]
    (grad, mixed, inverse, cq, kv, p, after, n1, w_cm, w_cout, w_cq, gains) = refs[:12]
    parts, (self_grad, g_cross, g_small, dq, dkv) = refs[12:-5], refs[-5:]
    rows, width = enc.shape[1:]
    low = grad[...].astype(LOW)
    g_cross[:, 3 * width :] = tn(mixed[...].astype(LOW), low).astype(LOW)
    up = nt(low, w_cout[...]).astype(LOW).astype(WIDE)
    attend_back(up, mixed, inverse, cq, kv, p, dq, dkv, plan_of(n))
    dq_low = dq[...]
    g_cross[:, 2 * width : 3 * width] = tn(n1[...], dq_low).astype(LOW)
    total = tn(enc[order[0]], dkv[0:rows, :])
    for d in range(1, n):
        total = total + tn(el[d - 1][...], dkv[d * rows : (d + 1) * rows, :])
    for j in range(n // 4):
        total = total + tn(es[j], dkv[(n + j) * rows : (n + j + 1) * rows, :])
    g_cross[:, : 2 * width] = total.astype(LOW)
    for b in range(n + n // 4):
        parts[b][...] = nt(dkv[b * rows : (b + 1) * rows, :], w_cm[...]).astype(LOW)
    inner, gain, shift = norm_back(after[...], gains[1:2], nt(dq_low, w_cq[...]))
    self_grad[...] = grad[...] + inner
    g_small[0, :] = gain
    g_small[1, :] = shift


def self_back_kernel(
    n, self_grad, mixed, inverse, q, kv, p, w_in, w_out, _, *refs
):
    parts, (dq, dkv, low) = refs[:-3], refs[-3:]
    rows, width = parts[0].shape
    low[...] = self_grad[...].astype(LOW)
    up = nt(low[...], w_out[...]).astype(LOW).astype(WIDE)
    attend_back(up, mixed, inverse, q, kv, p, dq, dkv, plan_of(n))
    for b in range(n + n // 4):
        parts[b][...] = nt(dkv[b * rows : (b + 1) * rows, :], w_in[:, width:]).astype(LOW)


def self_sums_kernel(n, order, codes, x, *refs):
    xl, parts, refs = refs[: n - 1], refs[n - 1 : 2 * n - 1 + n // 4], refs[2 * n - 1 + n // 4 :]
    (
        xs, low, mixed, dq, dkv, w_in, gains, shifts, small_feed, g_bias, small_cross,
        g_cross, _, own, near, far,
    ) = refs
    rows, width = x.shape[1:]
    spread(near, far, codes[0], g_cross[...], 0, slice(0, 4 * width))
    spread(near, far, codes[1], tn(mixed[...].astype(LOW), low[...]).astype(LOW), 0,
           slice(7 * width, 8 * width))
    mine = jnp.concatenate([x[order[0]], x[order[1]]], axis=0).astype(WIDE)
    unit = standard(mine)[0]
    normed = (unit * gains[0:1] + shifts[0:1]).astype(LOW)
    spread(near, far, codes[1], tn(normed, dq[...]).astype(LOW), 0, slice(4 * width, 5 * width))
    mine = nt(dq[...], w_in[:, :width])
    own[...] = mine
    gain = jnp.sum(mine * unit, axis=0)
    shift = jnp.sum(mine, axis=0)
    total = None
    for b in range(n + n // 4):
        if b == 0:
            key_unit, key_low = unit[:rows], normed[:rows]
        else:
            v = xl[b - 1][...] if b < n else xs[b - n]
            key_unit = standard(v.astype(WIDE))[0]
            key_low = (key_unit * gains[0:1] + shifts[0:1]).astype(LOW)
        term = tn(key_low, dkv[b * rows : (b + 1) * rows, :])
        total = term if total is None else total + term
        back = parts[b][...].astype(WIDE)
        gain = gain + jnp.sum(back * key_unit, axis=0)
        shift = shift + jnp.sum(back, axis=0)
    spread(near, far, codes[1], total.astype(LOW), 0, slice(5 * width, 7 * width))
    small = [gain[None], small_cross[0:1], small_feed[1:2], shift[None], small_cross[1:2],
             small_feed[2:3], small_feed[0:1], g_bias[...]]
    small = [v[:, i : i + 128] for v in small for i in range(0, v.shape[1], 128)]
    small.append(jnp.zeros((width - len(small), 128), WIDE))
    spread(near, far, codes[1], jnp.concatenate(small, axis=0).astype(LOW), 0,
           slice(8 * width, 8 * width + 128))


def unpack(plan, codes, pieces, outs):
    for out, (at, count, which, lane, side) in zip(outs, plan):
        wide = out.shape[1]
        depth, tall = pieces[at].shape[:2]
        for k in range(count * depth):
            first = (codes[which] ^ k) * (tall * side)
            for i in range(side):
                start = pl.multiple_of(first + i * tall, tall)
                lanes = slice(lane + i * wide, lane + (i + 1) * wide)
                out[pl.ds(start, tall), :] = pieces[at + k // depth][k % depth, :, lanes].astype(WIDE)


def unpack_feed_kernel(plan, codes, *refs):
    unpack(plan, codes, refs[: -len(plan)], refs[-len(plan) :])


def unpack_rest_kernel(plan, codes, *refs):
    *refs, up_bias, down_bias, gains, shifts, small = refs
    count = len(plan) - 1
    unpack(plan, codes, refs[:-count], refs[-count:] + [small])
    at = 0
    for out, count in ((gains, 3), (shifts, 3), (down_bias, 1), (up_bias, 1)):
        for i in range(count):
            across = out.shape[1] // 128
            row = [small[at + j : at + j + 1, :] for j in range(across)]
            out[i : i + 1, :] = jnp.concatenate(row, axis=1)
            at += across


def last_kernel(n, order, rank, x, self_grad, own, gains, part, e_long, *refs):
    taken, refs = refs[: n - 1], refs[n - 1 :]
    shorts, e_shorts, (grad, e_grad) = refs[: n // 4], refs[n // 4 : n // 2], refs[-2:]
    rows = x.shape[1]

    def mine(helds):
        total = jnp.zeros(part.shape, WIDE)
        for root, held in enumerate(helds):
            total = jnp.where(rank[0] == root, held[...].astype(WIDE), total)
        return total

    long_up = own[:rows] + part[...].astype(WIDE)
    for ref in taken:
        long_up = long_up + ref[...].astype(WIDE)
    short_up = own[rows:] + mine(shorts)
    for which, up, at in ((order[0], long_up, 0), (order[1], short_up, rows)):
        inner, _, _ = norm_back(x[which].astype(WIDE), gains[0:1], up)
        grad[which] = self_grad[at : at + rows] + inner
    e_grad[order[0]] = e_long[...]
    e_grad[order[1]] = mine(e_shorts)


def add_core(near, got, *outs):
    at = 0
    half = near.shape[0] // 2
    for keep, send in zip(outs[::2], outs[1::2]):
        lanes = slice(at, at + keep.shape[2])
        keep[...] = near[:half, :, lanes] + got[:half, :, lanes]
        send[...] = near[half:, :, lanes] + got[half:, :, lanes]
        at = lanes.stop


def add_halves(keep, got, *outs):
    half = keep.shape[0] // 2
    outs[-2][...] = keep[:half] + got[:half]
    outs[-1][...] = keep[half:] + got[half:]


def add_to_pieces(a, got_a, b, got_b, *outs):
    wide = a.shape[2]
    for k, out in enumerate(outs[-a.shape[0] :]):
        out[:, :, :wide] = a[k : k + 1] + got_a[k : k + 1]
        out[:, :, wide:] = b[k : k + 1] + got_b[k : k + 1]


def note(*refs):
    pass


def add_all(_, *refs):
    *parts, out = refs
    total = parts[0][...].astype(WIDE)
    for part in parts[1:]:
        total = total + part[...].astype(WIDE)
    out[...] = total.astype(out.dtype)


def lay_whole(_, *refs):
    for k, ref in enumerate(refs[:-1]):
        refs[-1][k : k + 1] = ref[...]


def lay(*refs):
    *parts, a, b = refs
    wide = a.shape[2]
    for k, part in enumerate(parts):
        a[k : k + 1] = part[:, :, :wide]
        b[k : k + 1] = part[:, :, wide:]


def join(a, b, out):
    out[: a.shape[0]] = a[...]
    out[a.shape[0] :] = b[...]


def steps_kernel(steps, *refs):
    refs = list(refs)
    at_in, at_out = 0, sum(count for _, count, _ in steps)
    for kernel, ins, outs in steps:
        kernel(*refs[at_in : at_in + ins], *refs[at_out : at_out + outs])
        at_in += ins
        at_out += outs


def call(kernel, ins, outs, us, scratch=(), smem=0, room=62):
    return pl.pallas_call(
        kernel,
        out_shape=[jax.ShapeDtypeStruct(s, t) for s, t in outs],
        in_specs=[pl.BlockSpec(memory_space=pltpu.SMEM)] * smem
        + [pl.BlockSpec(memory_space=pltpu.VMEM)] * (len(ins) - smem),
        out_specs=[pl.BlockSpec(memory_space=pltpu.VMEM)] * len(outs),
        scratch_shapes=[pltpu.VMEM(s, t) for s, t in scratch],
        compiler_params=pltpu.CompilerParams(vmem_limit_bytes=room << 20),
        cost_estimate=pl.CostEstimate(flops=us * 10**9, bytes_accessed=0, transcendentals=0),
    )(*ins)


def small_steps(steps):
    outs = call(
        functools.partial(steps_kernel, [(k, len(i), len(o)) for k, i, o in steps]),
        [v for _, ins, _ in steps for v in ins],
        [o if isinstance(o[0], tuple) else (o, LOW) for _, _, outs in steps for o in outs],
        2,
        room=16,
    )
    got = []
    for _, _, shapes in steps:
        got.append(outs[: len(shapes)])
        outs = outs[len(shapes) :]
    return got


def send_long(block, n, wrap):
    got = []
    for d in range(1, n):
        pairs = [(i, (i + d) % n) for i in range(n) if wrap or i + d < n]
        got.append(lax.ppermute(block, "blk", pairs))
    return got


def return_long(block, n, distance, wrap):
    pairs = [(i, (i - distance) % n) for i in range(n) if wrap or i >= distance]
    return lax.ppermute(block, "blk", pairs)


def return_short(held, n, root, distance):
    pairs = [((root + k + distance) % n, (root + k) % n) for k in range(0, n, 2 * distance)]
    return lax.ppermute(held, "blk", pairs)


def return_short_rest(helds, n):
    got = []
    for root, held in enumerate(helds):
        d = 4
        while d < n:
            held = held + return_short(held, n, root, d)
            d *= 2
        got.append(held)
    return got


def send_short_first(block, n, rank):
    got = []
    for root in range(n // 4):
        held = jnp.where(rank == root, block, jnp.zeros_like(block))
        got.append([held, lax.ppermute(held, "blk", [(root, (root + n // 2) % n)])])
    return got


def send_short_rest(terms, n):
    for root in range(n // 4):
        d = n // 4
        while d:
            pairs = [((root + k) % n, (root + k + d) % n) for k in range(0, n, 2 * d)]
            held = functools.reduce(jnp.add, terms[root])
            terms[root].append(lax.ppermute(held, "blk", pairs))
            d //= 2
    return [v for several in terms for v in several]


def tied(value, *others):
    return lax.optimization_barrier((value, others))[0]


def trade(v, axis, distance):
    return lax.ppermute(v, axis, [(i, i ^ distance) for i in range(lax.axis_size(axis))])


class Sharing:
    def __init__(self, batch, n):
        self.rest = [("batch", d) for d in (8, 16, 32) if d < batch]
        self.rest += [("blk", d) for d in (4, 8, 16, 32) if d < n]
        self.chunks = 32

    def codes(self):
        codes = []
        for first, second in ((2, 4), (4, 2)):
            code = jnp.int32(0)
            for axis, distance in (("batch", 1), ("batch", first), ("batch", second), ("blk", 2),
                                   ("blk", 1)):
                code = 2 * code + (lax.axis_index(axis) // distance) % 2
            codes.append(code.astype(jnp.int32))
        return jnp.stack(codes)

    def doubled(self, v):
        for axis, distance in self.rest:
            v = v + trade(v, axis, distance)
        return v


def to_tall(pieces):
    return [trade(v, "blk", j) for j, v in enumerate(pieces) if j]


def on_device(
    decoder_input, encoder_output, sequence_lengths, chain_breaks,
    self_inward, self_outward, cross_query, cross_memory, cross_outward,
    feed_up, feed_up_bias, feed_down, feed_down_bias, norm_gains, norm_shifts,
    output_cotangent,
):
    sequences, rows, width = decoder_input.shape
    hidden = feed_up.shape[1]
    n = lax.axis_size("blk")
    rank = lax.axis_index("blk")
    ranks = rank.astype(jnp.int32)[None]
    longest = (sequence_lengths[1] > sequence_lengths[0]).astype(jnp.int32)
    order = jnp.stack([longest, 1 - longest])
    both = 2 * rows
    nk = (n + n // 4) * rows
    pairs = width // PAIR

    def pick(v, i):
        return jnp.where(order[i] == 0, v[0], v[1])

    sharing = Sharing(lax.axis_size("batch"), n)
    codes = sharing.codes()
    chunks = sharing.chunks
    tall = width // chunks
    blocks = nk // rows

    room = 62 if n > 4 else 40
    x_long, x_short = pick(decoder_input, 0), pick(decoder_input, 1)
    e_long, e_short = pick(encoder_output, 0), pick(encoder_output, 1)
    xs = send_short_first(x_short, n, rank)
    xl = send_long(x_long, n, False)
    xs = send_short_rest(xs, n)
    shorts = len(xs) // (n // 4)
    e_long, e_short = tied((e_long, e_short), *xl)
    el = send_long(e_long, n, True)
    es = send_short_first(e_short, n, rank)

    q, kv, p, mixed, inverse, after, cq, n1, xs = call(
        functools.partial(self_kernel, n, shorts),
        (order, ranks, decoder_input, *xl, *xs, self_inward, self_outward, cross_query,
         norm_gains, norm_shifts),
        [((both, width), LOW), ((nk, 2 * width), LOW), ((nk, pairs * both), LOW),
         ((both, width), WIDE), ((both, width), WIDE), ((both, width), WIDE),
         ((both, width), LOW), ((both, width), LOW), ((n // 4, rows, width), LOW)],
        13,
        smem=2,
        room=room,
    )
    es = send_short_rest([[v, tied(w, n1)] for v, w in es], n)
    ckv, cp, cmixed, cinverse, crossed, es = call(
        functools.partial(cross_kernel, n, shorts),
        (order, ranks, chain_breaks, encoder_output, *el, *es, cq, after, cross_memory,
         cross_outward),
        [((nk, 2 * width), LOW), ((nk, pairs * both), LOW),
         ((both, width), WIDE), ((both, width), WIDE), ((both, width), WIDE),
         ((n // 4, rows, width), LOW)],
        13,
        smem=3,
        room=room,
    )
    half = chunks // 2
    layer_output, cross_grad, near, far, g_bias, small_feed = call(
        feed_kernel,
        (order, codes, crossed, output_cotangent, feed_up, feed_up_bias[None], feed_down,
         feed_down_bias[None], norm_gains, norm_shifts),
        [(decoder_input.shape, LOW), ((both, width), WIDE), ((half, tall, 2 * hidden), LOW),
         ((half, tall, 2 * hidden), LOW), ((1, hidden), WIDE), ((3, width), WIDE)],
        16,
        smem=2,
        room=room,
    )
    wide = [hidden, hidden]
    wide_rest = [hidden, hidden + 128]

    def shape(count, lanes):
        return (count, tall, lanes)

    ((a, a_send, b, b_send),) = small_steps(
        [(add_core, (near, trade(far, "batch", 1)), [shape(8, w) for w in wide for _ in "ks"])]
    )
    *e_parts, self_grad, g_cross, small_cross = call(
        functools.partial(cross_back_kernel, n),
        (order, encoder_output, *el, es, tied(cross_grad, a), cmixed, cinverse,
         cq, ckv, cp, after, n1, cross_memory, cross_outward, cross_query, norm_gains),
        [((rows, width), LOW)] * blocks
        + [((both, width), WIDE), ((width, 4 * width), LOW), ((2, width), WIDE)],
        14,
        scratch=[((both, width), LOW), ((nk, 2 * width), LOW)],
        smem=1,
        room=room,
    )
    roots = range(n // 4)
    block = ((rows, width), LOW)
    a_got, b_got = trade(a_send, "batch", 2), trade(b_send, "batch", 4)
    (a, a_send), (b, b_send) = small_steps(
        [(add_halves, (a, a_got, small_cross), [shape(4, wide[0])] * 2),
         (add_halves, (b, b_got), [shape(4, wide[1])] * 2)]
    )
    a_got, b_got = trade(a_send, "batch", 4), trade(b_send, "batch", 2)
    e_near = [return_long(e_parts[d], n, d, True) for d in sorted({1, n - 1})]
    e_got = [return_short(e_parts[n + k], n, k, 1) for k in roots]
    *parts, dq, dkv, self_low = call(
        functools.partial(self_back_kernel, n),
        (self_grad, mixed, inverse, q, kv, p, self_inward, self_outward, a),
        [block] * blocks + [((both, width), LOW), ((nk, 2 * width), LOW), ((both, width), LOW)],
        10,
        room=room,
    )
    feed, (e_long,), *e_short = small_steps(
        [(add_to_pieces, (a, a_got, b, b_got, self_low), [shape(1, sum(wide))] * 4),
         (add_all, (self_low, e_parts[0], *e_near), [((rows, width), WIDE)])]
        + [(add_all, (self_low, e_parts[n + k], e_got[k]), [(rows, width)]) for k in roots]
    )
    feed_got = to_tall(feed)
    e_far = [return_long(e_parts[d], n, d, True) for d in range(2, n - 1)]
    e_got = [return_short(e_short[k][0], n, k, 2) for k in roots]
    own, near, far = call(
        functools.partial(self_sums_kernel, n),
        (order, codes, decoder_input, *xl, *parts, xs, self_low, mixed, dq, dkv, self_inward,
         norm_gains, norm_shifts, small_feed, g_bias, small_cross, g_cross, feed[0]),
        [((both, width), WIDE), (shape(half, sum(wide_rest)), LOW),
         (shape(half, sum(wide_rest)), LOW)],
        7,
        smem=2,
        room=room,
    )
    (a, a_send, b, b_send), (feed,), (e_long,), *e_short = small_steps(
        [(add_core, (near, trade(far, "batch", 1)), [shape(8, w) for w in wide_rest for _ in "ks"]),
         (add_all, (own, feed[0], *feed_got), [shape(1, sum(wide))]),
         (add_all, (own, e_long, *e_far), [((rows, width), WIDE)])]
        + [(add_all, (own, e_short[k][0], e_got[k]), [(rows, width)]) for k in roots]
    )
    e_short = return_short_rest([held for held, in e_short], n)
    feed = sharing.doubled(feed)
    a_got, b_got = trade(a_send, "batch", 2), trade(b_send, "batch", 4)
    (a, a_send), (b, b_send), (fa, fb) = small_steps(
        [(add_halves, (a, a_got), [shape(4, wide_rest[0])] * 2),
         (add_halves, (b, b_got), [shape(4, wide_rest[1])] * 2),
         (lay, (feed, *to_tall([feed] * 4)), [shape(4, w) for w in wide])]
    )
    a_got, b_got = trade(a_send, "batch", 4), trade(b_send, "batch", 2)
    taken = {d: return_long(tied(parts[d], a_send), n, d, False) for d in sorted({1, n - 1})}
    rest, (fa,), (fb,), _ = small_steps(
        [(add_to_pieces, (a, a_got, b, b_got), [shape(1, sum(wide_rest))] * 4),
         (join, (fa, trade(fa, "batch", 4)), [shape(8, wide[0])]),
         (join, (fb, trade(fb, "batch", 2)), [shape(8, wide[1])]),
         (note, tuple(taken.values()), [])]
    )
    fa_got, fb_got = trade(fa, "batch", 2), trade(fb, "batch", 4)
    (rest,), _ = small_steps(
        [(add_all, (own, rest[0], *to_tall(rest)), [shape(1, sum(wide_rest))]),
         (note, (fa_got, fb_got), [])]
    )
    rest = sharing.doubled(rest)
    feed = [fa, fa_got, fb, fb_got]
    feed_got = [trade(tied(v, rest), "batch", 1) for v in feed]
    (ra, rb), _ = small_steps(
        [(lay, (rest, *to_tall([rest] * 4)), [shape(4, w) for w in wide_rest]),
         (note, tuple(feed_got), [])]
    )
    ra_got, rb_got = trade(ra, "batch", 4), trade(rb, "batch", 2)
    for d in range(2, n - 1):
        taken[d] = return_long(tied(parts[d], ra), n, d, False)
    got = [return_short(tied(parts[n + k], ra), n, k, 1) for k in roots]
    (ra,), (rb,), _, *short = small_steps(
        [(join, (ra, ra_got), [shape(8, wide_rest[0])]),
         (join, (rb, rb_got), [shape(8, wide_rest[1])]),
         (note, tuple(taken[d] for d in range(2, n - 1)), [])]
        + [(add_all, (own, parts[n + k], got[k]), [(rows, width)]) for k in roots]
    )
    rest = [ra, trade(ra, "batch", 2), rb, trade(rb, "batch", 4)]
    short = [held + return_short(held, n, k, 2) for k, (held,) in enumerate(short)]
    short = return_short_rest(short, n)
    feed = feed[:2] + feed_got[:2] + feed[2:] + feed_got[2:]
    s_up, s_down = call(
        functools.partial(unpack_feed_kernel, [(0, 4, 0, 0, 1), (4, 4, 1, 0, hidden // width)]),
        (codes, *feed),
        [(feed_up.shape, WIDE), (feed_down.shape, WIDE)],
        6,
        smem=1,
        room=room,
    )
    input_gradient, encoder_gradient = call(
        functools.partial(last_kernel, n),
        (order, ranks, decoder_input, self_grad, own, norm_gains, parts[0], e_long,
         *[taken[d] for d in range(1, n)], *short, *e_short),
        [(decoder_input.shape, WIDE), (decoder_input.shape, WIDE)],
        3,
        smem=2,
        room=room,
    )
    rest_got = [trade(v, "batch", 1) for v in rest]
    rest = rest[:2] + rest_got[:2] + rest[2:] + rest_got[2:]
    places = [(0, 4, 0, 0, 1), (0, 4, 0, 2 * width, 1), (0, 4, 0, 3 * width, 1),
              (4, 4, 1, 0, 1), (4, 4, 1, 3 * width, 1), (4, 4, 1, 4 * width, 1)]
    s_cm, s_cq, s_cout, s_in, s_out, up_bias, down_bias, gains, shifts = call(
        functools.partial(unpack_rest_kernel, places),
        (codes, *rest),
        [(s, WIDE) for s in (cross_memory.shape, cross_query.shape, cross_outward.shape,
                             self_inward.shape, self_outward.shape, (1, hidden), (1, width),
                             norm_gains.shape, norm_shifts.shape)],
        5,
        scratch=[((width, 128), WIDE)],
        smem=1,
        room=room,
    )
    return (
        layer_output, input_gradient, encoder_gradient, s_in, s_out, s_cq, s_cm, s_cout,
        s_up, up_bias[0], s_down, down_bias[0], gains, shifts,
    )


def solution(mesh):
    blocked = P("batch", "blk", None)
    placed = (blocked, blocked, P("batch"), P("batch", None)) + (P(),) * 11 + (blocked,)
    return jax.shard_map(
        on_device,
        mesh=mesh,
        in_specs=placed,
        out_specs=(blocked,) * 3 + (P(),) * 11,
        check_vma=False,
    )
```

```python
import functools

import jax
import jax.numpy as jnp
from jax import lax
from jax.experimental import pallas as pl
from jax.experimental.pallas import tpu as pltpu
from jax.sharding import PartitionSpec as P

HEAD = 64
PAIR = 2 * HEAD
EPSILON = 1e-05
FAR = 1e30
LOW = jnp.bfloat16
WIDE = jnp.float32


def contract(left, right, a, b):
    return lax.dot_general(left, right, (((a,), (b,)), ((), ())), preferred_element_type=WIDE)


def nn(left, right):
    return contract(left, right, 1, 0)


def nt(left, right):
    return contract(left, right, 1, 1)


def tn(left, right):
    return contract(left, right, 0, 0)


def standard(values):
    center = values - jnp.mean(values, axis=-1, keepdims=True)
    spread = jnp.mean(center * center, axis=-1, keepdims=True)
    inverse = lax.rsqrt(spread + EPSILON)
    return center * inverse, inverse


def norm_back(values, gain, upstream):
    unit, inverse = standard(values)
    m = upstream * gain
    grad = inverse * (
        m
        - jnp.mean(m, axis=-1, keepdims=True)
        - unit * jnp.mean(m * unit, axis=-1, keepdims=True)
    )
    return grad, jnp.sum(upstream * unit, axis=0), jnp.sum(upstream, axis=0)


def gelu_pair(x):
    z = jnp.abs(x) * 0.7071067811865476
    t = 1.0 / (1.0 + 0.5 * z)
    poly = 0.17087277
    for c in (
        -0.82215223,
        1.48851587,
        -1.13520398,
        0.27886807,
        -0.18628806,
        0.09678418,
        0.37409196,
        1.00002368,
        -1.26551223,
    ):
        poly = poly * t + c
    bell = jnp.exp(-z * z)
    tail = 0.5 * t * jnp.exp(poly) * bell
    share = jnp.where(x >= 0, 1.0 - tail, tail)
    return x * share, share + x * bell * 0.3989422804014327


def by_head(pair_rows):
    lane = lax.broadcasted_iota(jnp.int32, pair_rows.shape, 1)
    zero = jnp.zeros_like(pair_rows)
    return jnp.concatenate(
        [jnp.where(lane < HEAD, pair_rows, zero), jnp.where(lane >= HEAD, pair_rows, zero)], axis=0
    )


def own_parts(both):
    rows = both.shape[1] // 2
    return jnp.concatenate([both[:HEAD, :rows], both[HEAD:, rows:]], axis=0)


def columns(place, wide):
    return pl.ds(pl.multiple_of(place * wide, wide), wide)


def attend(q_ref, kv_ref, p_ref, low_ref, inverse_ref, plan, mask, done):
    rows = q_ref.shape[0] // 2
    width = q_ref.shape[1]

    @pl.loop(0, width // PAIR)
    def _(pair):
        lanes = columns(pair, PAIR)
        values = columns(width // PAIR + pair, PAIR)
        spot = columns(pair, 2 * rows)
        for seq, blocks in enumerate(plan):
            mine = slice(seq * rows, (seq + 1) * rows)
            queries = by_head(q_ref[mine, lanes])
            scores, tops = [], []
            for block in blocks:
                s = nt(kv_ref[block * rows : (block + 1) * rows, lanes], queries)
                s, far = mask(block, s)
                scores.append((s, far))
                tops.append(jnp.max(s, axis=0, keepdims=True) - far)
            top = functools.reduce(jnp.maximum, tops)
            total = jnp.zeros_like(top)
            mixed = jnp.zeros((PAIR, 2 * rows), WIDE)
            for block, (s, far) in zip(blocks, scores):
                at = slice(block * rows, (block + 1) * rows)
                p = jnp.exp(s - (top + far))
                total = total + jnp.sum(p, axis=0, keepdims=True)
                p = p.astype(LOW)
                p_ref[at, spot] = p
                mixed = mixed + tn(kv_ref[at, values], p)
            inverse = 1.0 / total
            low_ref[mine, lanes] = own_parts(mixed * inverse).T.astype(LOW)
            inverse_ref[pl.ds(2 * pair + seq, 1), :] = inverse
        done(pair)


def attend_back(up, low_ref, inverse_ref, q_ref, kv_ref, p_ref, dq_ref, dkv_ref, plan, ready, done):
    rows = q_ref.shape[0] // 2
    width = q_ref.shape[1]
    scale = HEAD ** (-0.5)

    @pl.loop(0, width // PAIR)
    def _(pair):
        lanes = columns(pair, PAIR)
        values = columns(width // PAIR + pair, PAIR)
        slot = lax.rem(pair, 2)
        ready(pair)
        for seq, blocks in enumerate(plan):
            mine = slice(seq * rows, (seq + 1) * rows)
            queries = by_head(q_ref[mine, lanes])
            inverse = inverse_ref[pl.ds(2 * pair + seq, 1), :]
            scaled = up[mine, lanes].astype(WIDE) * own_parts(jnp.broadcast_to(inverse, (PAIR, 2 * rows))).T
            inner = (scaled * low_ref[mine, lanes].astype(WIDE)).T
            offset = jnp.concatenate(
                [
                    jnp.sum(inner[:HEAD], axis=0, keepdims=True),
                    jnp.sum(inner[HEAD:], axis=0, keepdims=True),
                ],
                axis=1,
            )
            upper = by_head(scaled.astype(LOW))
            dq = jnp.zeros((PAIR, 2 * rows), WIDE)
            for block in blocks:
                at = slice(block * rows, (block + 1) * rows)
                p = p_ref[slot, at, :]
                dp = nt(kv_ref[at, values], upper)
                ds = (p.astype(WIDE) * (dp - offset)).astype(LOW)
                dkv_ref[at, values] = nn(p, upper).astype(LOW)
                dkv_ref[at, lanes] = nn(ds, queries).astype(LOW)
                dq = dq + tn(kv_ref[at, lanes], ds)
            dq_ref[mine, lanes] = (own_parts(dq).T * scale).astype(LOW)
        done(pair)


def columns_copy(source, target, sem, place, wide):
    at = columns(place, wide)
    return pltpu.make_async_copy(source.at[:, at], target.at[:, at], sem)


def plan_of(n):
    return (tuple(range(n)), tuple(range(n, n + n // 4)))


def add_terms(out, refs, terms):
    for j in range(out.shape[0]):
        total = refs[j * terms][...]
        for ref in refs[j * terms + 1 : (j + 1) * terms]:
            total = total + ref[...]
        out[j] = total


def self_kernel(n, terms, order, rank, x, *refs):
    xl, refs = refs[: n - 1], refs[n - 1 :]
    shorts, refs = refs[: terms * (n // 4)], refs[terms * (n // 4) :]
    (
        w_in, w_out, w_cq, gains, shifts,
        q, kv_far, p_far, mixed, inverse, after, cq, n1, xs, kv, p, sems,
    ) = refs
    pairs = q.shape[1] // PAIR
    kv_save = pltpu.make_async_copy(kv, kv_far, sems.at[pairs])

    def p_save(pair):
        return columns_copy(p, p_far, sems.at[pair], pair, p.shape[1] // pairs)
    add_terms(xs, shorts, terms)
    rows, width = x.shape[1:]
    r = rank[0]

    def first_norm(v):
        return (standard(v.astype(WIDE))[0] * gains[0:1] + shifts[0:1]).astype(LOW)

    def keys(v, block):
        kv[block * rows : (block + 1) * rows, :] = nn(first_norm(v), w_in[:, width:]).astype(LOW)

    mine = jnp.concatenate([x[order[0]], x[order[1]]], axis=0)
    normed = first_norm(mine)
    kv[0:rows, :] = nn(normed[:rows], w_in[:, width:]).astype(LOW)
    for d in range(1, n):
        keys(xl[d - 1][...], d)
    for j in range(n // 4):
        keys(xs[j], n + j)
    kv_save.start()
    q[...] = nn(normed, w_in[:, :width]).astype(LOW) * HEAD ** (-0.5)

    def mask(block, s):
        if 0 < block < n:
            return s, jnp.where(r >= block, 0.0, FAR)
        key = lax.broadcasted_iota(jnp.int32, s.shape, 0)
        query = lax.broadcasted_iota(jnp.int32, s.shape, 1)
        query = jnp.where(query >= rows, query - rows, query)
        if block >= n:
            query = query + (r - (block - n)) * rows
        return jnp.where(key <= query, s, -FAR), 0.0

    attend(q, kv, p, mixed, inverse, plan_of(n), mask, lambda pair: p_save(pair).start())
    total = mine.astype(WIDE) + nn(mixed[...], w_out[...])
    after[...] = total
    second = (standard(total)[0] * gains[1:2] + shifts[1:2]).astype(LOW)
    n1[...] = second
    cq[...] = nn(second, w_cq[...]).astype(LOW) * HEAD ** (-0.5)
    kv_save.wait()
    for pair in range(pairs):
        p_save(pair).wait()


def cross_kernel(n, terms, order, rank, breaks, enc, *refs):
    el, refs = refs[: n - 1], refs[n - 1 :]
    shorts, refs = refs[: terms * (n // 4)], refs[terms * (n // 4) :]
    cq, after, w_cm, w_out, kv_far, p_far, mixed, inverse, crossed, es, kv, p, sems = refs
    pairs = cq.shape[1] // PAIR
    kv_save = pltpu.make_async_copy(kv, kv_far, sems.at[pairs])

    def p_save(pair):
        return columns_copy(p, p_far, sems.at[pair], pair, p.shape[1] // pairs)
    add_terms(es, shorts, terms)
    rows, width = enc.shape[1:]
    r = rank[0]
    kv[0:rows, :] = nn(enc[order[0]], w_cm[...]).astype(LOW)
    for d in range(1, n):
        kv[d * rows : (d + 1) * rows, :] = nn(el[d - 1][...], w_cm[...]).astype(LOW)
    for j in range(n // 4):
        kv[(n + j) * rows : (n + j + 1) * rows, :] = nn(es[j], w_cm[...]).astype(LOW)

    kv_save.start()

    def mask(block, s):
        key = lax.broadcasted_iota(jnp.int32, s.shape, 0)
        if block < n:
            first = lax.rem(r - block + n, n) * rows
            which = order[0]
        else:
            first = (block - n) * rows
            which = order[1]
        shut = key == breaks[which, 0] - first
        for i in range(1, breaks.shape[1]):
            shut = shut | (key == breaks[which, i] - first)
        return jnp.where(shut, -FAR, s), 0.0

    attend(cq, kv, p, mixed, inverse, plan_of(n), mask, lambda pair: p_save(pair).start())
    crossed[...] = after[...] + nn(mixed[...], w_out[...])
    kv_save.wait()
    for pair in range(pairs):
        p_save(pair).wait()


def spread(sums, code, value, lane):
    tall = sums.shape[1]
    for k in range(sums.shape[0]):
        part = value[k * tall : (k + 1) * tall, :]
        sums[k ^ code, :, lane : lane + value.shape[1]] = part


def feed_kernel(
    order, codes, crossed, cot, w_up, b_up, w_down, b_down, gains, shifts,
    out, grad, near, far, g_bias, g_small, third, total, back, sums, sems,
):
    rows, width = cot.shape[1:]
    hidden = w_up.shape[1]
    half, tall = near.shape[:2]
    deep = hidden // (2 * half)
    third[...] = (standard(crossed[...])[0] * gains[2:3] + shifts[2:3]).astype(LOW)
    up_low = jnp.concatenate([cot[order[0]], cot[order[1]]], axis=0)
    total[...] = crossed[...] + b_down[...].astype(WIDE)
    back[...] = jnp.zeros_like(back)

    @pl.loop(0, hidden // width)
    def _(c):
        at = columns(c, width)
        rising = nn(third[...], w_up[:, at]) + b_up[:, at].astype(WIDE)
        active, slope = gelu_pair(rising)
        active = active.astype(LOW)
        total[...] += nn(active, w_down[at, :])
        rising_grad = nt(up_low, w_down[at, :]) * slope
        g_bias[:, at] = jnp.sum(rising_grad, axis=0, keepdims=True)
        rising_grad = rising_grad.astype(LOW)
        back[...] += nt(rising_grad, w_up[:, at])
        g_up = tn(third[...], rising_grad).astype(LOW)
        for k in range(2 * half):
            sums[k ^ codes[0], :, at] = g_up[k * tall : (k + 1) * tall]
        g_down = tn(active, up_low).astype(LOW)
        for k in range(width // deep):
            for i in range(deep // tall):
                first = k * deep + i * tall
                lanes = slice(hidden + i * width, hidden + (i + 1) * width)
                sums[(c * (width // deep) + k) ^ codes[1], :, lanes] = g_down[first : first + tall]

    saves = [
        pltpu.make_async_copy(sums.at[:half], near, sems.at[0]),
        pltpu.make_async_copy(sums.at[half:], far, sems.at[1]),
    ]
    for save in saves:
        save.start()
    low = total[...].astype(LOW)
    out[order[0]] = low[:rows]
    out[order[1]] = low[rows:]
    upward = up_low.astype(WIDE)
    inner, gain, shift = norm_back(crossed[...], gains[2:3], back[...])
    grad[...] = upward + inner
    g_small[0, :] = jnp.sum(upward, axis=0)
    g_small[1, :] = gain
    g_small[2, :] = shift
    for save in saves:
        save.wait()


def loads(kv_far, p_far, kv, p, sems):
    pairs = kv.shape[1] // (2 * PAIR)

    def p_copy(pair):
        at = columns(pair, p.shape[2])
        return pltpu.make_async_copy(p_far.at[:, at], p.at[lax.rem(pair, 2)], sems.at[pair])

    def kv_copies(pair):
        return (
            columns_copy(kv_far, kv, sems.at[pairs + pair], pair, PAIR),
            columns_copy(kv_far, kv, sems.at[2 * pairs + pair], pairs + pair, PAIR),
        )

    for pair in range(pairs):
        if pair < 2:
            p_copy(pair).start()
        for copy in kv_copies(pair):
            copy.start()

    def ready(pair):
        for copy in (p_copy(pair), *kv_copies(pair)):
            copy.wait()

    def done(pair):
        @pl.when(pair + 2 < pairs)
        def _():
            p_copy(pair + 2).start()

    return ready, done


def put_part(parts, n, b, value):
    rows = value.shape[0]
    if b < len(parts):
        parts[b][:rows, :] = value
    else:
        parts[1][(b - n + 1) * rows : (b - n + 2) * rows, :] = value


def cross_back_kernel(n, order, enc, *refs):
    el, es, refs = refs[: n - 1], refs[n - 1], refs[n:]
    (grad, mixed, inverse, cq, kv_far, p_far, after, n1, w_cm, w_cout, w_cq, gains) = refs[:12]
    parts, (self_grad, g_cross, g_small, dq, up, dkv, kv, p, sems) = refs[12:-9], refs[-9:]
    ready, done = loads(kv_far, p_far, kv, p, sems)
    rows, width = enc.shape[1:]
    low = grad[...].astype(LOW)
    g_cross[:, 3 * width :] = tn(mixed[...], low).astype(LOW)
    up[...] = nt(low, w_cout[...]).astype(LOW)
    attend_back(up, mixed, inverse, cq, kv, p, dq, dkv, plan_of(n), ready, done)
    dq_low = dq[...]
    g_cross[:, 2 * width : 3 * width] = tn(n1[...], dq_low).astype(LOW)
    total = tn(enc[order[0]], dkv[0:rows, :])
    for d in range(1, n):
        total = total + tn(el[d - 1][...], dkv[d * rows : (d + 1) * rows, :])
    for j in range(n // 4):
        total = total + tn(es[j], dkv[(n + j) * rows : (n + j + 1) * rows, :])
    g_cross[:, : 2 * width] = total.astype(LOW)
    for b in range(n + n // 4):
        put_part(parts, n, b, nt(dkv[b * rows : (b + 1) * rows, :], w_cm[...]).astype(LOW))
    inner, gain, shift = norm_back(after[...], gains[1:2], nt(dq_low, w_cq[...]))
    self_grad[...] = grad[...] + inner
    g_small[0, :] = gain
    g_small[1, :] = shift


def self_back_kernel(n, order, codes, x, *refs):
    xl, refs = refs[: n - 1], refs[n - 1 :]
    (
        xs, self_grad, mixed, inverse, q, kv_far, p_far, w_in, w_out, gains, shifts, small_feed, g_bias,
        small_cross, g_cross, _,
    ) = refs[:16]
    parts, (own, near, far, sums, dq, up, dkv, kv, p, sems) = refs[16:-10], refs[-10:]
    ready, done = loads(kv_far, p_far, kv, p, sems)
    rows, width = x.shape[1:]
    low = self_grad[...].astype(LOW)
    up[...] = nt(low, w_out[...]).astype(LOW)
    attend_back(up, mixed, inverse, q, kv, p, dq, dkv, plan_of(n), ready, done)
    mine = jnp.concatenate([x[order[0]], x[order[1]]], axis=0).astype(WIDE)
    unit = standard(mine)[0]
    normed = (unit * gains[0:1] + shifts[0:1]).astype(LOW)
    g_out = tn(mixed[...], low).astype(LOW)
    g_query = tn(normed, dq[...]).astype(LOW)
    mine = nt(dq[...], w_in[:, :width])
    own[...] = mine
    gain = jnp.sum(mine * unit, axis=0)
    shift = jnp.sum(mine, axis=0)
    total = None
    for b in range(n + n // 4):
        if b == 0:
            key_unit, key_low = unit[:rows], normed[:rows]
        else:
            v = xl[b - 1][...] if b < n else xs[b - n]
            key_unit = standard(v.astype(WIDE))[0]
            key_low = (key_unit * gains[0:1] + shifts[0:1]).astype(LOW)
        pairs = dkv[b * rows : (b + 1) * rows, :]
        term = tn(key_low, pairs)
        total = term if total is None else total + term
        back = nt(pairs, w_in[:, width:])
        put_part(parts, n, b, back.astype(LOW))
        gain = gain + jnp.sum(back * key_unit, axis=0)
        shift = shift + jnp.sum(back, axis=0)
    small = [gain[None], small_cross[0:1], small_feed[1:2], shift[None], small_cross[1:2],
             small_feed[2:3], small_feed[0:1], g_bias[...]]
    small = [v[:, i : i + 128] for v in small for i in range(0, v.shape[1], 128)]
    small.append(jnp.zeros((width - len(small), 128), WIDE))
    small = jnp.concatenate(small, axis=0).astype(LOW)
    spread(sums, codes[0], g_cross, 0)
    spread(sums, codes[1], g_query, 4 * width)
    spread(sums, codes[1], total.astype(LOW), 5 * width)
    spread(sums, codes[1], g_out, 7 * width)
    spread(sums, codes[1], small, 8 * width)
    half = sums.shape[0] // 2
    saves = [
        pltpu.make_async_copy(sums.at[:half], near, sems.at[0]),
        pltpu.make_async_copy(sums.at[half:], far, sems.at[1]),
    ]
    for save in saves:
        save.start()
    for save in saves:
        save.wait()


def unpack(plan, codes, pieces, outs):
    for out, (at, count, which, lane, side) in zip(outs, plan):
        wide = out.shape[1]
        depth, tall = pieces[at].shape[:2]
        for k in range(count * depth):
            first = (codes[which] ^ k) * (tall * side)
            for i in range(side):
                start = pl.multiple_of(first + i * tall, tall)
                lanes = slice(lane + i * wide, lane + (i + 1) * wide)
                out[pl.ds(start, tall), :] = pieces[at + k // depth][k % depth, :, lanes].astype(WIDE)


def unpack_feed_kernel(plan, codes, *refs):
    unpack(plan, codes, refs[: -len(plan)], refs[-len(plan) :])


def unpack_rest_kernel(plan, codes, *refs):
    *refs, up_bias, down_bias, gains, shifts, small = refs
    count = len(plan) - 1
    unpack(plan, codes, refs[:-count], refs[-count:] + [small])
    at = 0
    for out, count in ((gains, 3), (shifts, 3), (down_bias, 1), (up_bias, 1)):
        for i in range(count):
            across = out.shape[1] // 128
            row = [small[at + j : at + j + 1, :] for j in range(across)]
            out[i : i + 1, :] = jnp.concatenate(row, axis=1)
            at += across


def last_kernel(n, order, rank, x, self_grad, own, gains, part, part_got, e_long, *refs):
    shorts, e_shorts, (grad, e_grad) = refs[: n // 4], refs[n // 4 : n // 2], refs[-2:]
    rows = x.shape[1]

    def mine(helds):
        total = jnp.zeros(part.shape, WIDE)
        for root, held in enumerate(helds):
            total = jnp.where(rank[0] == root, held[...].astype(WIDE), total)
        return total

    long_up = own[:rows] + part[...].astype(WIDE) + part_got[...].astype(WIDE)
    short_up = own[rows:] + mine(shorts)
    for which, up, at in ((order[0], long_up, 0), (order[1], short_up, rows)):
        inner, _, _ = norm_back(x[which].astype(WIDE), gains[0:1], up)
        grad[which] = self_grad[at : at + rows] + inner
    e_grad[order[0]] = e_long[...]
    e_grad[order[1]] = mine(e_shorts)


def add_core(near, got, *outs):
    at = 0
    half = near.shape[0] // 2
    for keep, send in zip(outs[::2], outs[1::2]):
        lanes = slice(at, at + keep.shape[2])
        keep[...] = near[:half, :, lanes] + got[:half, :, lanes]
        send[...] = near[half:, :, lanes] + got[half:, :, lanes]
        at = lanes.stop


def add_returns(own, near, near_got, *refs):
    rows = own.shape[0]
    count = near.shape[0] // rows
    total = own[...].astype(WIDE) + near_got[:rows, :].astype(WIDE)
    for ref in refs[:-count]:
        total = total + ref[...].astype(WIDE)
    refs[-count][...] = total
    for k in range(1, count):
        at = slice(k * rows, (k + 1) * rows)
        refs[k - count][...] = near[at, :] + near_got[at, :]


def add_halves(keep, got, *outs):
    half = keep.shape[0] // 2
    outs[-2][...] = keep[:half] + got[:half]
    outs[-1][...] = keep[half:] + got[half:]


def add_to_pieces(a, got_a, b, got_b, *outs):
    wide = a.shape[2]
    for k, out in enumerate(outs[-a.shape[0] :]):
        out[:, :, :wide] = a[k : k + 1] + got_a[k : k + 1]
        out[:, :, wide:] = b[k : k + 1] + got_b[k : k + 1]


def note(*refs):
    pass


def add_all(_, *refs):
    *parts, out = refs
    total = parts[0][...].astype(WIDE)
    for part in parts[1:]:
        total = total + part[...].astype(WIDE)
    out[...] = total.astype(out.dtype)


def lay_whole(_, *refs):
    for k, ref in enumerate(refs[:-1]):
        refs[-1][k : k + 1] = ref[...]


def lay(*refs):
    *parts, a, b = refs
    wide = a.shape[2]
    for k, part in enumerate(parts):
        a[k : k + 1] = part[:, :, :wide]
        b[k : k + 1] = part[:, :, wide:]


def join(a, b, out):
    out[: a.shape[0]] = a[...]
    out[a.shape[0] :] = b[...]


def beside(a, got_a, b, got_b, out):
    half, _, wide = a.shape
    out[:half, :, :wide] = a[...]
    out[half:, :, :wide] = got_a[...]
    out[:half, :, wide:] = b[...]
    out[half:, :, wide:] = got_b[...]


def steps_kernel(steps, *refs):
    refs = list(refs)
    at_in, at_out = 0, sum(count for _, count, _ in steps)
    for kernel, ins, outs in steps:
        kernel(*refs[at_in : at_in + ins], *refs[at_out : at_out + outs])
        at_in += ins
        at_out += outs


def call(kernel, ins, outs, us, scratch=(), smem=0, room=62, far_ins=(), far_outs=(), sems=0):
    vmem = pl.BlockSpec(memory_space=pltpu.VMEM)
    far = pl.BlockSpec(memory_space=pltpu.HBM)
    in_specs = [vmem] * len(ins)
    in_specs[:smem] = [pl.BlockSpec(memory_space=pltpu.SMEM)] * smem
    for i in far_ins:
        in_specs[i] = far
    scratch_shapes = [pltpu.VMEM(s, t) for s, t in scratch]
    if sems:
        scratch_shapes.append(pltpu.SemaphoreType.DMA((sems,)))
    return pl.pallas_call(
        kernel,
        out_shape=[jax.ShapeDtypeStruct(s, t) for s, t in outs],
        in_specs=in_specs,
        out_specs=[far if i in far_outs else vmem for i in range(len(outs))],
        scratch_shapes=scratch_shapes,
        compiler_params=pltpu.CompilerParams(vmem_limit_bytes=room << 20),
        cost_estimate=pl.CostEstimate(flops=us * 10**9, bytes_accessed=0, transcendentals=0),
    )(*ins)


def small_steps(steps):
    outs = call(
        functools.partial(steps_kernel, [(k, len(i), len(o)) for k, i, o in steps]),
        [v for _, ins, _ in steps for v in ins],
        [o if isinstance(o[0], tuple) else (o, LOW) for _, _, outs in steps for o in outs],
        2,
        room=20,
    )
    got = []
    for _, _, shapes in steps:
        got.append(outs[: len(shapes)])
        outs = outs[len(shapes) :]
    return got


def send_long(block, n, wrap):
    got = []
    for d in range(1, n):
        pairs = [(i, (i + d) % n) for i in range(n) if wrap or i + d < n]
        got.append(lax.ppermute(block, "blk", pairs))
    return got


def return_long(block, n, distance, wrap):
    pairs = [(i, (i - distance) % n) for i in range(n) if wrap or i >= distance]
    return lax.ppermute(block, "blk", pairs)


def return_short(held, n, root, distance):
    pairs = [((root + k + distance) % n, (root + k) % n) for k in range(0, n, 2 * distance)]
    return lax.ppermute(held, "blk", pairs)


def return_short_rest(helds, n):
    got = []
    for root, held in enumerate(helds):
        d = 4
        while d < n:
            held = held + return_short(held, n, root, d)
            d *= 2
        got.append(held)
    return got


def send_short_first(block, n, rank):
    got = []
    for root in range(n // 4):
        held = jnp.where(rank == root, block, jnp.zeros_like(block))
        got.append([held, lax.ppermute(held, "blk", [(root, (root + n // 2) % n)])])
    return got


def send_short_rest(terms, n):
    for root in range(n // 4):
        d = n // 4
        while d:
            pairs = [((root + k) % n, (root + k + d) % n) for k in range(0, n, 2 * d)]
            held = functools.reduce(jnp.add, terms[root])
            terms[root].append(lax.ppermute(held, "blk", pairs))
            d //= 2
    return [v for several in terms for v in several]


def tied(value, *others):
    return lax.optimization_barrier((value, others))[0]


def trade(v, axis, distance):
    return lax.ppermute(v, axis, [(i, i ^ distance) for i in range(lax.axis_size(axis))])


class Sharing:
    def __init__(self, batch, n):
        self.rest = [("batch", d) for d in (8, 16, 32) if d < batch]
        self.rest += [("blk", d) for d in (4, 8, 16, 32) if d < n]
        self.chunks = 32

    def codes(self):
        codes = []
        for first, second in ((2, 4), (4, 2)):
            code = jnp.int32(0)
            for axis, distance in (("batch", 1), ("batch", first), ("batch", second), ("blk", 2),
                                   ("blk", 1)):
                code = 2 * code + (lax.axis_index(axis) // distance) % 2
            codes.append(code.astype(jnp.int32))
        return jnp.stack(codes)

    def doubled(self, v):
        for axis, distance in self.rest:
            v = v + trade(v, axis, distance)
        return v


def to_tall(pieces):
    return [trade(v, "blk", j) for j, v in enumerate(pieces) if j]


def on_device(
    decoder_input, encoder_output, sequence_lengths, chain_breaks,
    self_inward, self_outward, cross_query, cross_memory, cross_outward,
    feed_up, feed_up_bias, feed_down, feed_down_bias, norm_gains, norm_shifts,
    output_cotangent,
):
    sequences, rows, width = decoder_input.shape
    hidden = feed_up.shape[1]
    n = lax.axis_size("blk")
    rank = lax.axis_index("blk")
    ranks = rank.astype(jnp.int32)[None]
    longest = (sequence_lengths[1] > sequence_lengths[0]).astype(jnp.int32)
    order = jnp.stack([longest, 1 - longest])
    both = 2 * rows
    nk = (n + n // 4) * rows
    pairs = width // PAIR

    def pick(v, i):
        return jnp.where(order[i] == 0, v[0], v[1])

    sharing = Sharing(lax.axis_size("batch"), n)
    codes = sharing.codes()
    chunks = sharing.chunks
    tall = width // chunks
    blocks = nk // rows

    room = 62 if n > 4 else 40
    x_long, x_short = pick(decoder_input, 0), pick(decoder_input, 1)
    e_long, e_short = pick(encoder_output, 0), pick(encoder_output, 1)
    firsts = send_short_first(jnp.concatenate([x_short, e_short]), n, rank)
    xl = send_long(x_long, n, False)
    xs = send_short_rest([[v[:rows] for v in terms] for terms in firsts], n)
    shorts = len(xs) // (n // 4)
    e_long = tied(e_long, *xl)
    es = send_short_rest([[tied(v[rows:], *xl) for v in terms] for terms in firsts], n)
    el = send_long(e_long, n, True)

    kept = [((nk, 2 * width), LOW), ((nk, pairs * both), LOW)]
    loaded = [kept[0], ((2, nk, both), LOW)]
    inverses = ((2 * pairs, both), WIDE)
    low_rows, wide_rows = ((both, width), LOW), ((both, width), WIDE)
    q, kv, p, mixed, inverse, after, cq, n1, xs = call(
        functools.partial(self_kernel, n, shorts),
        (order, ranks, decoder_input, *xl, *xs, self_inward, self_outward, cross_query,
         norm_gains, norm_shifts),
        [low_rows, *kept, low_rows, inverses, wide_rows, low_rows, low_rows,
         ((n // 4, rows, width), LOW)],
        12,
        scratch=kept,
        smem=2,
        room=room,
        far_outs=(1, 2),
        sems=pairs + 1,
    )
    ckv, cp, cmixed, cinverse, crossed, es = call(
        functools.partial(cross_kernel, n, shorts),
        (order, ranks, chain_breaks, encoder_output, *el, *es, cq, after, cross_memory,
         cross_outward),
        [*kept, low_rows, inverses, wide_rows, ((n // 4, rows, width), LOW)],
        11,
        scratch=kept,
        smem=3,
        room=room,
        far_outs=(0, 1),
        sems=pairs + 1,
    )
    half = chunks // 2
    layer_output, cross_grad, near, far, g_bias, small_feed = call(
        feed_kernel,
        (order, codes, crossed, output_cotangent, feed_up, feed_up_bias[None], feed_down,
         feed_down_bias[None], norm_gains, norm_shifts),
        [(decoder_input.shape, LOW), ((both, width), WIDE), ((half, tall, 2 * hidden), LOW),
         ((half, tall, 2 * hidden), LOW), ((1, hidden), WIDE), ((3, width), WIDE)],
        14,
        scratch=[low_rows, wide_rows, wide_rows, ((chunks, tall, 2 * hidden), LOW)],
        smem=2,
        room=room,
        far_outs=(2, 3),
        sems=2,
    )
    wide = [hidden, hidden]
    wide_rest = [hidden, hidden + 128]

    def shape(count, lanes):
        return (count, tall, lanes)

    roots = range(n // 4)
    part_shapes = [((rows, width), LOW)] * n
    part_shapes[1] = (((n // 4 + 1) * rows, width), LOW)
    feed_core = trade(far, "batch", 1)
    feed_near = near
    *e_parts, self_grad, g_cross, small_cross = call(
        functools.partial(cross_back_kernel, n),
        (order, encoder_output, *el, es, cross_grad, cmixed, cinverse,
         cq, ckv, cp, after, n1, cross_memory, cross_outward, cross_query, norm_gains),
        part_shapes + [((both, width), WIDE), ((width, 4 * width), LOW), ((2, width), WIDE)],
        14,
        scratch=[low_rows, low_rows, kept[0], *loaded],
        smem=1,
        room=room,
        far_ins=(n + 6, n + 7),
        sems=3 * pairs,
    )
    (a, a_send, b, b_send), _ = small_steps(
        [(add_core, (feed_near, feed_core), [shape(8, w) for w in wide for _ in "ks"]),
         (note, (small_cross,), [])]
    )
    a_got, b_got = trade(a_send, "batch", 2), trade(b_send, "batch", 4)
    e_got = [return_long(e_parts[d], n, d, True) for d in range(1, n)]
    *parts, own, near, far = call(
        functools.partial(self_back_kernel, n),
        (order, codes, decoder_input, *xl, xs, self_grad, mixed, inverse, q, kv, p, self_inward,
         self_outward, norm_gains, norm_shifts, small_feed, g_bias, small_cross, g_cross, a),
        [((rows, width), LOW)] * blocks
        + [((both, width), WIDE), (shape(half, sum(wide_rest)), LOW),
           (shape(half, sum(wide_rest)), LOW)],
        16,
        scratch=[(shape(chunks, sum(wide_rest)), LOW), low_rows, low_rows, kept[0], *loaded],
        smem=2,
        room=room,
        far_ins=(n + 7, n + 8),
        far_outs=(blocks + 1, blocks + 2),
        sems=3 * pairs,
    )
    (a, a_send), (b, b_send), (e_long, *e_short) = small_steps(
        [(add_halves, (a, a_got, own), [shape(4, wide[0])] * 2),
         (add_halves, (b, b_got), [shape(4, wide[1])] * 2),
         (add_returns, (e_parts[0], e_parts[1], *e_got),
          [((rows, width), WIDE)] + [(rows, width)] * (n // 4))]
    )
    a_got, b_got = trade(a_send, "batch", 4), trade(b_send, "batch", 2)
    e_got = [return_short(e_short[k], n, k, 2) for k in roots]
    feed, (a, a_send, b, b_send), *e_short = small_steps(
        [(add_to_pieces, (a, a_got, b, b_got), [shape(1, sum(wide))] * 4),
         (add_core, (near, trade(tied(far, a_send), "batch", 1)),
          [shape(8, w) for w in wide_rest for _ in "ks"])]
        + [(add_all, (own, e_short[k], e_got[k]), [(rows, width)]) for k in roots]
    )
    e_short = return_short_rest([v for v, in e_short], n)
    a_got, b_got = trade(a_send, "batch", 2), trade(b_send, "batch", 4)
    (a, a_send), (b, b_send), (feed,) = small_steps(
        [(add_halves, (a, a_got), [shape(4, wide_rest[0])] * 2),
         (add_halves, (b, b_got), [shape(4, wide_rest[1])] * 2),
         (add_all, (own, feed[0], *to_tall(feed)), [shape(1, sum(wide))])]
    )
    feed = sharing.doubled(feed)
    a_got, b_got = trade(a_send, "batch", 4), trade(b_send, "batch", 2)
    rest, (fa, fb) = small_steps(
        [(add_to_pieces, (a, a_got, b, b_got), [shape(1, sum(wide_rest))] * 4),
         (lay, (feed, *to_tall([feed] * 4)), [shape(4, w) for w in wide])]
    )
    (rest,), (fa,), (fb,) = small_steps(
        [(add_all, (own, rest[0], *to_tall(rest)), [shape(1, sum(wide_rest))]),
         (join, (fa, trade(fa, "batch", 4)), [shape(8, wide[0])]),
         (join, (fb, trade(fb, "batch", 2)), [shape(8, wide[1])])]
    )
    rest = sharing.doubled(rest)
    (ra, rb), (feed,) = small_steps(
        [(lay, (rest, *to_tall([rest] * 4)), [shape(4, w) for w in wide_rest]),
         (beside, (fa, trade(fa, "batch", 2), fb, trade(fb, "batch", 4)),
          [shape(16, sum(wide))])]
    )
    ra_got, rb_got = trade(ra, "batch", 4), trade(rb, "batch", 2)
    feed_got = trade(feed, "batch", 1)
    held, *shorts = tied((parts[n - 1], *parts[n:]), ra)
    for d in range(n - 2, 2, -1):
        held = parts[d] + return_long(held, n, 1, False)
    long_got = return_long(held, n, 1, False)
    got = [return_short(shorts[k], n, k, 1) for k in roots]
    (ra,), (rb,), _, (held,), *shorts = small_steps(
        [(join, (ra, ra_got), [shape(8, wide_rest[0])]),
         (join, (rb, rb_got), [shape(8, wide_rest[1])]),
         (note, (feed_got,), []),
         (add_all, (own, parts[2], long_got), [(rows, width)])]
        + [(add_all, (own, parts[n + k], got[k]), [(rows, width)]) for k in roots]
    )
    ra_got, rb_got = trade(ra, "batch", 2), trade(rb, "batch", 4)
    long_got = return_long(held, n, 1, False)
    got = [return_short(shorts[k][0], n, k, 2) for k in roots]
    s_up, s_down = call(
        functools.partial(unpack_feed_kernel, [(0, 2, 0, 0, 1), (0, 2, 1, hidden, hidden // width)]),
        (codes, feed, feed_got),
        [(feed_up.shape, WIDE), (feed_down.shape, WIDE)],
        6,
        smem=1,
        room=room,
    )
    (rest,), _, (held,), *shorts = small_steps(
        [(beside, (ra, ra_got, rb, rb_got), [shape(16, sum(wide_rest))]),
         (note, (s_down[:8, :128],), []),
         (add_all, (own, parts[1], long_got), [(rows, width)])]
        + [(add_all, (own, shorts[k][0], got[k]), [(rows, width)]) for k in roots]
    )
    shorts = return_short_rest([v for v, in shorts], n)
    long_got = return_long(held, n, 1, False)
    rest_got = trade(rest, "batch", 1)
    input_gradient, encoder_gradient = call(
        functools.partial(last_kernel, n),
        (order, ranks, decoder_input, self_grad, own, norm_gains, parts[0], long_got, e_long,
         *shorts, *e_short),
        [(decoder_input.shape, WIDE), (decoder_input.shape, WIDE)],
        3,
        smem=2,
        room=room,
    )
    at = hidden
    places = [(0, 2, 0, 0, 1), (0, 2, 0, 2 * width, 1), (0, 2, 0, 3 * width, 1),
              (0, 2, 1, at, 1), (0, 2, 1, at + 3 * width, 1), (0, 2, 1, at + 4 * width, 1)]
    s_cm, s_cq, s_cout, s_in, s_out, up_bias, down_bias, gains, shifts = call(
        functools.partial(unpack_rest_kernel, places),
        (codes, rest, rest_got),
        [(s, WIDE) for s in (cross_memory.shape, cross_query.shape, cross_outward.shape,
                             self_inward.shape, self_outward.shape, (1, hidden), (1, width),
                             norm_gains.shape, norm_shifts.shape)],
        5,
        scratch=[((width, 128), WIDE)],
        smem=1,
        room=room,
    )
    return (
        layer_output, input_gradient, encoder_gradient, s_in, s_out, s_cq, s_cm, s_cout,
        s_up, up_bias[0], s_down, down_bias[0], gains, shifts,
    )


def solution(mesh):
    blocked = P("batch", "blk", None)
    placed = (blocked, blocked, P("batch"), P("batch", None)) + (P(),) * 11 + (blocked,)
    return jax.shard_map(
        on_device,
        mesh=mesh,
        in_specs=placed,
        out_specs=(blocked,) * 3 + (P(),) * 11,
        check_vma=False,
    )
```

```python
import functools

import jax
import jax.numpy as jnp
from jax import lax
from jax.experimental import pallas as pl
from jax.experimental.pallas import tpu as pltpu
from jax.sharding import PartitionSpec as P

HEAD = 64
PAIR = 2 * HEAD
EPSILON = 1e-05
FAR = 1e30
LOW = jnp.bfloat16
WIDE = jnp.float32


def contract(left, right, a, b):
    return lax.dot_general(left, right, (((a,), (b,)), ((), ())), preferred_element_type=WIDE)


def nn(left, right):
    return contract(left, right, 1, 0)


def nt(left, right):
    return contract(left, right, 1, 1)


def tn(left, right):
    return contract(left, right, 0, 0)


def standard(values):
    center = values - jnp.mean(values, axis=-1, keepdims=True)
    spread = jnp.mean(center * center, axis=-1, keepdims=True)
    inverse = lax.rsqrt(spread + EPSILON)
    return center * inverse, inverse


def norm_back(values, gain, upstream):
    unit, inverse = standard(values)
    m = upstream * gain
    grad = inverse * (
        m
        - jnp.mean(m, axis=-1, keepdims=True)
        - unit * jnp.mean(m * unit, axis=-1, keepdims=True)
    )
    return grad, jnp.sum(upstream * unit, axis=0), jnp.sum(upstream, axis=0)


def gelu_pair(x):
    z = jnp.abs(x) * 0.7071067811865476
    t = 1.0 / (1.0 + 0.5 * z)
    poly = 0.17087277
    for c in (
        -0.82215223,
        1.48851587,
        -1.13520398,
        0.27886807,
        -0.18628806,
        0.09678418,
        0.37409196,
        1.00002368,
        -1.26551223,
    ):
        poly = poly * t + c
    bell = jnp.exp(-z * z)
    tail = 0.5 * t * jnp.exp(poly) * bell
    share = jnp.where(x >= 0, 1.0 - tail, tail)
    return x * share, share + x * bell * 0.3989422804014327


def by_head(pair_rows):
    lane = lax.broadcasted_iota(jnp.int32, pair_rows.shape, 1)
    zero = jnp.zeros_like(pair_rows)
    return jnp.concatenate(
        [jnp.where(lane < HEAD, pair_rows, zero), jnp.where(lane >= HEAD, pair_rows, zero)], axis=0
    )


def own_parts(both):
    rows = both.shape[1] // 2
    return jnp.concatenate([both[:HEAD, :rows], both[HEAD:, rows:]], axis=0)


def columns(place, wide):
    return pl.ds(pl.multiple_of(place * wide, wide), wide)


def attend(q_ref, kv_ref, p_ref, low_ref, inverse_ref, plan, mask, done):
    rows = q_ref.shape[0] // 2
    width = q_ref.shape[1]

    @pl.loop(0, width // PAIR)
    def _(pair):
        lanes = columns(pair, PAIR)
        values = columns(width // PAIR + pair, PAIR)
        spot = columns(pair, 2 * rows)
        for seq, blocks in enumerate(plan):
            mine = slice(seq * rows, (seq + 1) * rows)
            queries = by_head(q_ref[mine, lanes])
            scores, tops = [], []
            for block in blocks:
                s = nt(kv_ref[block * rows : (block + 1) * rows, lanes], queries)
                s, far = mask(block, s)
                scores.append((s, far))
                tops.append(jnp.max(s, axis=0, keepdims=True) - far)
            top = functools.reduce(jnp.maximum, tops)
            total = jnp.zeros_like(top)
            mixed = jnp.zeros((PAIR, 2 * rows), WIDE)
            for block, (s, far) in zip(blocks, scores):
                at = slice(block * rows, (block + 1) * rows)
                p = jnp.exp(s - (top + far))
                total = total + jnp.sum(p, axis=0, keepdims=True)
                p = p.astype(LOW)
                p_ref[at, spot] = p
                mixed = mixed + tn(kv_ref[at, values], p)
            inverse = 1.0 / total
            low_ref[mine, lanes] = own_parts(mixed * inverse).T.astype(LOW)
            inverse_ref[pl.ds(2 * pair + seq, 1), :] = inverse
        done(pair)


def attend_back(up, low_ref, inverse_ref, q_ref, kv_ref, p_ref, dq_ref, dkv_ref, plan, ready, done):
    rows = q_ref.shape[0] // 2
    width = q_ref.shape[1]
    scale = HEAD ** (-0.5)

    @pl.loop(0, width // PAIR)
    def _(pair):
        lanes = columns(pair, PAIR)
        values = columns(width // PAIR + pair, PAIR)
        slot = lax.rem(pair, 2)
        ready(pair)
        for seq, blocks in enumerate(plan):
            mine = slice(seq * rows, (seq + 1) * rows)
            queries = by_head(q_ref[mine, lanes])
            inverse = inverse_ref[pl.ds(2 * pair + seq, 1), :]
            scaled = up[mine, lanes].astype(WIDE) * own_parts(jnp.broadcast_to(inverse, (PAIR, 2 * rows))).T
            inner = (scaled * low_ref[mine, lanes].astype(WIDE)).T
            offset = jnp.concatenate(
                [
                    jnp.sum(inner[:HEAD], axis=0, keepdims=True),
                    jnp.sum(inner[HEAD:], axis=0, keepdims=True),
                ],
                axis=1,
            )
            upper = by_head(scaled.astype(LOW))
            dq = jnp.zeros((PAIR, 2 * rows), WIDE)
            for block in blocks:
                at = slice(block * rows, (block + 1) * rows)
                p = p_ref[slot, at, :]
                dp = nt(kv_ref[at, values], upper)
                ds = (p.astype(WIDE) * (dp - offset)).astype(LOW)
                dkv_ref[at, values] = nn(p, upper).astype(LOW)
                dkv_ref[at, lanes] = nn(ds, queries).astype(LOW)
                dq = dq + tn(kv_ref[at, lanes], ds)
            dq_ref[mine, lanes] = (own_parts(dq).T * scale).astype(LOW)
        done(pair)


def saves(kv, p, kept, sems):
    rows, width = slice(0, kv.shape[0]), kv.shape[1]
    wide = 2 * PAIR * p.shape[1] // width

    def p_save(pair):
        at = pl.ds(pl.multiple_of(width + pair * wide, PAIR), wide)
        return pltpu.make_async_copy(p.at[:, columns(pair, wide)], kept.at[rows, at], sems.at[pair])

    pairs = width // (2 * PAIR)
    return pltpu.make_async_copy(kv, kept.at[rows, :width], sems.at[pairs]), p_save


def plan_of(n):
    return (tuple(range(n)), tuple(range(n, n + n // 4)))


def add_terms(out, refs, terms):
    for j in range(out.shape[0]):
        total = refs[j * terms][...]
        for ref in refs[j * terms + 1 : (j + 1) * terms]:
            total = total + ref[...]
        out[j] = total


def pick_kernel(lengths, x, enc, x_long, e_long, *shorts):
    rows = x_long.shape[0]
    long = jnp.where(lengths[1] > lengths[0], 1, 0)
    x_long[...] = x[long]
    e_long[...] = enc[long]
    for root, ref in enumerate(shorts):
        share = (lax.axis_index("blk") == root).astype(jnp.int32).astype(WIDE)
        ref[:rows] = (x[1 - long].astype(WIDE) * share).astype(LOW)
        ref[rows:] = (enc[1 - long].astype(WIDE) * share).astype(LOW)


def self_kernel(n, terms, order, rank, x, *refs):
    xl, refs = refs[: n - 1], refs[n - 1 :]
    shorts, refs = refs[: terms * (n // 4)], refs[terms * (n // 4) :]
    (
        w_in, w_out, w_cq, gains, shifts,
        q, kept, mixed, inverse, after, cq, n1, xs, kv, p, sems,
    ) = refs
    pairs = q.shape[1] // PAIR
    kv_save, p_save = saves(kv, p, kept, sems)
    add_terms(xs, shorts, terms)
    rows, width = x.shape[1:]
    r = rank[0]

    def first_norm(v):
        return (standard(v.astype(WIDE))[0] * gains[0:1] + shifts[0:1]).astype(LOW)

    def keys(v, block):
        kv[block * rows : (block + 1) * rows, :] = nn(first_norm(v), w_in[:, width:]).astype(LOW)

    mine = jnp.concatenate([x[order[0]], x[order[1]]], axis=0)
    normed = first_norm(mine)
    kv[0:rows, :] = nn(normed[:rows], w_in[:, width:]).astype(LOW)
    for d in range(1, n):
        keys(xl[d - 1][...], d)
    for j in range(n // 4):
        keys(xs[j], n + j)
    kv_save.start()
    q[...] = nn(normed, w_in[:, :width]).astype(LOW) * HEAD ** (-0.5)

    def mask(block, s):
        if 0 < block < n:
            return s, jnp.where(r >= block, 0.0, FAR)
        key = lax.broadcasted_iota(jnp.int32, s.shape, 0)
        query = lax.broadcasted_iota(jnp.int32, s.shape, 1)
        query = jnp.where(query >= rows, query - rows, query)
        if block >= n:
            query = query + (r - (block - n)) * rows
        return jnp.where(key <= query, s, -FAR), 0.0

    attend(q, kv, p, mixed, inverse, plan_of(n), mask, lambda pair: p_save(pair).start())
    total = mine.astype(WIDE) + nn(mixed[...], w_out[...])
    after[...] = total
    second = (standard(total)[0] * gains[1:2] + shifts[1:2]).astype(LOW)
    n1[...] = second
    cq[...] = nn(second, w_cq[...]).astype(LOW) * HEAD ** (-0.5)
    kv_save.wait()
    for pair in range(pairs):
        p_save(pair).wait()


def cross_kernel(n, terms, order, rank, breaks, enc, *refs):
    el, refs = refs[: n - 1], refs[n - 1 :]
    shorts, refs = refs[: terms * (n // 4)], refs[terms * (n // 4) :]
    cq, after, w_cm, w_out, kept, mixed, inverse, crossed, es, kv, p, sems = refs
    pairs = cq.shape[1] // PAIR
    kv_save, p_save = saves(kv, p, kept, sems)
    add_terms(es, shorts, terms)
    rows, width = enc.shape[1:]
    r = rank[0]
    kv[0:rows, :] = nn(enc[order[0]], w_cm[...]).astype(LOW)
    for d in range(1, n):
        kv[d * rows : (d + 1) * rows, :] = nn(el[d - 1][...], w_cm[...]).astype(LOW)
    for j in range(n // 4):
        kv[(n + j) * rows : (n + j + 1) * rows, :] = nn(es[j], w_cm[...]).astype(LOW)

    kv_save.start()

    def mask(block, s):
        key = lax.broadcasted_iota(jnp.int32, s.shape, 0)
        if block < n:
            first = lax.rem(r - block + n, n) * rows
            which = order[0]
        else:
            first = (block - n) * rows
            which = order[1]
        shut = key == breaks[which, 0] - first
        for i in range(1, breaks.shape[1]):
            shut = shut | (key == breaks[which, i] - first)
        return jnp.where(shut, -FAR, s), 0.0

    attend(cq, kv, p, mixed, inverse, plan_of(n), mask, lambda pair: p_save(pair).start())
    crossed[...] = after[...] + nn(mixed[...], w_out[...])
    kv_save.wait()
    for pair in range(pairs):
        p_save(pair).wait()


def spread(sums, code, value, lane):
    tall = sums.shape[1]
    for k in range(sums.shape[0]):
        part = value[k * tall : (k + 1) * tall, :]
        sums[k ^ code, :, lane : lane + value.shape[1]] = part


def feed_kernel(
    order, codes, crossed, cot, w_up, b_up, w_down, b_down, gains, shifts,
    out, grad, near, far, g_bias, g_small, third, total, back, sums, sems,
):
    rows, width = cot.shape[1:]
    hidden = w_up.shape[1]
    half, tall = near.shape[:2]
    deep = hidden // (2 * half)
    third[...] = (standard(crossed[...])[0] * gains[2:3] + shifts[2:3]).astype(LOW)
    up_low = jnp.concatenate([cot[order[0]], cot[order[1]]], axis=0)
    total[...] = crossed[...] + b_down[...].astype(WIDE)
    back[...] = jnp.zeros_like(back)

    @pl.loop(0, hidden // width)
    def _(c):
        at = columns(c, width)
        rising = nn(third[...], w_up[:, at]) + b_up[:, at].astype(WIDE)
        active, slope = gelu_pair(rising)
        active = active.astype(LOW)
        total[...] += nn(active, w_down[at, :])
        rising_grad = nt(up_low, w_down[at, :]) * slope
        g_bias[:, at] = jnp.sum(rising_grad, axis=0, keepdims=True)
        rising_grad = rising_grad.astype(LOW)
        back[...] += nt(rising_grad, w_up[:, at])
        g_up = tn(third[...], rising_grad).astype(LOW)
        for k in range(2 * half):
            sums[k ^ codes[0], :, at] = g_up[k * tall : (k + 1) * tall]
        g_down = tn(active, up_low).astype(LOW)
        for k in range(width // deep):
            for i in range(deep // tall):
                first = k * deep + i * tall
                lanes = slice(hidden + i * width, hidden + (i + 1) * width)
                sums[(c * (width // deep) + k) ^ codes[1], :, lanes] = g_down[first : first + tall]

    saves = [
        pltpu.make_async_copy(sums.at[:half], near, sems.at[0]),
        pltpu.make_async_copy(sums.at[half:], far, sems.at[1]),
    ]
    for save in saves:
        save.start()
    low = total[...].astype(LOW)
    out[order[0]] = low[:rows]
    out[order[1]] = low[rows:]
    upward = up_low.astype(WIDE)
    inner, gain, shift = norm_back(crossed[...], gains[2:3], back[...])
    grad[...] = upward + inner
    g_small[0, :] = jnp.sum(upward, axis=0)
    g_small[1, :] = gain
    g_small[2, :] = shift
    for save in saves:
        save.wait()


def loads(kept, kv, p, sems):
    rows, width, wide = slice(0, kv.shape[0]), kv.shape[1], p.shape[2]
    pairs = width // (2 * PAIR)

    def p_copy(pair):
        at = pl.ds(pl.multiple_of(width + pair * wide, PAIR), wide)
        return pltpu.make_async_copy(kept.at[rows, at], p.at[lax.rem(pair, 2)], sems.at[pair])

    def kv_copies(pair):
        return [
            pltpu.make_async_copy(
                kept.at[rows, columns(i, PAIR)], kv.at[:, columns(i, PAIR)], sems.at[pairs + i]
            )
            for i in (pair, pairs + pair)
        ]

    for pair in range(pairs):
        if pair < 2:
            p_copy(pair).start()
        for copy in kv_copies(pair):
            copy.start()

    def ready(pair):
        for copy in (p_copy(pair), *kv_copies(pair)):
            copy.wait()

    def done(pair):
        @pl.when(pair + 2 < pairs)
        def _():
            p_copy(pair + 2).start()

    return ready, done


def put_part(parts, n, b, value):
    rows = value.shape[0]
    if b < len(parts):
        parts[b][:rows, :] = value
    else:
        parts[1][(b - n + 1) * rows : (b - n + 2) * rows, :] = value


def cross_back_kernel(n, order, enc, *refs):
    el, es, refs = refs[: n - 1], refs[n - 1], refs[n:]
    (grad, mixed, inverse, cq, kept, after, n1, w_cm, w_cout, w_cq, gains) = refs[:11]
    parts, (self_grad, g_cross, g_small, dq, up, dkv, kv, p, sems) = refs[11:-9], refs[-9:]
    ready, done = loads(kept, kv, p, sems)
    rows, width = enc.shape[1:]
    low = grad[...].astype(LOW)
    g_cross[:, 3 * width :] = tn(mixed[...], low).astype(LOW)
    up[...] = nt(low, w_cout[...]).astype(LOW)
    attend_back(up, mixed, inverse, cq, kv, p, dq, dkv, plan_of(n), ready, done)
    dq_low = dq[...]
    g_cross[:, 2 * width : 3 * width] = tn(n1[...], dq_low).astype(LOW)
    total = tn(enc[order[0]], dkv[0:rows, :])
    for d in range(1, n):
        total = total + tn(el[d - 1][...], dkv[d * rows : (d + 1) * rows, :])
    for j in range(n // 4):
        total = total + tn(es[j], dkv[(n + j) * rows : (n + j + 1) * rows, :])
    g_cross[:, : 2 * width] = total.astype(LOW)
    for b in range(n + n // 4):
        put_part(parts, n, b, nt(dkv[b * rows : (b + 1) * rows, :], w_cm[...]).astype(LOW))
    inner, gain, shift = norm_back(after[...], gains[1:2], nt(dq_low, w_cq[...]))
    self_grad[...] = grad[...] + inner
    g_small[0, :] = gain
    g_small[1, :] = shift


def self_back_kernel(n, order, codes, x, *refs):
    xl, refs = refs[: n - 1], refs[n - 1 :]
    (
        xs, self_grad, mixed, inverse, q, kept, w_in, w_out, gains, shifts, small_feed, g_bias,
        small_cross, g_cross, _,
    ) = refs[:15]
    parts, (own, near, far, sums, dq, up, dkv, kv, p, sems) = refs[15:-10], refs[-10:]
    ready, done = loads(kept, kv, p, sems)
    rows, width = x.shape[1:]
    low = self_grad[...].astype(LOW)
    up[...] = nt(low, w_out[...]).astype(LOW)
    attend_back(up, mixed, inverse, q, kv, p, dq, dkv, plan_of(n), ready, done)
    mine = jnp.concatenate([x[order[0]], x[order[1]]], axis=0).astype(WIDE)
    unit = standard(mine)[0]
    normed = (unit * gains[0:1] + shifts[0:1]).astype(LOW)
    g_out = tn(mixed[...], low).astype(LOW)
    g_query = tn(normed, dq[...]).astype(LOW)
    mine = nt(dq[...], w_in[:, :width])
    own[...] = mine
    gain = jnp.sum(mine * unit, axis=0)
    shift = jnp.sum(mine, axis=0)
    total = None
    for b in range(n + n // 4):
        if b == 0:
            key_unit, key_low = unit[:rows], normed[:rows]
        else:
            v = xl[b - 1][...] if b < n else xs[b - n]
            key_unit = standard(v.astype(WIDE))[0]
            key_low = (key_unit * gains[0:1] + shifts[0:1]).astype(LOW)
        pairs = dkv[b * rows : (b + 1) * rows, :]
        term = tn(key_low, pairs)
        total = term if total is None else total + term
        back = nt(pairs, w_in[:, width:])
        put_part(parts, n, b, back.astype(LOW))
        gain = gain + jnp.sum(back * key_unit, axis=0)
        shift = shift + jnp.sum(back, axis=0)
    small = [gain[None], small_cross[0:1], small_feed[1:2], shift[None], small_cross[1:2],
             small_feed[2:3], small_feed[0:1], g_bias[...]]
    small = [v[:, i : i + 128] for v in small for i in range(0, v.shape[1], 128)]
    small.append(jnp.zeros((width - len(small), 128), WIDE))
    small = jnp.concatenate(small, axis=0).astype(LOW)
    spread(sums, codes[0], g_cross, 0)
    spread(sums, codes[1], g_query, 4 * width)
    spread(sums, codes[1], total.astype(LOW), 5 * width)
    spread(sums, codes[1], g_out, 7 * width)
    spread(sums, codes[1], small, 8 * width)
    half = sums.shape[0] // 2
    saves = [
        pltpu.make_async_copy(sums.at[:half], near, sems.at[0]),
        pltpu.make_async_copy(sums.at[half:], far, sems.at[1]),
    ]
    for save in saves:
        save.start()
    for save in saves:
        save.wait()


def unpack(plan, codes, pieces, outs):
    for out, (at, count, which, lane, side) in zip(outs, plan):
        wide = out.shape[1]
        depth, tall = pieces[at].shape[:2]
        for k in range(count * depth):
            first = (codes[which] ^ k) * (tall * side)
            for i in range(side):
                start = pl.multiple_of(first + i * tall, tall)
                lanes = slice(lane + i * wide, lane + (i + 1) * wide)
                out[pl.ds(start, tall), :] = pieces[at + k // depth][k % depth, :, lanes].astype(WIDE)


def unpack_feed_kernel(plan, codes, *refs):
    unpack(plan, codes, refs[: -len(plan)], refs[-len(plan) :])


def unpack_rest_kernel(plan, codes, *refs):
    *refs, up_bias, down_bias, gains, shifts, small = refs
    count = len(plan) - 1
    unpack(plan, codes, refs[:-count], refs[-count:] + [small])
    at = 0
    for out, count in ((gains, 3), (shifts, 3), (down_bias, 1), (up_bias, 1)):
        for i in range(count):
            across = out.shape[1] // 128
            row = [small[at + j : at + j + 1, :] for j in range(across)]
            out[i : i + 1, :] = jnp.concatenate(row, axis=1)
            at += across


def last_kernel(n, order, rank, x, self_grad, own, gains, part, part_got, e_long, *refs):
    shorts, e_shorts, (grad, e_grad) = refs[: n // 4], refs[n // 4 : n // 2], refs[-2:]
    rows = x.shape[1]

    def mine(helds):
        total = jnp.zeros(part.shape, WIDE)
        for root, held in enumerate(helds):
            total = jnp.where(rank[0] == root, held[...].astype(WIDE), total)
        return total

    long_up = own[:rows] + part[...].astype(WIDE) + part_got[...].astype(WIDE)
    short_up = own[rows:] + mine(shorts)
    for which, up, at in ((order[0], long_up, 0), (order[1], short_up, rows)):
        inner, _, _ = norm_back(x[which].astype(WIDE), gains[0:1], up)
        grad[which] = self_grad[at : at + rows] + inner
    e_grad[order[0]] = e_long[...]
    e_grad[order[1]] = mine(e_shorts)


def add_core(near, got, *outs):
    at = 0
    half = near.shape[0] // 2
    for keep, send in zip(outs[::2], outs[1::2]):
        lanes = slice(at, at + keep.shape[2])
        keep[...] = near[:half, :, lanes] + got[:half, :, lanes]
        send[...] = near[half:, :, lanes] + got[half:, :, lanes]
        at = lanes.stop


def add_returns(own, near, near_got, *refs):
    rows = own.shape[0]
    count = near.shape[0] // rows
    total = own[...].astype(WIDE) + near_got[:rows, :].astype(WIDE)
    for ref in refs[:-count]:
        total = total + ref[...].astype(WIDE)
    refs[-count][...] = total
    for k in range(1, count):
        at = slice(k * rows, (k + 1) * rows)
        refs[k - count][...] = near[at, :] + near_got[at, :]


def add_halves(keep, got, *outs):
    half = keep.shape[0] // 2
    outs[-2][...] = keep[:half] + got[:half]
    outs[-1][...] = keep[half:] + got[half:]


def add_to_pieces(a, got_a, b, got_b, *outs):
    wide = a.shape[2]
    for k, out in enumerate(outs[-a.shape[0] :]):
        out[:, :, :wide] = a[k : k + 1] + got_a[k : k + 1]
        out[:, :, wide:] = b[k : k + 1] + got_b[k : k + 1]


def note(*refs):
    pass


def add_all(_, *refs):
    *parts, out = refs
    total = parts[0][...].astype(WIDE)
    for part in parts[1:]:
        total = total + part[...].astype(WIDE)
    out[...] = total.astype(out.dtype)


def lay_whole(_, *refs):
    for k, ref in enumerate(refs[:-1]):
        refs[-1][k : k + 1] = ref[...]


def lay(*refs):
    *parts, a, b = refs
    wide = a.shape[2]
    for k, part in enumerate(parts):
        a[k : k + 1] = part[:, :, :wide]
        b[k : k + 1] = part[:, :, wide:]


def join(a, b, out):
    out[: a.shape[0]] = a[...]
    out[a.shape[0] :] = b[...]


def beside(a, got_a, b, got_b, out):
    half, _, wide = a.shape
    out[:half, :, :wide] = a[...]
    out[half:, :, :wide] = got_a[...]
    out[:half, :, wide:] = b[...]
    out[half:, :, wide:] = got_b[...]


def steps_kernel(steps, *refs):
    refs = list(refs)
    at_in, at_out = 0, sum(count for _, count, _ in steps)
    for kernel, ins, outs in steps:
        kernel(*refs[at_in : at_in + ins], *refs[at_out : at_out + outs])
        at_in += ins
        at_out += outs


def call(kernel, ins, outs, us, scratch=(), smem=0, room=62, far_ins=(), far_outs=(), sems=0):
    vmem = pl.BlockSpec(memory_space=pltpu.VMEM)
    far = pl.BlockSpec(memory_space=pltpu.HBM)
    in_specs = [vmem] * len(ins)
    in_specs[:smem] = [pl.BlockSpec(memory_space=pltpu.SMEM)] * smem
    for i in far_ins:
        in_specs[i] = far
    scratch_shapes = [pltpu.VMEM(s, t) for s, t in scratch]
    if sems:
        scratch_shapes.append(pltpu.SemaphoreType.DMA((sems,)))
    return pl.pallas_call(
        kernel,
        out_shape=[jax.ShapeDtypeStruct(s, t) for s, t in outs],
        in_specs=in_specs,
        out_specs=[far if i in far_outs else vmem for i in range(len(outs))],
        scratch_shapes=scratch_shapes,
        compiler_params=pltpu.CompilerParams(vmem_limit_bytes=room << 20),
        cost_estimate=pl.CostEstimate(flops=us * 10**9, bytes_accessed=0, transcendentals=0),
    )(*ins)


def small_steps(steps):
    outs = call(
        functools.partial(steps_kernel, [(k, len(i), len(o)) for k, i, o in steps]),
        [v for _, ins, _ in steps for v in ins],
        [o if isinstance(o[0], tuple) else (o, LOW) for _, _, outs in steps for o in outs],
        2,
        room=20,
    )
    got = []
    for _, _, shapes in steps:
        got.append(outs[: len(shapes)])
        outs = outs[len(shapes) :]
    return got


def send_long(block, n, wrap):
    got = []
    for d in range(1, n):
        pairs = [(i, (i + d) % n) for i in range(n) if wrap or i + d < n]
        got.append(lax.ppermute(block, "blk", pairs))
    return got


def return_long(block, n, distance, wrap):
    pairs = [(i, (i - distance) % n) for i in range(n) if wrap or i >= distance]
    return lax.ppermute(block, "blk", pairs)


def return_short(held, n, root, distance):
    pairs = [((root + k + distance) % n, (root + k) % n) for k in range(0, n, 2 * distance)]
    return lax.ppermute(held, "blk", pairs)


def return_short_rest(helds, n):
    got = []
    for root, held in enumerate(helds):
        d = 4
        while d < n:
            held = held + return_short(held, n, root, d)
            d *= 2
        got.append(held)
    return got


def send_short_first(shorts, n):
    return [
        [held, lax.ppermute(held, "blk", [(root, (root + n // 2) % n)])]
        for root, held in enumerate(shorts)
    ]


def send_short_rest(terms, n):
    for root in range(n // 4):
        d = n // 4
        while d:
            pairs = [((root + k) % n, (root + k + d) % n) for k in range(0, n, 2 * d)]
            held = functools.reduce(jnp.add, terms[root])
            terms[root].append(lax.ppermute(held, "blk", pairs))
            d //= 2
    return [v for several in terms for v in several]


def tied(value, *others):
    return lax.optimization_barrier((value, others))[0]


def trade(v, axis, distance):
    return lax.ppermute(v, axis, [(i, i ^ distance) for i in range(lax.axis_size(axis))])


class Sharing:
    def __init__(self, batch, n):
        self.rest = [("batch", d) for d in (8, 16, 32) if d < batch]
        self.rest += [("blk", d) for d in (4, 8, 16, 32) if d < n]
        self.chunks = 32

    def codes(self):
        codes = []
        for first, second in ((2, 4), (4, 2)):
            code = jnp.int32(0)
            for axis, distance in (("batch", 1), ("batch", first), ("batch", second), ("blk", 2),
                                   ("blk", 1)):
                code = 2 * code + (lax.axis_index(axis) // distance) % 2
            codes.append(code.astype(jnp.int32))
        return jnp.stack(codes)

    def doubled(self, v):
        for axis, distance in self.rest:
            v = v + trade(v, axis, distance)
        return v


def to_tall(pieces):
    return [trade(v, "blk", j) for j, v in enumerate(pieces) if j]


def on_device(
    decoder_input, encoder_output, sequence_lengths, chain_breaks,
    self_inward, self_outward, cross_query, cross_memory, cross_outward,
    feed_up, feed_up_bias, feed_down, feed_down_bias, norm_gains, norm_shifts,
    output_cotangent,
):
    sequences, rows, width = decoder_input.shape
    hidden = feed_up.shape[1]
    n = lax.axis_size("blk")
    rank = lax.axis_index("blk")
    ranks = rank.astype(jnp.int32)[None]
    longest = (sequence_lengths[1] > sequence_lengths[0]).astype(jnp.int32)
    order = jnp.stack([longest, 1 - longest])
    both = 2 * rows
    nk = (n + n // 4) * rows
    pairs = width // PAIR

    sharing = Sharing(lax.axis_size("batch"), n)
    codes = sharing.codes()
    chunks = sharing.chunks
    tall = width // chunks
    blocks = nk // rows

    room = 62 if n > 4 else 22
    block = ((rows, width), LOW)
    x_long, e_long, *shorts = call(
        pick_kernel,
        (sequence_lengths, decoder_input, encoder_output),
        [block, block] + [((both, width), LOW)] * (n // 4),
        1,
        smem=1,
        room=60,
    )
    firsts = send_short_first(shorts, n)
    xl = send_long(x_long, n, False)
    xs = send_short_rest([[v[:rows] for v in terms] for terms in firsts], n)
    shorts = len(xs) // (n // 4)
    e_long = tied(e_long, *[terms[1] for terms in firsts])
    es = send_short_rest([[tied(v[rows:], *xl) for v in terms] for terms in firsts], n)
    el = send_long(e_long, n, True)

    pair_rows = ((nk, 2 * width), LOW)
    saved = [pair_rows, ((nk, pairs * both), LOW)]
    loaded = [pair_rows, ((2, nk, both), LOW)]
    kept_shape = ((nk * (9 if n == 4 else 1), 2 * width + pairs * both), LOW)
    inverses = ((2 * pairs, both), WIDE)
    low_rows, wide_rows = ((both, width), LOW), ((both, width), WIDE)
    q, kept, mixed, inverse, after, cq, n1, xs = call(
        functools.partial(self_kernel, n, shorts),
        (order, ranks, decoder_input, *xl, *xs, self_inward, self_outward, cross_query,
         norm_gains, norm_shifts),
        [low_rows, kept_shape, low_rows, inverses, wide_rows, low_rows, low_rows,
         ((n // 4, rows, width), LOW)],
        12,
        scratch=saved,
        smem=2,
        room=room,
        far_outs=(1,),
        sems=pairs + 1,
    )
    cross_kept, cmixed, cinverse, crossed, es = call(
        functools.partial(cross_kernel, n, shorts),
        (order, ranks, chain_breaks, encoder_output, *el, *es, cq, after, cross_memory,
         cross_outward),
        [kept_shape, low_rows, inverses, wide_rows, ((n // 4, rows, width), LOW)],
        11,
        scratch=saved,
        smem=3,
        room=room,
        far_outs=(0,),
        sems=pairs + 1,
    )
    half = chunks // 2
    layer_output, cross_grad, near, far, g_bias, small_feed = call(
        feed_kernel,
        (order, codes, crossed, output_cotangent, feed_up, feed_up_bias[None], feed_down,
         feed_down_bias[None], norm_gains, norm_shifts),
        [(decoder_input.shape, LOW), ((both, width), WIDE), ((half, tall, 2 * hidden), LOW),
         ((half, tall, 2 * hidden), LOW), ((1, hidden), WIDE), ((3, width), WIDE)],
        14,
        scratch=[low_rows, wide_rows, wide_rows, ((chunks, tall, 2 * hidden), LOW)],
        smem=2,
        room=room,
        far_outs=(2, 3),
        sems=2,
    )
    wide = [hidden, hidden]
    wide_rest = [hidden, hidden + 128]

    def shape(count, lanes):
        return (count, tall, lanes)

    roots = range(n // 4)
    part_shapes = [((rows, width), LOW)] * n
    part_shapes[1] = (((n // 4 + 1) * rows, width), LOW)
    feed_core = trade(far, "batch", 1)
    feed_near = near
    *e_parts, self_grad, g_cross, small_cross = call(
        functools.partial(cross_back_kernel, n),
        (order, encoder_output, *el, es, cross_grad, cmixed, cinverse,
         cq, cross_kept, after, n1, cross_memory, cross_outward, cross_query, norm_gains),
        part_shapes + [((both, width), WIDE), ((width, 4 * width), LOW), ((2, width), WIDE)],
        14,
        scratch=[low_rows, low_rows, pair_rows, *loaded],
        smem=1,
        room=room,
        far_ins=(n + 6,),
        sems=3 * pairs,
    )
    (a, a_send, b, b_send), _ = small_steps(
        [(add_core, (feed_near, feed_core), [shape(8, w) for w in wide for _ in "ks"]),
         (note, (small_cross,), [])]
    )
    a_got, b_got = trade(a_send, "batch", 2), trade(b_send, "batch", 4)
    e_got = [return_long(e_parts[d], n, d, True) for d in range(1, n)]
    *parts, own, near, far = call(
        functools.partial(self_back_kernel, n),
        (order, codes, decoder_input, *xl, xs, self_grad, mixed, inverse, q, kept, self_inward,
         self_outward, norm_gains, norm_shifts, small_feed, g_bias, small_cross, g_cross, a),
        [((rows, width), LOW)] * blocks
        + [((both, width), WIDE), (shape(half, sum(wide_rest)), LOW),
           (shape(half, sum(wide_rest)), LOW)],
        16,
        scratch=[(shape(chunks, sum(wide_rest)), LOW), low_rows, low_rows, pair_rows, *loaded],
        smem=2,
        room=room,
        far_ins=(n + 7,),
        far_outs=(blocks + 1, blocks + 2),
        sems=3 * pairs,
    )
    (a, a_send), (b, b_send), (e_long, *e_short) = small_steps(
        [(add_halves, (a, a_got, own), [shape(4, wide[0])] * 2),
         (add_halves, (b, b_got), [shape(4, wide[1])] * 2),
         (add_returns, (e_parts[0], e_parts[1], *e_got),
          [((rows, width), WIDE)] + [(rows, width)] * (n // 4))]
    )
    a_got, b_got = trade(a_send, "batch", 4), trade(b_send, "batch", 2)
    e_got = [return_short(e_short[k], n, k, 2) for k in roots]
    held = tied(parts[n - 1], a_send)
    for d in range(n - 2, 2, -1):
        held = parts[d] + return_long(held, n, 1, False)
    long_got = return_long(held, n, 1, False)
    feed, (a, a_send, b, b_send), (held,), *e_short = small_steps(
        [(add_to_pieces, (a, a_got, b, b_got), [shape(1, sum(wide))] * 4),
         (add_core, (near, trade(tied(far, a_send), "batch", 1)),
          [shape(8, w) for w in wide_rest for _ in "ks"]),
         (add_all, (own, parts[2], long_got), [(rows, width)])]
        + [(add_all, (own, e_short[k], e_got[k]), [(rows, width)]) for k in roots]
    )
    e_short = return_short_rest([v for v, in e_short], n)
    a_got, b_got = trade(a_send, "batch", 2), trade(b_send, "batch", 4)
    (a, a_send), (b, b_send), (feed,) = small_steps(
        [(add_halves, (a, a_got), [shape(4, wide_rest[0])] * 2),
         (add_halves, (b, b_got), [shape(4, wide_rest[1])] * 2),
         (add_all, (own, feed[0], *to_tall(feed)), [shape(1, sum(wide))])]
    )
    feed = sharing.doubled(feed)
    a_got, b_got = trade(a_send, "batch", 4), trade(b_send, "batch", 2)
    rest, (fa, fb) = small_steps(
        [(add_to_pieces, (a, a_got, b, b_got), [shape(1, sum(wide_rest))] * 4),
         (lay, (feed, *to_tall([feed] * 4)), [shape(4, w) for w in wide])]
    )
    (rest,), (fa,), (fb,) = small_steps(
        [(add_all, (own, rest[0], *to_tall(rest)), [shape(1, sum(wide_rest))]),
         (join, (fa, trade(fa, "batch", 4)), [shape(8, wide[0])]),
         (join, (fb, trade(fb, "batch", 2)), [shape(8, wide[1])])]
    )
    rest = sharing.doubled(rest)
    (ra, rb), (feed,) = small_steps(
        [(lay, (rest, *to_tall([rest] * 4)), [shape(4, w) for w in wide_rest]),
         (beside, (fa, trade(fa, "batch", 2), fb, trade(fb, "batch", 4)),
          [shape(16, sum(wide))])]
    )
    ra_got, rb_got = trade(ra, "batch", 4), trade(rb, "batch", 2)
    feed_got = trade(feed, "batch", 1)
    held, *shorts = tied((held, *parts[n:]), ra)
    long_got = return_long(held, n, 1, False)
    got = [return_short(shorts[k], n, k, 1) for k in roots]
    (ra,), (rb,), _, (held,), *shorts = small_steps(
        [(join, (ra, ra_got), [shape(8, wide_rest[0])]),
         (join, (rb, rb_got), [shape(8, wide_rest[1])]),
         (note, (feed_got,), []),
         (add_all, (own, parts[1], long_got), [(rows, width)])]
        + [(add_all, (own, parts[n + k], got[k]), [(rows, width)]) for k in roots]
    )
    ra_got, rb_got = trade(ra, "batch", 2), trade(rb, "batch", 4)
    long_got = return_long(held, n, 1, False)
    got = [return_short(shorts[k][0], n, k, 2) for k in roots]
    s_up, s_down = call(
        functools.partial(unpack_feed_kernel, [(0, 2, 0, 0, 1), (0, 2, 1, hidden, hidden // width)]),
        (codes, feed, feed_got),
        [(feed_up.shape, WIDE), (feed_down.shape, WIDE)],
        6,
        smem=1,
        room=room,
    )
    (rest,), _, *shorts = small_steps(
        [(beside, (ra, ra_got, rb, rb_got), [shape(16, sum(wide_rest))]),
         (note, (s_down[:8, :128], long_got), [])]
        + [(add_all, (own, shorts[k][0], got[k]), [(rows, width)]) for k in roots]
    )
    shorts = return_short_rest([v for v, in shorts], n)
    rest_got = trade(rest, "batch", 1)
    input_gradient, encoder_gradient = call(
        functools.partial(last_kernel, n),
        (order, ranks, decoder_input, self_grad, own, norm_gains, parts[0], long_got, e_long,
         *shorts, *e_short),
        [(decoder_input.shape, WIDE), (decoder_input.shape, WIDE)],
        3,
        smem=2,
        room=room,
    )
    at = hidden
    places = [(0, 2, 0, 0, 1), (0, 2, 0, 2 * width, 1), (0, 2, 0, 3 * width, 1),
              (0, 2, 1, at, 1), (0, 2, 1, at + 3 * width, 1), (0, 2, 1, at + 4 * width, 1)]
    s_cm, s_cq, s_cout, s_in, s_out, up_bias, down_bias, gains, shifts = call(
        functools.partial(unpack_rest_kernel, places),
        (codes, rest, rest_got),
        [(s, WIDE) for s in (cross_memory.shape, cross_query.shape, cross_outward.shape,
                             self_inward.shape, self_outward.shape, (1, hidden), (1, width),
                             norm_gains.shape, norm_shifts.shape)],
        5,
        scratch=[((width, 128), WIDE)],
        smem=1,
        room=room,
    )
    return (
        layer_output, input_gradient, encoder_gradient, s_in, s_out, s_cq, s_cm, s_cout,
        s_up, up_bias[0], s_down, down_bias[0], gains, shifts,
    )


def solution(mesh):
    blocked = P("batch", "blk", None)
    placed = (blocked, blocked, P("batch"), P("batch", None)) + (P(),) * 11 + (blocked,)
    return jax.shard_map(
        on_device,
        mesh=mesh,
        in_specs=placed,
        out_specs=(blocked,) * 3 + (P(),) * 11,
        check_vma=False,
    )
```

```python
import functools

import jax
import jax.numpy as jnp
from jax import lax
from jax.experimental import pallas as pl
from jax.experimental.pallas import tpu as pltpu
from jax.sharding import PartitionSpec as P

HEAD = 64
PAIR = 2 * HEAD
EPSILON = 1e-05
FAR = 1e30
LOW = jnp.bfloat16
WIDE = jnp.float32


def contract(left, right, a, b):
    return lax.dot_general(left, right, (((a,), (b,)), ((), ())), preferred_element_type=WIDE)


def nn(left, right):
    return contract(left, right, 1, 0)


def nt(left, right):
    return contract(left, right, 1, 1)


def tn(left, right):
    return contract(left, right, 0, 0)


def standard(values):
    center = values - jnp.mean(values, axis=-1, keepdims=True)
    spread = jnp.mean(center * center, axis=-1, keepdims=True)
    inverse = lax.rsqrt(spread + EPSILON)
    return center * inverse, inverse


def norm_back(values, gain, upstream):
    unit, inverse = standard(values)
    m = upstream * gain
    grad = inverse * (
        m
        - jnp.mean(m, axis=-1, keepdims=True)
        - unit * jnp.mean(m * unit, axis=-1, keepdims=True)
    )
    return grad, jnp.sum(upstream * unit, axis=0), jnp.sum(upstream, axis=0)


def gelu_pair(x):
    z = jnp.abs(x) * 0.7071067811865476
    t = 1.0 / (1.0 + 0.5 * z)
    poly = 0.17087277
    for c in (
        -0.82215223,
        1.48851587,
        -1.13520398,
        0.27886807,
        -0.18628806,
        0.09678418,
        0.37409196,
        1.00002368,
        -1.26551223,
    ):
        poly = poly * t + c
    bell = jnp.exp(-z * z)
    tail = 0.5 * t * jnp.exp(poly) * bell
    share = jnp.where(x >= 0, 1.0 - tail, tail)
    return x * share, share + x * bell * 0.3989422804014327


def by_head(pair_rows):
    lane = lax.broadcasted_iota(jnp.int32, pair_rows.shape, 1)
    zero = jnp.zeros_like(pair_rows)
    return jnp.concatenate(
        [jnp.where(lane < HEAD, pair_rows, zero), jnp.where(lane >= HEAD, pair_rows, zero)], axis=0
    )


def own_parts(both):
    rows = both.shape[1] // 2
    return jnp.concatenate([both[:HEAD, :rows], both[HEAD:, rows:]], axis=0)


def columns(place, wide):
    return pl.ds(pl.multiple_of(place * wide, wide), wide)


def attend(q_ref, kv_ref, p_ref, low_ref, inverse_ref, plan, mask, done):
    rows = q_ref.shape[0] // 2
    width = q_ref.shape[1]

    @pl.loop(0, width // PAIR)
    def _(pair):
        lanes = columns(pair, PAIR)
        values = columns(width // PAIR + pair, PAIR)
        spot = columns(pair, 2 * rows)
        for seq, blocks in enumerate(plan):
            mine = slice(seq * rows, (seq + 1) * rows)
            queries = by_head(q_ref[mine, lanes])
            scores, tops = [], []
            for block in blocks:
                s = nt(kv_ref[block * rows : (block + 1) * rows, lanes], queries)
                s, far = mask(block, s)
                scores.append((s, far))
                tops.append(jnp.max(s, axis=0, keepdims=True) - far)
            top = functools.reduce(jnp.maximum, tops)
            total = jnp.zeros_like(top)
            mixed = jnp.zeros((PAIR, 2 * rows), WIDE)
            for block, (s, far) in zip(blocks, scores):
                at = slice(block * rows, (block + 1) * rows)
                p = jnp.exp(s - (top + far))
                total = total + jnp.sum(p, axis=0, keepdims=True)
                p = p.astype(LOW)
                p_ref[at, spot] = p
                mixed = mixed + tn(kv_ref[at, values], p)
            inverse = 1.0 / total
            low_ref[mine, lanes] = own_parts(mixed * inverse).T.astype(LOW)
            inverse_ref[pl.ds(2 * pair + seq, 1), :] = inverse
        done(pair)


def attend_back(up, low_ref, inverse_ref, q_ref, kv_ref, p_ref, dq_ref, dkv_ref, plan, ready, done):
    rows = q_ref.shape[0] // 2
    width = q_ref.shape[1]
    scale = HEAD ** (-0.5)

    @pl.loop(0, width // PAIR)
    def _(pair):
        lanes = columns(pair, PAIR)
        values = columns(width // PAIR + pair, PAIR)
        slot = lax.rem(pair, 2)
        ready(pair)
        for seq, blocks in enumerate(plan):
            mine = slice(seq * rows, (seq + 1) * rows)
            queries = by_head(q_ref[mine, lanes])
            inverse = inverse_ref[pl.ds(2 * pair + seq, 1), :]
            scaled = up[mine, lanes].astype(WIDE) * own_parts(jnp.broadcast_to(inverse, (PAIR, 2 * rows))).T
            inner = (scaled * low_ref[mine, lanes].astype(WIDE)).T
            offset = jnp.concatenate(
                [
                    jnp.sum(inner[:HEAD], axis=0, keepdims=True),
                    jnp.sum(inner[HEAD:], axis=0, keepdims=True),
                ],
                axis=1,
            )
            upper = by_head(scaled.astype(LOW))
            dq = jnp.zeros((PAIR, 2 * rows), WIDE)
            for block in blocks:
                at = slice(block * rows, (block + 1) * rows)
                p = p_ref[slot, at, :]
                dp = nt(kv_ref[at, values], upper)
                ds = (p.astype(WIDE) * (dp - offset)).astype(LOW)
                dkv_ref[at, values] = nn(p, upper).astype(LOW)
                dkv_ref[at, lanes] = nn(ds, queries).astype(LOW)
                dq = dq + tn(kv_ref[at, lanes], ds)
            dq_ref[mine, lanes] = (own_parts(dq).T * scale).astype(LOW)
        done(pair)


def saves(kv, p, kept, sems):
    rows, width = slice(0, kv.shape[0]), kv.shape[1]
    wide = 2 * PAIR * p.shape[1] // width

    def p_save(pair):
        at = pl.ds(pl.multiple_of(width + pair * wide, PAIR), wide)
        return pltpu.make_async_copy(p.at[:, columns(pair, wide)], kept.at[rows, at], sems.at[pair])

    pairs = width // (2 * PAIR)
    return pltpu.make_async_copy(kv, kept.at[rows, :width], sems.at[pairs]), p_save


def plan_of(n):
    return (tuple(range(n)), tuple(range(n, n + n // 4)))


def add_terms(out, refs, terms):
    for j in range(out.shape[0]):
        total = refs[j * terms][...]
        for ref in refs[j * terms + 1 : (j + 1) * terms]:
            total = total + ref[...]
        out[j] = total


def pick_kernel(lengths, x, enc, x_long, e_long, *shorts):
    rows = x_long.shape[0]
    long = jnp.where(lengths[1] > lengths[0], 1, 0)
    x_long[...] = x[long]
    e_long[...] = enc[long]
    for root, ref in enumerate(shorts):
        share = (lax.axis_index("blk") == root).astype(jnp.int32).astype(WIDE)
        ref[:rows] = (x[1 - long].astype(WIDE) * share).astype(LOW)
        ref[rows:] = (enc[1 - long].astype(WIDE) * share).astype(LOW)


def self_kernel(n, terms, order, rank, x, *refs):
    xl, refs = refs[: n - 1], refs[n - 1 :]
    shorts, refs = refs[: terms * (n // 4)], refs[terms * (n // 4) :]
    (
        w_in, w_out, w_cq, gains, shifts,
        q, kept, mixed, inverse, after, cq, n1, xs, kv, p, sems,
    ) = refs
    pairs = q.shape[1] // PAIR
    kv_save, p_save = saves(kv, p, kept, sems)
    add_terms(xs, shorts, terms)
    rows, width = x.shape[1:]
    r = rank[0]

    def first_norm(v):
        return (standard(v.astype(WIDE))[0] * gains[0:1] + shifts[0:1]).astype(LOW)

    def keys(v, block):
        kv[block * rows : (block + 1) * rows, :] = nn(first_norm(v), w_in[:, width:]).astype(LOW)

    mine = jnp.concatenate([x[order[0]], x[order[1]]], axis=0)
    normed = first_norm(mine)
    kv[0:rows, :] = nn(normed[:rows], w_in[:, width:]).astype(LOW)
    for d in range(1, n):
        keys(xl[d - 1][...], d)
    for j in range(n // 4):
        keys(xs[j], n + j)
    kv_save.start()
    q[...] = nn(normed, w_in[:, :width]).astype(LOW) * HEAD ** (-0.5)

    def mask(block, s):
        if 0 < block < n:
            return s, jnp.where(r >= block, 0.0, FAR)
        key = lax.broadcasted_iota(jnp.int32, s.shape, 0)
        query = lax.broadcasted_iota(jnp.int32, s.shape, 1)
        query = jnp.where(query >= rows, query - rows, query)
        if block >= n:
            query = query + (r - (block - n)) * rows
        return jnp.where(key <= query, s, -FAR), 0.0

    attend(q, kv, p, mixed, inverse, plan_of(n), mask, lambda pair: p_save(pair).start())
    total = mine.astype(WIDE) + nn(mixed[...], w_out[...])
    after[...] = total
    second = (standard(total)[0] * gains[1:2] + shifts[1:2]).astype(LOW)
    n1[...] = second
    cq[...] = nn(second, w_cq[...]).astype(LOW) * HEAD ** (-0.5)
    kv_save.wait()
    for pair in range(pairs):
        p_save(pair).wait()


def cross_kernel(n, terms, order, rank, breaks, enc, *refs):
    el, refs = refs[: n - 1], refs[n - 1 :]
    shorts, refs = refs[: terms * (n // 4)], refs[terms * (n // 4) :]
    cq, after, w_cm, w_out, kept, mixed, inverse, crossed, es, kv, p, sems = refs
    pairs = cq.shape[1] // PAIR
    kv_save, p_save = saves(kv, p, kept, sems)
    add_terms(es, shorts, terms)
    rows, width = enc.shape[1:]
    r = rank[0]
    kv[0:rows, :] = nn(enc[order[0]], w_cm[...]).astype(LOW)
    for d in range(1, n):
        kv[d * rows : (d + 1) * rows, :] = nn(el[d - 1][...], w_cm[...]).astype(LOW)
    for j in range(n // 4):
        kv[(n + j) * rows : (n + j + 1) * rows, :] = nn(es[j], w_cm[...]).astype(LOW)

    kv_save.start()

    def mask(block, s):
        key = lax.broadcasted_iota(jnp.int32, s.shape, 0)
        if block < n:
            first = lax.rem(r - block + n, n) * rows
            which = order[0]
        else:
            first = (block - n) * rows
            which = order[1]
        shut = key == breaks[which, 0] - first
        for i in range(1, breaks.shape[1]):
            shut = shut | (key == breaks[which, i] - first)
        return jnp.where(shut, -FAR, s), 0.0

    attend(cq, kv, p, mixed, inverse, plan_of(n), mask, lambda pair: p_save(pair).start())
    crossed[...] = after[...] + nn(mixed[...], w_out[...])
    kv_save.wait()
    for pair in range(pairs):
        p_save(pair).wait()


def spread(sums, code, value, lane):
    tall = sums.shape[1]
    for k in range(sums.shape[0]):
        part = value[k * tall : (k + 1) * tall, :]
        sums[k ^ code, :, lane : lane + value.shape[1]] = part


def feed_kernel(
    order, codes, crossed, cot, w_up, b_up, w_down, b_down, gains, shifts,
    out, grad, near, far, g_bias, g_small, third, total, back, sums, sems,
):
    rows, width = cot.shape[1:]
    hidden = w_up.shape[1]
    half, tall = near.shape[:2]
    deep = hidden // (2 * half)
    third[...] = (standard(crossed[...])[0] * gains[2:3] + shifts[2:3]).astype(LOW)
    up_low = jnp.concatenate([cot[order[0]], cot[order[1]]], axis=0)
    total[...] = crossed[...] + b_down[...].astype(WIDE)
    back[...] = jnp.zeros_like(back)

    @pl.loop(0, hidden // width)
    def _(c):
        at = columns(c, width)
        rising = nn(third[...], w_up[:, at]) + b_up[:, at].astype(WIDE)
        active, slope = gelu_pair(rising)
        active = active.astype(LOW)
        total[...] += nn(active, w_down[at, :])
        rising_grad = nt(up_low, w_down[at, :]) * slope
        g_bias[:, at] = jnp.sum(rising_grad, axis=0, keepdims=True)
        rising_grad = rising_grad.astype(LOW)
        back[...] += nt(rising_grad, w_up[:, at])
        g_up = tn(third[...], rising_grad).astype(LOW)
        for k in range(2 * half):
            sums[k ^ codes[0], :, at] = g_up[k * tall : (k + 1) * tall]
        g_down = tn(active, up_low).astype(LOW)
        for k in range(width // deep):
            for i in range(deep // tall):
                first = k * deep + i * tall
                lanes = slice(hidden + i * width, hidden + (i + 1) * width)
                sums[(c * (width // deep) + k) ^ codes[1], :, lanes] = g_down[first : first + tall]

    saves = [
        pltpu.make_async_copy(sums.at[:half], near, sems.at[0]),
        pltpu.make_async_copy(sums.at[half:], far, sems.at[1]),
    ]
    for save in saves:
        save.start()
    low = total[...].astype(LOW)
    out[order[0]] = low[:rows]
    out[order[1]] = low[rows:]
    upward = up_low.astype(WIDE)
    inner, gain, shift = norm_back(crossed[...], gains[2:3], back[...])
    grad[...] = upward + inner
    g_small[0, :] = jnp.sum(upward, axis=0)
    g_small[1, :] = gain
    g_small[2, :] = shift
    for save in saves:
        save.wait()


def loads(kept, kv, p, sems):
    rows, width, wide = slice(0, kv.shape[0]), kv.shape[1], p.shape[2]
    pairs = width // (2 * PAIR)

    def p_copy(pair):
        at = pl.ds(pl.multiple_of(width + pair * wide, PAIR), wide)
        return pltpu.make_async_copy(kept.at[rows, at], p.at[lax.rem(pair, 2)], sems.at[pair])

    def kv_copies(pair):
        return [
            pltpu.make_async_copy(
                kept.at[rows, columns(i, PAIR)], kv.at[:, columns(i, PAIR)], sems.at[pairs + i]
            )
            for i in (pair, pairs + pair)
        ]

    for pair in range(pairs):
        if pair < 2:
            p_copy(pair).start()
        for copy in kv_copies(pair):
            copy.start()

    def ready(pair):
        for copy in (p_copy(pair), *kv_copies(pair)):
            copy.wait()

    def done(pair):
        @pl.when(pair + 2 < pairs)
        def _():
            p_copy(pair + 2).start()

    return ready, done


def put_part(parts, n, b, value):
    rows = value.shape[0]
    if b < len(parts):
        parts[b][:rows, :] = value
    else:
        parts[1][(b - n + 1) * rows : (b - n + 2) * rows, :] = value


def cross_back_kernel(n, grad, mixed, inverse, cq, kept, w_cm, w_cout, *refs):
    parts, (dq, dkv, low, up, kv, p, sems) = refs[:-7], refs[-7:]
    ready, done = loads(kept, kv, p, sems)
    rows = parts[0].shape[0]
    low[...] = grad[...].astype(LOW)
    up[...] = nt(low[...], w_cout[...]).astype(LOW)
    attend_back(up, mixed, inverse, cq, kv, p, dq, dkv, plan_of(n), ready, done)
    for b in range(n + n // 4):
        put_part(parts, n, b, nt(dkv[b * rows : (b + 1) * rows, :], w_cm[...]).astype(LOW))


def cross_sums_kernel(n, order, enc, *refs):
    el, es, refs = refs[: n - 1], refs[n - 1], refs[n:]
    grad, low, mixed, dq, dkv, after, n1, w_cq, gains, self_grad, g_cross, g_small = refs
    rows, width = enc.shape[1:]
    g_cross[:, 3 * width :] = tn(mixed[...], low[...]).astype(LOW)
    g_cross[:, 2 * width : 3 * width] = tn(n1[...], dq[...]).astype(LOW)
    total = tn(enc[order[0]], dkv[0:rows, :])
    for d in range(1, n):
        total = total + tn(el[d - 1][...], dkv[d * rows : (d + 1) * rows, :])
    for j in range(n // 4):
        total = total + tn(es[j], dkv[(n + j) * rows : (n + j + 1) * rows, :])
    g_cross[:, : 2 * width] = total.astype(LOW)
    inner, gain, shift = norm_back(after[...], gains[1:2], nt(dq[...], w_cq[...]))
    self_grad[...] = grad[...] + inner
    g_small[0, :] = gain
    g_small[1, :] = shift


def self_back_kernel(n, order, codes, x, *refs):
    xl, refs = refs[: n - 1], refs[n - 1 :]
    (
        xs, self_grad, mixed, inverse, q, kept, w_in, w_out, gains, shifts, small_feed, g_bias,
        small_cross, g_cross, _,
    ) = refs[:15]
    parts, (own, near, far, sums, dq, up, dkv, kv, p, sems) = refs[15:-10], refs[-10:]
    ready, done = loads(kept, kv, p, sems)
    rows, width = x.shape[1:]
    low = self_grad[...].astype(LOW)
    up[...] = nt(low, w_out[...]).astype(LOW)
    attend_back(up, mixed, inverse, q, kv, p, dq, dkv, plan_of(n), ready, done)
    mine = jnp.concatenate([x[order[0]], x[order[1]]], axis=0).astype(WIDE)
    unit = standard(mine)[0]
    normed = (unit * gains[0:1] + shifts[0:1]).astype(LOW)
    g_out = tn(mixed[...], low).astype(LOW)
    g_query = tn(normed, dq[...]).astype(LOW)
    mine = nt(dq[...], w_in[:, :width])
    own[...] = mine
    gain = jnp.sum(mine * unit, axis=0)
    shift = jnp.sum(mine, axis=0)
    total = None
    for b in range(n + n // 4):
        if b == 0:
            key_unit, key_low = unit[:rows], normed[:rows]
        else:
            v = xl[b - 1][...] if b < n else xs[b - n]
            key_unit = standard(v.astype(WIDE))[0]
            key_low = (key_unit * gains[0:1] + shifts[0:1]).astype(LOW)
        pairs = dkv[b * rows : (b + 1) * rows, :]
        term = tn(key_low, pairs)
        total = term if total is None else total + term
        back = nt(pairs, w_in[:, width:])
        put_part(parts, n, b, back.astype(LOW))
        gain = gain + jnp.sum(back * key_unit, axis=0)
        shift = shift + jnp.sum(back, axis=0)
    small = [gain[None], small_cross[0:1], small_feed[1:2], shift[None], small_cross[1:2],
             small_feed[2:3], small_feed[0:1], g_bias[...]]
    small = [v[:, i : i + 128] for v in small for i in range(0, v.shape[1], 128)]
    small.append(jnp.zeros((width - len(small), 128), WIDE))
    small = jnp.concatenate(small, axis=0).astype(LOW)
    spread(sums, codes[0], g_cross, 0)
    spread(sums, codes[1], g_query, 4 * width)
    spread(sums, codes[1], total.astype(LOW), 5 * width)
    spread(sums, codes[1], g_out, 7 * width)
    spread(sums, codes[1], small, 8 * width)
    half = sums.shape[0] // 2
    saves = [
        pltpu.make_async_copy(sums.at[:half], near, sems.at[0]),
        pltpu.make_async_copy(sums.at[half:], far, sems.at[1]),
    ]
    for save in saves:
        save.start()
    for save in saves:
        save.wait()


def unpack(plan, codes, pieces, outs):
    for out, (at, count, which, lane, side) in zip(outs, plan):
        wide = out.shape[1]
        depth, tall = pieces[at].shape[:2]
        for k in range(count * depth):
            first = (codes[which] ^ k) * (tall * side)
            for i in range(side):
                start = pl.multiple_of(first + i * tall, tall)
                lanes = slice(lane + i * wide, lane + (i + 1) * wide)
                out[pl.ds(start, tall), :] = pieces[at + k // depth][k % depth, :, lanes].astype(WIDE)


def unpack_feed_kernel(plan, codes, *refs):
    unpack(plan, codes, refs[: -len(plan)], refs[-len(plan) :])


def unpack_rest_kernel(plan, codes, *refs):
    *refs, up_bias, down_bias, gains, shifts, small = refs
    count = len(plan) - 1
    unpack(plan, codes, refs[:-count], refs[-count:] + [small])
    at = 0
    for out, count in ((gains, 3), (shifts, 3), (down_bias, 1), (up_bias, 1)):
        for i in range(count):
            across = out.shape[1] // 128
            row = [small[at + j : at + j + 1, :] for j in range(across)]
            out[i : i + 1, :] = jnp.concatenate(row, axis=1)
            at += across


def last_kernel(n, order, rank, x, self_grad, own, gains, part, part_got, e_long, *refs):
    shorts, e_shorts, (grad, e_grad) = refs[: n // 4], refs[n // 4 : n // 2], refs[-2:]
    rows = x.shape[1]

    def mine(helds):
        total = jnp.zeros(part.shape, WIDE)
        for root, held in enumerate(helds):
            total = jnp.where(rank[0] == root, held[...].astype(WIDE), total)
        return total

    long_up = own[:rows] + part[...].astype(WIDE) + part_got[...].astype(WIDE)
    short_up = own[rows:] + mine(shorts)
    for which, up, at in ((order[0], long_up, 0), (order[1], short_up, rows)):
        inner, _, _ = norm_back(x[which].astype(WIDE), gains[0:1], up)
        grad[which] = self_grad[at : at + rows] + inner
    e_grad[order[0]] = e_long[...]
    e_grad[order[1]] = mine(e_shorts)


def add_core(near, got, *outs):
    at = 0
    half = near.shape[0] // 2
    for keep, send in zip(outs[::2], outs[1::2]):
        lanes = slice(at, at + keep.shape[2])
        keep[...] = near[:half, :, lanes] + got[:half, :, lanes]
        send[...] = near[half:, :, lanes] + got[half:, :, lanes]
        at = lanes.stop


def add_returns(own, near, near_got, *refs):
    rows = own.shape[0]
    count = near.shape[0] // rows
    total = own[...].astype(WIDE) + near_got[:rows, :].astype(WIDE)
    for ref in refs[:-count]:
        total = total + ref[...].astype(WIDE)
    refs[-count][...] = total
    for k in range(1, count):
        at = slice(k * rows, (k + 1) * rows)
        refs[k - count][...] = near[at, :] + near_got[at, :]


def add_halves(keep, got, *outs):
    half = keep.shape[0] // 2
    outs[-2][...] = keep[:half] + got[:half]
    outs[-1][...] = keep[half:] + got[half:]


def add_to_pieces(a, got_a, b, got_b, *outs):
    wide = a.shape[2]
    for k, out in enumerate(outs[-a.shape[0] :]):
        out[:, :, :wide] = a[k : k + 1] + got_a[k : k + 1]
        out[:, :, wide:] = b[k : k + 1] + got_b[k : k + 1]


def note(*refs):
    pass


def add_all(_, *refs):
    *parts, out = refs
    total = parts[0][...].astype(WIDE)
    for part in parts[1:]:
        total = total + part[...].astype(WIDE)
    out[...] = total.astype(out.dtype)


def lay_whole(_, *refs):
    for k, ref in enumerate(refs[:-1]):
        refs[-1][k : k + 1] = ref[...]


def lay(*refs):
    *parts, a, b = refs
    wide = a.shape[2]
    for k, part in enumerate(parts):
        a[k : k + 1] = part[:, :, :wide]
        b[k : k + 1] = part[:, :, wide:]


def join(a, b, out):
    out[: a.shape[0]] = a[...]
    out[a.shape[0] :] = b[...]


def beside(a, got_a, b, got_b, out):
    half, _, wide = a.shape
    out[:half, :, :wide] = a[...]
    out[half:, :, :wide] = got_a[...]
    out[:half, :, wide:] = b[...]
    out[half:, :, wide:] = got_b[...]


def steps_kernel(steps, *refs):
    refs = list(refs)
    at_in, at_out = 0, sum(count for _, count, _ in steps)
    for kernel, ins, outs in steps:
        kernel(*refs[at_in : at_in + ins], *refs[at_out : at_out + outs])
        at_in += ins
        at_out += outs


def call(kernel, ins, outs, us, scratch=(), smem=0, room=62, far_ins=(), far_outs=(), sems=0):
    vmem = pl.BlockSpec(memory_space=pltpu.VMEM)
    far = pl.BlockSpec(memory_space=pltpu.HBM)
    in_specs = [vmem] * len(ins)
    in_specs[:smem] = [pl.BlockSpec(memory_space=pltpu.SMEM)] * smem
    for i in far_ins:
        in_specs[i] = far
    scratch_shapes = [pltpu.VMEM(s, t) for s, t in scratch]
    if sems:
        scratch_shapes.append(pltpu.SemaphoreType.DMA((sems,)))
    return pl.pallas_call(
        kernel,
        out_shape=[jax.ShapeDtypeStruct(s, t) for s, t in outs],
        in_specs=in_specs,
        out_specs=[far if i in far_outs else vmem for i in range(len(outs))],
        scratch_shapes=scratch_shapes,
        compiler_params=pltpu.CompilerParams(vmem_limit_bytes=room << 20),
        cost_estimate=pl.CostEstimate(flops=us * 10**9, bytes_accessed=0, transcendentals=0),
    )(*ins)


def small_steps(steps):
    outs = call(
        functools.partial(steps_kernel, [(k, len(i), len(o)) for k, i, o in steps]),
        [v for _, ins, _ in steps for v in ins],
        [o if isinstance(o[0], tuple) else (o, LOW) for _, _, outs in steps for o in outs],
        2,
        room=20,
    )
    got = []
    for _, _, shapes in steps:
        got.append(outs[: len(shapes)])
        outs = outs[len(shapes) :]
    return got


def send_long(block, n, wrap):
    got = []
    for d in range(1, n):
        pairs = [(i, (i + d) % n) for i in range(n) if wrap or i + d < n]
        got.append(lax.ppermute(block, "blk", pairs))
    return got


def return_long(block, n, distance, wrap):
    pairs = [(i, (i - distance) % n) for i in range(n) if wrap or i >= distance]
    return lax.ppermute(block, "blk", pairs)


def hand_down(held, n, distance):
    return lax.ppermute(held, "blk", [(i, i - 1) for i in range(distance, n)])


def return_short(held, n, root, distance):
    pairs = [((root + k + distance) % n, (root + k) % n) for k in range(0, n, 2 * distance)]
    return lax.ppermute(held, "blk", pairs)


def return_short_rest(helds, n):
    got = []
    for root, held in enumerate(helds):
        d = 4
        while d < n:
            held = held + return_short(held, n, root, d)
            d *= 2
        got.append(held)
    return got


def send_short_first(shorts, n):
    return [
        [held, lax.ppermute(held, "blk", [(root, (root + n // 2) % n)])]
        for root, held in enumerate(shorts)
    ]


def send_short_rest(terms, n):
    for root in range(n // 4):
        d = n // 4
        while d:
            pairs = [((root + k) % n, (root + k + d) % n) for k in range(0, n, 2 * d)]
            held = functools.reduce(jnp.add, terms[root])
            terms[root].append(lax.ppermute(held, "blk", pairs))
            d //= 2
    return [v for several in terms for v in several]


def tied(value, *others):
    return lax.optimization_barrier((value, others))[0]


def trade(v, axis, distance):
    return lax.ppermute(v, axis, [(i, i ^ distance) for i in range(lax.axis_size(axis))])


class Sharing:
    def __init__(self, batch, n):
        self.rest = [("batch", d) for d in (8, 16, 32) if d < batch]
        self.rest += [("blk", d) for d in (4, 8, 16, 32) if d < n]
        self.chunks = 32

    def codes(self):
        codes = []
        for first, second in ((2, 4), (4, 2)):
            code = jnp.int32(0)
            for axis, distance in (("batch", 1), ("batch", first), ("batch", second), ("blk", 2),
                                   ("blk", 1)):
                code = 2 * code + (lax.axis_index(axis) // distance) % 2
            codes.append(code.astype(jnp.int32))
        return jnp.stack(codes)

    def doubled(self, v):
        for axis, distance in self.rest:
            v = v + trade(v, axis, distance)
        return v


def to_tall(pieces):
    return [trade(v, "blk", j) for j, v in enumerate(pieces) if j]


def on_device(
    decoder_input, encoder_output, sequence_lengths, chain_breaks,
    self_inward, self_outward, cross_query, cross_memory, cross_outward,
    feed_up, feed_up_bias, feed_down, feed_down_bias, norm_gains, norm_shifts,
    output_cotangent,
):
    sequences, rows, width = decoder_input.shape
    hidden = feed_up.shape[1]
    n = lax.axis_size("blk")
    rank = lax.axis_index("blk")
    ranks = rank.astype(jnp.int32)[None]
    longest = (sequence_lengths[1] > sequence_lengths[0]).astype(jnp.int32)
    order = jnp.stack([longest, 1 - longest])
    both = 2 * rows
    nk = (n + n // 4) * rows
    pairs = width // PAIR

    sharing = Sharing(lax.axis_size("batch"), n)
    codes = sharing.codes()
    chunks = sharing.chunks
    tall = width // chunks
    blocks = nk // rows

    room = 62 if n > 4 else 22
    block = ((rows, width), LOW)
    x_long, e_long, *shorts = call(
        pick_kernel,
        (sequence_lengths, decoder_input, encoder_output),
        [block, block] + [((both, width), LOW)] * (n // 4),
        1,
        smem=1,
        room=60,
    )
    firsts = send_short_first(shorts, n)
    xl = send_long(x_long, n, False)
    xs = send_short_rest([[v[:rows] for v in terms] for terms in firsts], n)
    shorts = len(xs) // (n // 4)
    e_long = tied(e_long, *[terms[1] for terms in firsts])
    es = send_short_rest([[tied(v[rows:], *xl) for v in terms] for terms in firsts], n)
    el = send_long(e_long, n, True)

    pair_rows = ((nk, 2 * width), LOW)
    saved = [pair_rows, ((nk, pairs * both), LOW)]
    loaded = [pair_rows, ((2, nk, both), LOW)]
    kept_shape = ((nk * (9 if n == 4 else 1), 2 * width + pairs * both), LOW)
    inverses = ((2 * pairs, both), WIDE)
    low_rows, wide_rows = ((both, width), LOW), ((both, width), WIDE)
    q, kept, mixed, inverse, after, cq, n1, xs = call(
        functools.partial(self_kernel, n, shorts),
        (order, ranks, decoder_input, *xl, *xs, self_inward, self_outward, cross_query,
         norm_gains, norm_shifts),
        [low_rows, kept_shape, low_rows, inverses, wide_rows, low_rows, low_rows,
         ((n // 4, rows, width), LOW)],
        12,
        scratch=saved,
        smem=2,
        room=room,
        far_outs=(1,),
        sems=pairs + 1,
    )
    cross_kept, cmixed, cinverse, crossed, es = call(
        functools.partial(cross_kernel, n, shorts),
        (order, ranks, chain_breaks, encoder_output, *el, *es, cq, after, cross_memory,
         cross_outward),
        [kept_shape, low_rows, inverses, wide_rows, ((n // 4, rows, width), LOW)],
        11,
        scratch=saved,
        smem=3,
        room=room,
        far_outs=(0,),
        sems=pairs + 1,
    )
    half = chunks // 2
    layer_output, cross_grad, near, far, g_bias, small_feed = call(
        feed_kernel,
        (order, codes, crossed, output_cotangent, feed_up, feed_up_bias[None], feed_down,
         feed_down_bias[None], norm_gains, norm_shifts),
        [(decoder_input.shape, LOW), ((both, width), WIDE), ((half, tall, 2 * hidden), LOW),
         ((half, tall, 2 * hidden), LOW), ((1, hidden), WIDE), ((3, width), WIDE)],
        14,
        scratch=[low_rows, wide_rows, wide_rows, ((chunks, tall, 2 * hidden), LOW)],
        smem=2,
        room=room,
        far_outs=(2, 3),
        sems=2,
    )
    wide = [hidden, hidden]
    wide_rest = [hidden, hidden + 128]

    def shape(count, lanes):
        return (count, tall, lanes)

    roots = range(n // 4)
    part_shapes = [((rows, width), LOW)] * n
    part_shapes[1] = (((n // 4 + 1) * rows, width), LOW)
    feed_core = trade(far, "batch", 1)
    feed_near = near
    *e_parts, cross_dq, cross_dkv, cross_low = call(
        functools.partial(cross_back_kernel, n),
        (cross_grad, cmixed, cinverse, cq, cross_kept, cross_memory, cross_outward),
        part_shapes + [low_rows, pair_rows, low_rows],
        10,
        scratch=[low_rows, *loaded],
        room=room,
        far_ins=(4,),
        sems=3 * pairs,
    )
    self_grad, g_cross, small_cross = call(
        functools.partial(cross_sums_kernel, n),
        (order, encoder_output, *el, es, cross_grad, cross_low, cmixed, cross_dq, cross_dkv,
         after, n1, cross_query, norm_gains),
        [wide_rows, ((width, 4 * width), LOW), ((2, width), WIDE)],
        4,
        smem=1,
        room=room,
    )
    (a, a_send, b, b_send), _ = small_steps(
        [(add_core, (feed_near, feed_core), [shape(8, w) for w in wide for _ in "ks"]),
         (note, (small_cross,), [])]
    )
    a_got, b_got = trade(a_send, "batch", 2), trade(b_send, "batch", 4)
    e_got = [return_long(e_parts[d], n, d, True) for d in range(1, n)]
    *parts, own, near, far = call(
        functools.partial(self_back_kernel, n),
        (order, codes, decoder_input, *xl, xs, self_grad, mixed, inverse, q, kept, self_inward,
         self_outward, norm_gains, norm_shifts, small_feed, g_bias, small_cross, g_cross, a),
        [((rows, width), LOW)] * blocks
        + [((both, width), WIDE), (shape(half, sum(wide_rest)), LOW),
           (shape(half, sum(wide_rest)), LOW)],
        14,
        scratch=[(shape(chunks, sum(wide_rest)), LOW), low_rows, low_rows, pair_rows, *loaded],
        smem=2,
        room=room,
        far_ins=(n + 7,),
        far_outs=(blocks + 1, blocks + 2),
        sems=3 * pairs,
    )
    (a, a_send), (b, b_send), (e_long, *e_short) = small_steps(
        [(add_halves, (a, a_got, own), [shape(4, wide[0])] * 2),
         (add_halves, (b, b_got), [shape(4, wide[1])] * 2),
         (add_returns, (e_parts[0], e_parts[1], *e_got),
          [((rows, width), WIDE)] + [(rows, width)] * (n // 4))]
    )
    a_got, b_got = trade(a_send, "batch", 4), trade(b_send, "batch", 2)
    e_got = [return_short(e_short[k], n, k, 2) for k in roots]
    held = tied(parts[n - 1], a_send)
    for d in range(n - 2, 2, -1):
        held = parts[d] + hand_down(held, n, d + 1)
    long_got = hand_down(held, n, 3)
    feed, (a, a_send, b, b_send), (held,), *e_short = small_steps(
        [(add_to_pieces, (a, a_got, b, b_got), [shape(1, sum(wide))] * 4),
         (add_core, (near, trade(tied(far, a_send), "batch", 1)),
          [shape(8, w) for w in wide_rest for _ in "ks"]),
         (add_all, (own, parts[2], long_got), [(rows, width)])]
        + [(add_all, (own, e_short[k], e_got[k]), [(rows, width)]) for k in roots]
    )
    e_short = return_short_rest([v for v, in e_short], n)
    a_got, b_got = trade(a_send, "batch", 2), trade(b_send, "batch", 4)
    (a, a_send), (b, b_send), (feed,) = small_steps(
        [(add_halves, (a, a_got), [shape(4, wide_rest[0])] * 2),
         (add_halves, (b, b_got), [shape(4, wide_rest[1])] * 2),
         (add_all, (own, feed[0], *to_tall(feed)), [shape(1, sum(wide))])]
    )
    feed = sharing.doubled(feed)
    a_got, b_got = trade(a_send, "batch", 4), trade(b_send, "batch", 2)
    rest, (fa, fb) = small_steps(
        [(add_to_pieces, (a, a_got, b, b_got), [shape(1, sum(wide_rest))] * 4),
         (lay, (feed, *to_tall([feed] * 4)), [shape(4, w) for w in wide])]
    )
    (rest,), (fa,), (fb,) = small_steps(
        [(add_all, (own, rest[0], *to_tall(rest)), [shape(1, sum(wide_rest))]),
         (join, (fa, trade(fa, "batch", 4)), [shape(8, wide[0])]),
         (join, (fb, trade(fb, "batch", 2)), [shape(8, wide[1])])]
    )
    rest = sharing.doubled(rest)
    (ra, rb), (feed,) = small_steps(
        [(lay, (rest, *to_tall([rest] * 4)), [shape(4, w) for w in wide_rest]),
         (beside, (fa, trade(fa, "batch", 2), fb, trade(fb, "batch", 4)),
          [shape(16, sum(wide))])]
    )
    ra_got, rb_got = trade(ra, "batch", 4), trade(rb, "batch", 2)
    feed_got = trade(feed, "batch", 1)
    held, *shorts = tied((held, *parts[n:]), ra)
    long_got = hand_down(held, n, 2)
    got = [return_short(shorts[k], n, k, 1) for k in roots]
    (ra,), (rb,), _, (held,), *shorts = small_steps(
        [(join, (ra, ra_got), [shape(8, wide_rest[0])]),
         (join, (rb, rb_got), [shape(8, wide_rest[1])]),
         (note, (feed_got,), []),
         (add_all, (own, parts[1], long_got), [(rows, width)])]
        + [(add_all, (own, parts[n + k], got[k]), [(rows, width)]) for k in roots]
    )
    ra_got, rb_got = trade(ra, "batch", 2), trade(rb, "batch", 4)
    long_got = hand_down(held, n, 1)
    got = [return_short(shorts[k][0], n, k, 2) for k in roots]
    s_up, s_down = call(
        functools.partial(unpack_feed_kernel, [(0, 2, 0, 0, 1), (0, 2, 1, hidden, hidden // width)]),
        (codes, feed, feed_got),
        [(feed_up.shape, WIDE), (feed_down.shape, WIDE)],
        6,
        smem=1,
        room=room,
    )
    (rest,), _, *shorts = small_steps(
        [(beside, (ra, ra_got, rb, rb_got), [shape(16, sum(wide_rest))]),
         (note, (s_down[:8, :128], long_got), [])]
        + [(add_all, (own, shorts[k][0], got[k]), [(rows, width)]) for k in roots]
    )
    shorts = return_short_rest([v for v, in shorts], n)
    rest_got = trade(rest, "batch", 1)
    input_gradient, encoder_gradient = call(
        functools.partial(last_kernel, n),
        (order, ranks, decoder_input, self_grad, own, norm_gains, parts[0], long_got, e_long,
         *shorts, *e_short),
        [(decoder_input.shape, WIDE), (decoder_input.shape, WIDE)],
        3,
        smem=2,
        room=room,
    )
    at = hidden
    places = [(0, 2, 0, 0, 1), (0, 2, 0, 2 * width, 1), (0, 2, 0, 3 * width, 1),
              (0, 2, 1, at, 1), (0, 2, 1, at + 3 * width, 1), (0, 2, 1, at + 4 * width, 1)]
    s_cm, s_cq, s_cout, s_in, s_out, up_bias, down_bias, gains, shifts = call(
        functools.partial(unpack_rest_kernel, places),
        (codes, rest, rest_got),
        [(s, WIDE) for s in (cross_memory.shape, cross_query.shape, cross_outward.shape,
                             self_inward.shape, self_outward.shape, (1, hidden), (1, width),
                             norm_gains.shape, norm_shifts.shape)],
        5,
        scratch=[((width, 128), WIDE)],
        smem=1,
        room=room,
    )
    return (
        layer_output, input_gradient, encoder_gradient, s_in, s_out, s_cq, s_cm, s_cout,
        s_up, up_bias[0], s_down, down_bias[0], gains, shifts,
    )


def solution(mesh):
    blocked = P("batch", "blk", None)
    placed = (blocked, blocked, P("batch"), P("batch", None)) + (P(),) * 11 + (blocked,)
    return jax.shard_map(
        on_device,
        mesh=mesh,
        in_specs=placed,
        out_specs=(blocked,) * 3 + (P(),) * 11,
        check_vma=False,
    )
```

```python
import functools

import jax
import jax.numpy as jnp
from jax import lax
from jax.experimental import pallas as pl
from jax.experimental.pallas import tpu as pltpu
from jax.sharding import PartitionSpec as P

HEAD = 64
PAIR = 2 * HEAD
EPSILON = 1e-05
FAR = 1e30
LOW = jnp.bfloat16
WIDE = jnp.float32


def contract(left, right, a, b):
    return lax.dot_general(left, right, (((a,), (b,)), ((), ())), preferred_element_type=WIDE)


def nn(left, right):
    return contract(left, right, 1, 0)


def nt(left, right):
    return contract(left, right, 1, 1)


def tn(left, right):
    return contract(left, right, 0, 0)


def standard(values):
    center = values - jnp.mean(values, axis=-1, keepdims=True)
    spread = jnp.mean(center * center, axis=-1, keepdims=True)
    inverse = lax.rsqrt(spread + EPSILON)
    return center * inverse, inverse


def norm_back(values, gain, upstream):
    unit, inverse = standard(values)
    m = upstream * gain
    grad = inverse * (
        m
        - jnp.mean(m, axis=-1, keepdims=True)
        - unit * jnp.mean(m * unit, axis=-1, keepdims=True)
    )
    return grad, jnp.sum(upstream * unit, axis=0), jnp.sum(upstream, axis=0)


def gelu_pair(x):
    z = jnp.abs(x) * 0.7071067811865476
    t = 1.0 / (1.0 + 0.5 * z)
    poly = 0.17087277
    for c in (
        -0.82215223,
        1.48851587,
        -1.13520398,
        0.27886807,
        -0.18628806,
        0.09678418,
        0.37409196,
        1.00002368,
        -1.26551223,
    ):
        poly = poly * t + c
    bell = jnp.exp(-z * z)
    tail = 0.5 * t * jnp.exp(poly) * bell
    share = jnp.where(x >= 0, 1.0 - tail, tail)
    return x * share, share + x * bell * 0.3989422804014327


def by_head(pair_rows):
    lane = lax.broadcasted_iota(jnp.int32, pair_rows.shape, 1)
    zero = jnp.zeros_like(pair_rows)
    return jnp.concatenate(
        [jnp.where(lane < HEAD, pair_rows, zero), jnp.where(lane >= HEAD, pair_rows, zero)], axis=0
    )


def own_parts(both):
    rows = both.shape[1] // 2
    return jnp.concatenate([both[:HEAD, :rows], both[HEAD:, rows:]], axis=0)


def columns(place, wide):
    return pl.ds(pl.multiple_of(place * wide, wide), wide)


def attend(q_ref, kv_ref, p_ref, low_ref, inverse_ref, plan, mask, done):
    rows = q_ref.shape[0] // 2
    width = q_ref.shape[1]

    @pl.loop(0, width // PAIR)
    def _(pair):
        lanes = columns(pair, PAIR)
        values = columns(width // PAIR + pair, PAIR)
        spot = columns(pair, 2 * rows)
        for seq, blocks in enumerate(plan):
            mine = slice(seq * rows, (seq + 1) * rows)
            queries = by_head(q_ref[mine, lanes])
            scores, tops = [], []
            for block in blocks:
                s = nt(kv_ref[block * rows : (block + 1) * rows, lanes], queries)
                s, far = mask(block, s)
                scores.append((s, far))
                tops.append(jnp.max(s, axis=0, keepdims=True) - far)
            top = functools.reduce(jnp.maximum, tops)
            total = jnp.zeros_like(top)
            mixed = jnp.zeros((PAIR, 2 * rows), WIDE)
            for block, (s, far) in zip(blocks, scores):
                at = slice(block * rows, (block + 1) * rows)
                p = jnp.exp(s - (top + far))
                total = total + jnp.sum(p, axis=0, keepdims=True)
                p = p.astype(LOW)
                p_ref[at, spot] = p
                mixed = mixed + tn(kv_ref[at, values], p)
            inverse = 1.0 / total
            low_ref[mine, lanes] = own_parts(mixed * inverse).T.astype(LOW)
            inverse_ref[pl.ds(2 * pair + seq, 1), :] = inverse
        done(pair)


def attend_back(up, low_ref, inverse_ref, q_ref, kv_ref, p_ref, dq_ref, dkv_ref, plan, ready, done):
    rows = q_ref.shape[0] // 2
    width = q_ref.shape[1]
    scale = HEAD ** (-0.5)

    @pl.loop(0, width // PAIR)
    def _(pair):
        lanes = columns(pair, PAIR)
        values = columns(width // PAIR + pair, PAIR)
        slot = lax.rem(pair, 2)
        ready(pair)
        for seq, blocks in enumerate(plan):
            mine = slice(seq * rows, (seq + 1) * rows)
            queries = by_head(q_ref[mine, lanes])
            inverse = inverse_ref[pl.ds(2 * pair + seq, 1), :]
            scaled = up[mine, lanes].astype(WIDE) * own_parts(jnp.broadcast_to(inverse, (PAIR, 2 * rows))).T
            inner = (scaled * low_ref[mine, lanes].astype(WIDE)).T
            offset = jnp.concatenate(
                [
                    jnp.sum(inner[:HEAD], axis=0, keepdims=True),
                    jnp.sum(inner[HEAD:], axis=0, keepdims=True),
                ],
                axis=1,
            )
            upper = by_head(scaled.astype(LOW))
            dq = jnp.zeros((PAIR, 2 * rows), WIDE)
            for block in blocks:
                at = slice(block * rows, (block + 1) * rows)
                p = p_ref[slot, at, :]
                dp = nt(kv_ref[at, values], upper)
                ds = (p.astype(WIDE) * (dp - offset)).astype(LOW)
                dkv_ref[at, values] = nn(p, upper).astype(LOW)
                dkv_ref[at, lanes] = nn(ds, queries).astype(LOW)
                dq = dq + tn(kv_ref[at, lanes], ds)
            dq_ref[mine, lanes] = (own_parts(dq).T * scale).astype(LOW)
        done(pair)


def saves(kv, p, kept, sems):
    rows, width = slice(0, kv.shape[0]), kv.shape[1]
    wide = 2 * PAIR * p.shape[1] // width

    def p_save(pair):
        at = pl.ds(pl.multiple_of(width + pair * wide, PAIR), wide)
        return pltpu.make_async_copy(p.at[:, columns(pair, wide)], kept.at[rows, at], sems.at[pair])

    pairs = width // (2 * PAIR)
    return pltpu.make_async_copy(kv, kept.at[rows, :width], sems.at[pairs]), p_save


def plan_of(n):
    return (tuple(range(n)), tuple(range(n, n + n // 4)))


def add_terms(out, refs, terms):
    for j in range(out.shape[0]):
        total = refs[j * terms][...]
        for ref in refs[j * terms + 1 : (j + 1) * terms]:
            total = total + ref[...]
        out[j] = total


def pick_kernel(lengths, x, enc, x_long, e_long, *shorts):
    rows = x_long.shape[0]
    long = jnp.where(lengths[1] > lengths[0], 1, 0)
    x_long[...] = x[long]
    e_long[...] = enc[long]
    for root, ref in enumerate(shorts):
        share = (lax.axis_index("blk") == root).astype(jnp.int32).astype(WIDE)
        ref[:rows] = (x[1 - long].astype(WIDE) * share).astype(LOW)
        ref[rows:] = (enc[1 - long].astype(WIDE) * share).astype(LOW)


def self_kernel(n, terms, order, rank, x, *refs):
    xl, refs = refs[: n - 1], refs[n - 1 :]
    shorts, refs = refs[: terms * (n // 4)], refs[terms * (n // 4) :]
    (
        w_in, w_out, w_cq, gains, shifts,
        q, kept, mixed, inverse, after, cq, n1, xs, kv, p, sems,
    ) = refs
    pairs = q.shape[1] // PAIR
    kv_save, p_save = saves(kv, p, kept, sems)
    add_terms(xs, shorts, terms)
    rows, width = x.shape[1:]
    r = rank[0]

    def first_norm(v):
        return (standard(v.astype(WIDE))[0] * gains[0:1] + shifts[0:1]).astype(LOW)

    def keys(v, block):
        kv[block * rows : (block + 1) * rows, :] = nn(first_norm(v), w_in[:, width:]).astype(LOW)

    mine = jnp.concatenate([x[order[0]], x[order[1]]], axis=0)
    normed = first_norm(mine)
    kv[0:rows, :] = nn(normed[:rows], w_in[:, width:]).astype(LOW)
    for d in range(1, n):
        keys(xl[d - 1][...], d)
    for j in range(n // 4):
        keys(xs[j], n + j)
    kv_save.start()
    q[...] = nn(normed, w_in[:, :width]).astype(LOW) * HEAD ** (-0.5)

    def mask(block, s):
        if 0 < block < n:
            return s, jnp.where(r >= block, 0.0, FAR)
        key = lax.broadcasted_iota(jnp.int32, s.shape, 0)
        query = lax.broadcasted_iota(jnp.int32, s.shape, 1)
        query = jnp.where(query >= rows, query - rows, query)
        if block >= n:
            query = query + (r - (block - n)) * rows
        return jnp.where(key <= query, s, -FAR), 0.0

    attend(q, kv, p, mixed, inverse, plan_of(n), mask, lambda pair: p_save(pair).start())
    total = mine.astype(WIDE) + nn(mixed[...], w_out[...])
    after[...] = total
    second = (standard(total)[0] * gains[1:2] + shifts[1:2]).astype(LOW)
    n1[...] = second
    cq[...] = nn(second, w_cq[...]).astype(LOW) * HEAD ** (-0.5)
    kv_save.wait()
    for pair in range(pairs):
        p_save(pair).wait()


def cross_kernel(n, terms, order, rank, breaks, enc, *refs):
    el, refs = refs[: n - 1], refs[n - 1 :]
    shorts, refs = refs[: terms * (n // 4)], refs[terms * (n // 4) :]
    cq, after, w_cm, w_out, kept, mixed, inverse, crossed, es, kv, p, sems = refs
    pairs = cq.shape[1] // PAIR
    kv_save, p_save = saves(kv, p, kept, sems)
    add_terms(es, shorts, terms)
    rows, width = enc.shape[1:]
    r = rank[0]
    kv[0:rows, :] = nn(enc[order[0]], w_cm[...]).astype(LOW)
    for d in range(1, n):
        kv[d * rows : (d + 1) * rows, :] = nn(el[d - 1][...], w_cm[...]).astype(LOW)
    for j in range(n // 4):
        kv[(n + j) * rows : (n + j + 1) * rows, :] = nn(es[j], w_cm[...]).astype(LOW)

    kv_save.start()

    def mask(block, s):
        key = lax.broadcasted_iota(jnp.int32, s.shape, 0)
        if block < n:
            first = lax.rem(r - block + n, n) * rows
            which = order[0]
        else:
            first = (block - n) * rows
            which = order[1]
        shut = key == breaks[which, 0] - first
        for i in range(1, breaks.shape[1]):
            shut = shut | (key == breaks[which, i] - first)
        return jnp.where(shut, -FAR, s), 0.0

    attend(cq, kv, p, mixed, inverse, plan_of(n), mask, lambda pair: p_save(pair).start())
    crossed[...] = after[...] + nn(mixed[...], w_out[...])
    kv_save.wait()
    for pair in range(pairs):
        p_save(pair).wait()


def spread(sums, code, value, lane):
    tall = sums.shape[1]
    for k in range(sums.shape[0]):
        part = value[k * tall : (k + 1) * tall, :]
        sums[k ^ code, :, lane : lane + value.shape[1]] = part


def feed_kernel(
    order, codes, crossed, cot, w_up, b_up, w_down, b_down, gains, shifts,
    out, grad, near, far, g_bias, g_small, third, total, back, sums, sems,
):
    rows, width = cot.shape[1:]
    hidden = w_up.shape[1]
    half, tall = near.shape[:2]
    deep = hidden // (2 * half)
    third[...] = (standard(crossed[...])[0] * gains[2:3] + shifts[2:3]).astype(LOW)
    up_low = jnp.concatenate([cot[order[0]], cot[order[1]]], axis=0)
    total[...] = crossed[...] + b_down[...].astype(WIDE)
    back[...] = jnp.zeros_like(back)

    @pl.loop(0, hidden // width)
    def _(c):
        at = columns(c, width)
        rising = nn(third[...], w_up[:, at]) + b_up[:, at].astype(WIDE)
        active, slope = gelu_pair(rising)
        active = active.astype(LOW)
        total[...] += nn(active, w_down[at, :])
        rising_grad = nt(up_low, w_down[at, :]) * slope
        g_bias[:, at] = jnp.sum(rising_grad, axis=0, keepdims=True)
        rising_grad = rising_grad.astype(LOW)
        back[...] += nt(rising_grad, w_up[:, at])
        g_up = tn(third[...], rising_grad).astype(LOW)
        for k in range(2 * half):
            sums[k ^ codes[0], :, at] = g_up[k * tall : (k + 1) * tall]
        g_down = tn(active, up_low).astype(LOW)
        for k in range(width // deep):
            for i in range(deep // tall):
                first = k * deep + i * tall
                lanes = slice(hidden + i * width, hidden + (i + 1) * width)
                sums[(c * (width // deep) + k) ^ codes[1], :, lanes] = g_down[first : first + tall]

    saves = [
        pltpu.make_async_copy(sums.at[:half], near, sems.at[0]),
        pltpu.make_async_copy(sums.at[half:], far, sems.at[1]),
    ]
    for save in saves:
        save.start()
    low = total[...].astype(LOW)
    out[order[0]] = low[:rows]
    out[order[1]] = low[rows:]
    upward = up_low.astype(WIDE)
    inner, gain, shift = norm_back(crossed[...], gains[2:3], back[...])
    grad[...] = upward + inner
    g_small[0, :] = jnp.sum(upward, axis=0)
    g_small[1, :] = gain
    g_small[2, :] = shift
    for save in saves:
        save.wait()


def loads(kept, kv, p, sems):
    rows, width, wide = slice(0, kv.shape[0]), kv.shape[1], p.shape[2]
    pairs = width // (2 * PAIR)

    def p_copy(pair):
        at = pl.ds(pl.multiple_of(width + pair * wide, PAIR), wide)
        return pltpu.make_async_copy(kept.at[rows, at], p.at[lax.rem(pair, 2)], sems.at[pair])

    def kv_copies(pair):
        return [
            pltpu.make_async_copy(
                kept.at[rows, columns(i, PAIR)], kv.at[:, columns(i, PAIR)], sems.at[pairs + i]
            )
            for i in (pair, pairs + pair)
        ]

    for pair in range(pairs):
        if pair < 2:
            p_copy(pair).start()
        for copy in kv_copies(pair):
            copy.start()

    def ready(pair):
        for copy in (p_copy(pair), *kv_copies(pair)):
            copy.wait()

    def done(pair):
        @pl.when(pair + 2 < pairs)
        def _():
            p_copy(pair + 2).start()

    return ready, done


def put_part(parts, n, b, value):
    rows = value.shape[0]
    if b < len(parts):
        parts[b][:rows, :] = value
    else:
        parts[1][(b - n + 1) * rows : (b - n + 2) * rows, :] = value


def cross_back_kernel(n, grad, mixed, inverse, cq, kept, w_cm, w_cout, *refs):
    parts, (dq, dkv, low, up, kv, p, sems) = refs[:-7], refs[-7:]
    ready, done = loads(kept, kv, p, sems)
    rows = parts[0].shape[0]
    low[...] = grad[...].astype(LOW)
    up[...] = nt(low[...], w_cout[...]).astype(LOW)
    attend_back(up, mixed, inverse, cq, kv, p, dq, dkv, plan_of(n), ready, done)
    for b in range(n + n // 4):
        put_part(parts, n, b, nt(dkv[b * rows : (b + 1) * rows, :], w_cm[...]).astype(LOW))


def cross_sums_kernel(n, order, enc, *refs):
    el, es, refs = refs[: n - 1], refs[n - 1], refs[n:]
    grad, low, mixed, dq, dkv, after, n1, w_cq, gains, self_grad, g_cross, g_small = refs
    rows, width = enc.shape[1:]
    g_cross[:, 3 * width :] = tn(mixed[...], low[...]).astype(LOW)
    g_cross[:, 2 * width : 3 * width] = tn(n1[...], dq[...]).astype(LOW)
    total = tn(enc[order[0]], dkv[0:rows, :])
    for d in range(1, n):
        total = total + tn(el[d - 1][...], dkv[d * rows : (d + 1) * rows, :])
    for j in range(n // 4):
        total = total + tn(es[j], dkv[(n + j) * rows : (n + j + 1) * rows, :])
    g_cross[:, : 2 * width] = total.astype(LOW)
    inner, gain, shift = norm_back(after[...], gains[1:2], nt(dq[...], w_cq[...]))
    self_grad[...] = grad[...] + inner
    g_small[0, :] = gain
    g_small[1, :] = shift


def self_back_kernel(n, order, codes, x, *refs):
    xl, refs = refs[: n - 1], refs[n - 1 :]
    (
        xs, self_grad, mixed, inverse, q, kept, w_in, w_out, gains, shifts, small_feed, g_bias,
        small_cross, g_cross, _,
    ) = refs[:15]
    parts, (own, near, far, sums, dq, up, dkv, kv, p, sems) = refs[15:-10], refs[-10:]
    ready, done = loads(kept, kv, p, sems)
    rows, width = x.shape[1:]
    low = self_grad[...].astype(LOW)
    up[...] = nt(low, w_out[...]).astype(LOW)
    attend_back(up, mixed, inverse, q, kv, p, dq, dkv, plan_of(n), ready, done)
    mine = jnp.concatenate([x[order[0]], x[order[1]]], axis=0).astype(WIDE)
    unit = standard(mine)[0]
    normed = (unit * gains[0:1] + shifts[0:1]).astype(LOW)
    g_out = tn(mixed[...], low).astype(LOW)
    g_query = tn(normed, dq[...]).astype(LOW)
    mine = nt(dq[...], w_in[:, :width])
    own[...] = mine
    gain = jnp.sum(mine * unit, axis=0)
    shift = jnp.sum(mine, axis=0)
    total = None
    for b in range(n + n // 4):
        if b == 0:
            key_unit, key_low = unit[:rows], normed[:rows]
        else:
            v = xl[b - 1][...] if b < n else xs[b - n]
            key_unit = standard(v.astype(WIDE))[0]
            key_low = (key_unit * gains[0:1] + shifts[0:1]).astype(LOW)
        pairs = dkv[b * rows : (b + 1) * rows, :]
        term = tn(key_low, pairs)
        total = term if total is None else total + term
        back = nt(pairs, w_in[:, width:])
        put_part(parts, n, b, back.astype(LOW))
        gain = gain + jnp.sum(back * key_unit, axis=0)
        shift = shift + jnp.sum(back, axis=0)
    small = [gain[None], small_cross[0:1], small_feed[1:2], shift[None], small_cross[1:2],
             small_feed[2:3], small_feed[0:1], g_bias[...]]
    small = [v[:, i : i + 128] for v in small for i in range(0, v.shape[1], 128)]
    small.append(jnp.zeros((width - len(small), 128), WIDE))
    small = jnp.concatenate(small, axis=0).astype(LOW)
    spread(sums, codes[0], g_cross, 0)
    spread(sums, codes[1], g_query, 4 * width)
    spread(sums, codes[1], total.astype(LOW), 5 * width)
    spread(sums, codes[1], g_out, 7 * width)
    spread(sums, codes[1], small, 8 * width)
    half = sums.shape[0] // 2
    saves = [
        pltpu.make_async_copy(sums.at[:half], near, sems.at[0]),
        pltpu.make_async_copy(sums.at[half:], far, sems.at[1]),
    ]
    for save in saves:
        save.start()
    for save in saves:
        save.wait()


def unpack(plan, codes, pieces, outs):
    for out, (at, count, which, lane, side) in zip(outs, plan):
        wide = out.shape[1]
        depth, tall = pieces[at].shape[:2]
        for k in range(count * depth):
            first = (codes[which] ^ k) * (tall * side)
            for i in range(side):
                start = pl.multiple_of(first + i * tall, tall)
                lanes = slice(lane + i * wide, lane + (i + 1) * wide)
                out[pl.ds(start, tall), :] = pieces[at + k // depth][k % depth, :, lanes].astype(WIDE)


def unpack_feed_kernel(plan, codes, *refs):
    unpack(plan, codes, refs[: -len(plan)], refs[-len(plan) :])


def unpack_rest_kernel(plan, codes, *refs):
    *refs, up_bias, down_bias, gains, shifts, small = refs
    count = len(plan) - 1
    unpack(plan, codes, refs[:-count], refs[-count:] + [small])
    at = 0
    for out, count in ((gains, 3), (shifts, 3), (down_bias, 1), (up_bias, 1)):
        for i in range(count):
            across = out.shape[1] // 128
            row = [small[at + j : at + j + 1, :] for j in range(across)]
            out[i : i + 1, :] = jnp.concatenate(row, axis=1)
            at += across


def last_kernel(n, order, rank, x, self_grad, own, gains, part, part_got, e_long, *refs):
    shorts, e_shorts, (grad, e_grad) = refs[: n // 4], refs[n // 4 : n // 2], refs[-2:]
    rows = x.shape[1]

    def mine(helds):
        total = jnp.zeros(part.shape, WIDE)
        for root, held in enumerate(helds):
            total = jnp.where(rank[0] == root, held[...].astype(WIDE), total)
        return total

    long_up = own[:rows] + part[...].astype(WIDE) + part_got[...].astype(WIDE)
    short_up = own[rows:] + mine(shorts)
    for which, up, at in ((order[0], long_up, 0), (order[1], short_up, rows)):
        inner, _, _ = norm_back(x[which].astype(WIDE), gains[0:1], up)
        grad[which] = self_grad[at : at + rows] + inner
    e_grad[order[0]] = e_long[...]
    e_grad[order[1]] = mine(e_shorts)


def add_core(near, got, *outs):
    at = 0
    half = near.shape[0] // 2
    for keep, send in zip(outs[::2], outs[1::2]):
        lanes = slice(at, at + keep.shape[2])
        keep[...] = near[:half, :, lanes] + got[:half, :, lanes]
        send[...] = near[half:, :, lanes] + got[half:, :, lanes]
        at = lanes.stop


def add_returns(own, near, near_got, *refs):
    rows = own.shape[0]
    count = near.shape[0] // rows
    total = own[...].astype(WIDE) + near_got[:rows, :].astype(WIDE)
    for ref in refs[:-count]:
        total = total + ref[...].astype(WIDE)
    refs[-count][...] = total
    for k in range(1, count):
        at = slice(k * rows, (k + 1) * rows)
        refs[k - count][...] = near[at, :] + near_got[at, :]


def add_halves(keep, got, *outs):
    half = keep.shape[0] // 2
    outs[-2][...] = keep[:half] + got[:half]
    outs[-1][...] = keep[half:] + got[half:]


def add_to_pieces(a, got_a, b, got_b, *outs):
    wide = a.shape[2]
    for k, out in enumerate(outs[-a.shape[0] :]):
        out[:, :, :wide] = a[k : k + 1] + got_a[k : k + 1]
        out[:, :, wide:] = b[k : k + 1] + got_b[k : k + 1]


def note(*refs):
    pass


def add_all(_, *refs):
    *parts, out = refs
    total = parts[0][...].astype(WIDE)
    for part in parts[1:]:
        total = total + part[...].astype(WIDE)
    out[...] = total.astype(out.dtype)


def lay_whole(_, *refs):
    for k, ref in enumerate(refs[:-1]):
        refs[-1][k : k + 1] = ref[...]


def lay(*refs):
    *parts, a, b = refs
    wide = a.shape[2]
    for k, part in enumerate(parts):
        a[k : k + 1] = part[:, :, :wide]
        b[k : k + 1] = part[:, :, wide:]


def join(a, b, out):
    out[: a.shape[0]] = a[...]
    out[a.shape[0] :] = b[...]


def beside(a, got_a, b, got_b, out):
    half, _, wide = a.shape
    out[:half, :, :wide] = a[...]
    out[half:, :, :wide] = got_a[...]
    out[:half, :, wide:] = b[...]
    out[half:, :, wide:] = got_b[...]


def steps_kernel(steps, *refs):
    refs = list(refs)
    at_in, at_out = 0, sum(count for _, count, _ in steps)
    for kernel, ins, outs in steps:
        kernel(*refs[at_in : at_in + ins], *refs[at_out : at_out + outs])
        at_in += ins
        at_out += outs


def call(kernel, ins, outs, us, scratch=(), smem=0, room=62, far_ins=(), far_outs=(), sems=0):
    vmem = pl.BlockSpec(memory_space=pltpu.VMEM)
    far = pl.BlockSpec(memory_space=pltpu.HBM)
    in_specs = [vmem] * len(ins)
    in_specs[:smem] = [pl.BlockSpec(memory_space=pltpu.SMEM)] * smem
    for i in far_ins:
        in_specs[i] = far
    scratch_shapes = [pltpu.VMEM(s, t) for s, t in scratch]
    if sems:
        scratch_shapes.append(pltpu.SemaphoreType.DMA((sems,)))
    return pl.pallas_call(
        kernel,
        out_shape=[jax.ShapeDtypeStruct(s, t) for s, t in outs],
        in_specs=in_specs,
        out_specs=[far if i in far_outs else vmem for i in range(len(outs))],
        scratch_shapes=scratch_shapes,
        compiler_params=pltpu.CompilerParams(vmem_limit_bytes=room << 20),
        cost_estimate=pl.CostEstimate(flops=us * 10**9, bytes_accessed=0, transcendentals=0),
    )(*ins)


def small_steps(steps):
    outs = call(
        functools.partial(steps_kernel, [(k, len(i), len(o)) for k, i, o in steps]),
        [v for _, ins, _ in steps for v in ins],
        [o if isinstance(o[0], tuple) else (o, LOW) for _, _, outs in steps for o in outs],
        2,
        room=20,
    )
    got = []
    for _, _, shapes in steps:
        got.append(outs[: len(shapes)])
        outs = outs[len(shapes) :]
    return got


def send_long(block, n, wrap):
    got = []
    for d in range(1, n):
        pairs = [(i, (i + d) % n) for i in range(n) if wrap or i + d < n]
        got.append(lax.ppermute(block, "blk", pairs))
    return got


def return_long(block, n, distance, wrap):
    pairs = [(i, (i - distance) % n) for i in range(n) if wrap or i >= distance]
    return lax.ppermute(block, "blk", pairs)


def hand_down(held, n, distance):
    return lax.ppermute(held, "blk", [(i, i - 1) for i in range(distance, n)])


def return_short(held, n, root, distance):
    pairs = [((root + k + distance) % n, (root + k) % n) for k in range(0, n, 2 * distance)]
    return lax.ppermute(held, "blk", pairs)


def return_short_rest(helds, n):
    got = []
    for root, held in enumerate(helds):
        d = 4
        while d < n:
            held = held + return_short(held, n, root, d)
            d *= 2
        got.append(held)
    return got


def send_short_first(shorts, n):
    return [
        [held, lax.ppermute(held, "blk", [(root, (root + n // 2) % n)])]
        for root, held in enumerate(shorts)
    ]


def send_short_rest(terms, n):
    for root in range(n // 4):
        d = n // 4
        while d:
            pairs = [((root + k) % n, (root + k + d) % n) for k in range(0, n, 2 * d)]
            held = functools.reduce(jnp.add, terms[root])
            terms[root].append(lax.ppermute(held, "blk", pairs))
            d //= 2
    return [v for several in terms for v in several]


def tied(value, *others):
    return lax.optimization_barrier((value, others))[0]


def trade(v, axis, distance):
    return lax.ppermute(v, axis, [(i, i ^ distance) for i in range(lax.axis_size(axis))])


class Sharing:
    def __init__(self, batch, n):
        self.rest = [("batch", d) for d in (8, 16, 32) if d < batch]
        self.rest += [("blk", d) for d in (4, 8, 16, 32) if d < n]
        self.chunks = 32

    def codes(self):
        codes = []
        for first, second in ((2, 4), (4, 2)):
            code = jnp.int32(0)
            for axis, distance in (("batch", 1), ("batch", first), ("batch", second), ("blk", 2),
                                   ("blk", 1)):
                code = 2 * code + (lax.axis_index(axis) // distance) % 2
            codes.append(code.astype(jnp.int32))
        return jnp.stack(codes)

    def doubled(self, v):
        for axis, distance in self.rest:
            v = v + trade(v, axis, distance)
        return v


def to_tall(pieces):
    return [trade(v, "blk", j) for j, v in enumerate(pieces) if j]


def on_device(
    decoder_input, encoder_output, sequence_lengths, chain_breaks,
    self_inward, self_outward, cross_query, cross_memory, cross_outward,
    feed_up, feed_up_bias, feed_down, feed_down_bias, norm_gains, norm_shifts,
    output_cotangent,
):
    sequences, rows, width = decoder_input.shape
    hidden = feed_up.shape[1]
    n = lax.axis_size("blk")
    rank = lax.axis_index("blk")
    ranks = rank.astype(jnp.int32)[None]
    longest = (sequence_lengths[1] > sequence_lengths[0]).astype(jnp.int32)
    order = jnp.stack([longest, 1 - longest])
    both = 2 * rows
    nk = (n + n // 4) * rows
    pairs = width // PAIR

    sharing = Sharing(lax.axis_size("batch"), n)
    codes = sharing.codes()
    chunks = sharing.chunks
    tall = width // chunks
    blocks = nk // rows

    room = 62 if n > 4 else 22
    block = ((rows, width), LOW)
    x_long, e_long, *shorts = call(
        pick_kernel,
        (sequence_lengths, decoder_input, encoder_output),
        [block, block] + [((both, width), LOW)] * (n // 4),
        1,
        smem=1,
        room=60,
    )
    firsts = send_short_first(shorts, n)
    xl = send_long(x_long, n, False)
    xs = send_short_rest([[v[:rows] for v in terms] for terms in firsts], n)
    shorts = len(xs) // (n // 4)
    e_long = tied(e_long, *[terms[1] for terms in firsts])
    es = send_short_rest([[tied(v[rows:], *xl) for v in terms] for terms in firsts], n)
    el = send_long(e_long, n, True)

    pair_rows = ((nk, 2 * width), LOW)
    saved = [pair_rows, ((nk, pairs * both), LOW)]
    loaded = [pair_rows, ((2, nk, both), LOW)]
    kept_shape = ((nk * (9 if n == 4 else 1), 2 * width + pairs * both), LOW)
    inverses = ((2 * pairs, both), WIDE)
    low_rows, wide_rows = ((both, width), LOW), ((both, width), WIDE)
    q, kept, mixed, inverse, after, cq, n1, xs = call(
        functools.partial(self_kernel, n, shorts),
        (order, ranks, decoder_input, *xl, *xs, self_inward, self_outward, cross_query,
         norm_gains, norm_shifts),
        [low_rows, kept_shape, low_rows, inverses, wide_rows, low_rows, low_rows,
         ((n // 4, rows, width), LOW)],
        12,
        scratch=saved,
        smem=2,
        room=room,
        far_outs=(1,),
        sems=pairs + 1,
    )
    cross_kept, cmixed, cinverse, crossed, es = call(
        functools.partial(cross_kernel, n, shorts),
        (order, ranks, chain_breaks, encoder_output, *el, *es, cq, after, cross_memory,
         cross_outward),
        [kept_shape, low_rows, inverses, wide_rows, ((n // 4, rows, width), LOW)],
        11,
        scratch=saved,
        smem=3,
        room=room,
        far_outs=(0,),
        sems=pairs + 1,
    )
    half = chunks // 2
    layer_output, cross_grad, near, far, g_bias, small_feed = call(
        feed_kernel,
        (order, codes, crossed, output_cotangent, feed_up, feed_up_bias[None], feed_down,
         feed_down_bias[None], norm_gains, norm_shifts),
        [(decoder_input.shape, LOW), ((both, width), WIDE), ((half, tall, 2 * hidden), LOW),
         ((half, tall, 2 * hidden), LOW), ((1, hidden), WIDE), ((3, width), WIDE)],
        14,
        scratch=[low_rows, wide_rows, wide_rows, ((chunks, tall, 2 * hidden), LOW)],
        smem=2,
        room=room,
        far_outs=(2, 3),
        sems=2,
    )
    wide = [hidden, hidden]
    wide_rest = [hidden, hidden + 128]

    def shape(count, lanes):
        return (count, tall, lanes)

    roots = range(n // 4)
    part_shapes = [((rows, width), LOW)] * n
    part_shapes[1] = (((n // 4 + 1) * rows, width), LOW)
    feed_core = trade(far, "batch", 1)
    feed_near = near
    *e_parts, cross_dq, cross_dkv, cross_low = call(
        functools.partial(cross_back_kernel, n),
        (cross_grad, cmixed, cinverse, cq, cross_kept, cross_memory, cross_outward),
        part_shapes + [low_rows, pair_rows, low_rows],
        10,
        scratch=[low_rows, *loaded],
        room=room,
        far_ins=(4,),
        sems=3 * pairs,
    )
    self_grad, g_cross, small_cross = call(
        functools.partial(cross_sums_kernel, n),
        (order, encoder_output, *el, es, cross_grad, cross_low, cmixed, cross_dq, cross_dkv,
         after, n1, cross_query, norm_gains),
        [wide_rows, ((width, 4 * width), LOW), ((2, width), WIDE)],
        4,
        smem=1,
        room=room,
    )
    (a, a_send, b, b_send), _ = small_steps(
        [(add_core, (feed_near, feed_core), [shape(8, w) for w in wide for _ in "ks"]),
         (note, (small_cross,), [])]
    )
    a_got, b_got = trade(a_send, "batch", 2), trade(b_send, "batch", 4)
    e_got = [return_long(e_parts[d], n, d, True) for d in range(1, n)]
    *parts, own, near, far = call(
        functools.partial(self_back_kernel, n),
        (order, codes, decoder_input, *xl, xs, self_grad, mixed, inverse, q, kept, self_inward,
         self_outward, norm_gains, norm_shifts, small_feed, g_bias, small_cross, g_cross, a),
        [((rows, width), LOW)] * blocks
        + [((both, width), WIDE), (shape(half, sum(wide_rest)), LOW),
           (shape(half, sum(wide_rest)), LOW)],
        14,
        scratch=[(shape(chunks, sum(wide_rest)), LOW), low_rows, low_rows, pair_rows, *loaded],
        smem=2,
        room=room,
        far_ins=(n + 7,),
        far_outs=(blocks + 1, blocks + 2),
        sems=3 * pairs,
    )
    (a, a_send), (b, b_send) = small_steps(
        [(add_halves, (a, a_got, own), [shape(4, wide[0])] * 2),
         (add_halves, (b, b_got), [shape(4, wide[1])] * 2)]
    )
    a_got, b_got = trade(a_send, "batch", 4), trade(b_send, "batch", 2)
    ((e_long, *e_short),) = small_steps(
        [(add_returns, (tied(e_parts[0], a_send), e_parts[1], *e_got),
          [((rows, width), WIDE)] + [(rows, width)] * (n // 4))]
    )
    held = tied(parts[n - 1], e_short[0])
    for d in range(n - 2, 2, -1):
        held = parts[d] + hand_down(held, n, d + 1)
    long_got = hand_down(held, n, 3)
    feed, (a, a_send, b, b_send), (held,) = small_steps(
        [(add_to_pieces, (a, a_got, b, b_got), [shape(1, sum(wide))] * 4),
         (add_core, (near, trade(tied(far, e_short[0]), "batch", 1)),
          [shape(8, w) for w in wide_rest for _ in "ks"]),
         (add_all, (own, parts[2], long_got), [(rows, width)])]
    )
    a_got, b_got = trade(a_send, "batch", 2), trade(b_send, "batch", 4)
    (a, a_send), (b, b_send), (feed,) = small_steps(
        [(add_halves, (a, a_got), [shape(4, wide_rest[0])] * 2),
         (add_halves, (b, b_got), [shape(4, wide_rest[1])] * 2),
         (add_all, (own, feed[0], *to_tall(feed)), [shape(1, sum(wide))])]
    )
    feed = sharing.doubled(feed)
    a_got, b_got = trade(a_send, "batch", 4), trade(b_send, "batch", 2)
    rest, (fa, fb) = small_steps(
        [(add_to_pieces, (a, a_got, b, b_got), [shape(1, sum(wide_rest))] * 4),
         (lay, (feed, *to_tall([feed] * 4)), [shape(4, w) for w in wide])]
    )
    (rest,), (fa,), (fb,) = small_steps(
        [(add_all, (own, rest[0], *to_tall(rest)), [shape(1, sum(wide_rest))]),
         (join, (fa, trade(fa, "batch", 4)), [shape(8, wide[0])]),
         (join, (fb, trade(fb, "batch", 2)), [shape(8, wide[1])])]
    )
    rest = sharing.doubled(rest)
    (ra, rb), (feed,) = small_steps(
        [(lay, (rest, *to_tall([rest] * 4)), [shape(4, w) for w in wide_rest]),
         (beside, (fa, trade(fa, "batch", 2), fb, trade(fb, "batch", 4)),
          [shape(16, sum(wide))])]
    )
    ra_got, rb_got = trade(ra, "batch", 4), trade(rb, "batch", 2)
    held, *shorts = tied((held, *parts[n:]), ra)
    long_got = hand_down(held, n, 2)
    got = [return_short(shorts[k], n, k, 1) for k in roots]
    e_got = [return_short(tied(e_short[k], ra), n, k, 2) for k in roots]
    (ra,), (rb,), (held,), *shorts = small_steps(
        [(join, (ra, ra_got), [shape(8, wide_rest[0])]),
         (join, (rb, rb_got), [shape(8, wide_rest[1])]),
         (add_all, (own, parts[1], long_got), [(rows, width)])]
        + [(add_all, (own, parts[n + k], got[k]), [(rows, width)]) for k in roots]
        + [(add_all, (own, e_short[k], e_got[k]), [(rows, width)]) for k in roots]
    )
    shorts, e_short = shorts[: n // 4], return_short_rest([v for v, in shorts[n // 4 :]], n)
    ra_got, rb_got = trade(ra, "batch", 2), trade(rb, "batch", 4)
    feed_got = trade(tied(feed, ra), "batch", 1)
    long_got = hand_down(held, n, 1)
    got = [return_short(shorts[k][0], n, k, 2) for k in roots]
    s_up, s_down = call(
        functools.partial(unpack_feed_kernel, [(0, 2, 0, 0, 1), (0, 2, 1, hidden, hidden // width)]),
        (codes, feed, feed_got),
        [(feed_up.shape, WIDE), (feed_down.shape, WIDE)],
        6,
        smem=1,
        room=room,
    )
    (rest,), _, *shorts = small_steps(
        [(beside, (ra, ra_got, rb, rb_got), [shape(16, sum(wide_rest))]),
         (note, (s_down[:8, :128], long_got), [])]
        + [(add_all, (own, shorts[k][0], got[k]), [(rows, width)]) for k in roots]
    )
    shorts = return_short_rest([v for v, in shorts], n)
    rest_got = trade(rest, "batch", 1)
    input_gradient, encoder_gradient = call(
        functools.partial(last_kernel, n),
        (order, ranks, decoder_input, self_grad, own, norm_gains, parts[0], long_got, e_long,
         *shorts, *e_short),
        [(decoder_input.shape, WIDE), (decoder_input.shape, WIDE)],
        3,
        smem=2,
        room=room,
    )
    at = hidden
    places = [(0, 2, 0, 0, 1), (0, 2, 0, 2 * width, 1), (0, 2, 0, 3 * width, 1),
              (0, 2, 1, at, 1), (0, 2, 1, at + 3 * width, 1), (0, 2, 1, at + 4 * width, 1)]
    s_cm, s_cq, s_cout, s_in, s_out, up_bias, down_bias, gains, shifts = call(
        functools.partial(unpack_rest_kernel, places),
        (codes, rest, rest_got),
        [(s, WIDE) for s in (cross_memory.shape, cross_query.shape, cross_outward.shape,
                             self_inward.shape, self_outward.shape, (1, hidden), (1, width),
                             norm_gains.shape, norm_shifts.shape)],
        5,
        scratch=[((width, 128), WIDE)],
        smem=1,
        room=room,
    )
    return (
        layer_output, input_gradient, encoder_gradient, s_in, s_out, s_cq, s_cm, s_cout,
        s_up, up_bias[0], s_down, down_bias[0], gains, shifts,
    )


def solution(mesh):
    blocked = P("batch", "blk", None)
    placed = (blocked, blocked, P("batch"), P("batch", None)) + (P(),) * 11 + (blocked,)
    return jax.shard_map(
        on_device,
        mesh=mesh,
        in_specs=placed,
        out_specs=(blocked,) * 3 + (P(),) * 11,
        check_vma=False,
    )
```

```python
import functools

import jax
import jax.numpy as jnp
from jax import lax
from jax.experimental import pallas as pl
from jax.experimental.pallas import tpu as pltpu
from jax.sharding import PartitionSpec as P

HEAD = 64
PAIR = 2 * HEAD
EPSILON = 1e-05
FAR = 1e30
LOW = jnp.bfloat16
WIDE = jnp.float32


def contract(left, right, a, b):
    return lax.dot_general(left, right, (((a,), (b,)), ((), ())), preferred_element_type=WIDE)


def nn(left, right):
    return contract(left, right, 1, 0)


def nt(left, right):
    return contract(left, right, 1, 1)


def tn(left, right):
    return contract(left, right, 0, 0)


def standard(values):
    center = values - jnp.mean(values, axis=-1, keepdims=True)
    spread = jnp.mean(center * center, axis=-1, keepdims=True)
    inverse = lax.rsqrt(spread + EPSILON)
    return center * inverse, inverse


def norm_back(values, gain, upstream):
    unit, inverse = standard(values)
    m = upstream * gain
    grad = inverse * (
        m
        - jnp.mean(m, axis=-1, keepdims=True)
        - unit * jnp.mean(m * unit, axis=-1, keepdims=True)
    )
    return grad, jnp.sum(upstream * unit, axis=0), jnp.sum(upstream, axis=0)


def gelu_pair(x):
    z = jnp.abs(x) * 0.7071067811865476
    t = 1.0 / (1.0 + 0.5 * z)
    poly = 0.17087277
    for c in (
        -0.82215223,
        1.48851587,
        -1.13520398,
        0.27886807,
        -0.18628806,
        0.09678418,
        0.37409196,
        1.00002368,
        -1.26551223,
    ):
        poly = poly * t + c
    bell = jnp.exp(-z * z)
    tail = 0.5 * t * jnp.exp(poly) * bell
    share = jnp.where(x >= 0, 1.0 - tail, tail)
    return x * share, share + x * bell * 0.3989422804014327


def by_head(pair_rows):
    lane = lax.broadcasted_iota(jnp.int32, pair_rows.shape, 1)
    zero = jnp.zeros_like(pair_rows)
    return jnp.concatenate(
        [jnp.where(lane < HEAD, pair_rows, zero), jnp.where(lane >= HEAD, pair_rows, zero)], axis=0
    )


def own_parts(both):
    rows = both.shape[1] // 2
    return jnp.concatenate([both[:HEAD, :rows], both[HEAD:, rows:]], axis=0)


def columns(place, wide):
    return pl.ds(pl.multiple_of(place * wide, wide), wide)


def attend(q_ref, kv_ref, p_ref, low_ref, inverse_ref, plan, mask, done):
    rows = q_ref.shape[0] // 2
    width = q_ref.shape[1]

    @pl.loop(0, width // PAIR)
    def _(pair):
        lanes = columns(pair, PAIR)
        values = columns(width // PAIR + pair, PAIR)
        spot = columns(pair, 2 * rows)
        for seq, blocks in enumerate(plan):
            mine = slice(seq * rows, (seq + 1) * rows)
            queries = by_head(q_ref[mine, lanes])
            scores, tops = [], []
            for block in blocks:
                s = nt(kv_ref[block * rows : (block + 1) * rows, lanes], queries)
                s, far = mask(block, s)
                scores.append((s, far))
                tops.append(jnp.max(s, axis=0, keepdims=True) - far)
            top = functools.reduce(jnp.maximum, tops)
            total = jnp.zeros_like(top)
            mixed = jnp.zeros((PAIR, 2 * rows), WIDE)
            for block, (s, far) in zip(blocks, scores):
                at = slice(block * rows, (block + 1) * rows)
                p = jnp.exp(s - (top + far))
                total = total + jnp.sum(p, axis=0, keepdims=True)
                p = p.astype(LOW)
                p_ref[at, spot] = p
                mixed = mixed + tn(kv_ref[at, values], p)
            inverse = 1.0 / total
            low_ref[mine, lanes] = own_parts(mixed * inverse).T.astype(LOW)
            inverse_ref[pl.ds(2 * pair + seq, 1), :] = inverse
        done(pair)


def attend_back(up, low_ref, inverse_ref, q_ref, kv_ref, p_ref, dq_ref, dkv_ref, plan, ready, done):
    rows = q_ref.shape[0] // 2
    width = q_ref.shape[1]
    scale = HEAD ** (-0.5)

    @pl.loop(0, width // PAIR)
    def _(pair):
        lanes = columns(pair, PAIR)
        values = columns(width // PAIR + pair, PAIR)
        slot = lax.rem(pair, 2)
        ready(pair)
        for seq, blocks in enumerate(plan):
            mine = slice(seq * rows, (seq + 1) * rows)
            queries = by_head(q_ref[mine, lanes])
            inverse = inverse_ref[pl.ds(2 * pair + seq, 1), :]
            scaled = up[mine, lanes].astype(WIDE) * own_parts(jnp.broadcast_to(inverse, (PAIR, 2 * rows))).T
            inner = (scaled * low_ref[mine, lanes].astype(WIDE)).T
            offset = jnp.concatenate(
                [
                    jnp.sum(inner[:HEAD], axis=0, keepdims=True),
                    jnp.sum(inner[HEAD:], axis=0, keepdims=True),
                ],
                axis=1,
            )
            upper = by_head(scaled.astype(LOW))
            dq = jnp.zeros((PAIR, 2 * rows), WIDE)
            for block in blocks:
                at = slice(block * rows, (block + 1) * rows)
                p = p_ref[slot, at, :]
                dp = nt(kv_ref[at, values], upper)
                ds = (p.astype(WIDE) * (dp - offset)).astype(LOW)
                dkv_ref[at, values] = nn(p, upper).astype(LOW)
                dkv_ref[at, lanes] = nn(ds, queries).astype(LOW)
                dq = dq + tn(kv_ref[at, lanes], ds)
            dq_ref[mine, lanes] = (own_parts(dq).T * scale).astype(LOW)
        done(pair)


def saves(kv, p, kept, sems):
    rows, width = slice(0, kv.shape[0]), kv.shape[1]
    wide = 2 * PAIR * p.shape[1] // width

    def p_save(pair):
        at = pl.ds(pl.multiple_of(width + pair * wide, PAIR), wide)
        return pltpu.make_async_copy(p.at[:, columns(pair, wide)], kept.at[rows, at], sems.at[pair])

    pairs = width // (2 * PAIR)
    return pltpu.make_async_copy(kv, kept.at[rows, :width], sems.at[pairs]), p_save


def plan_of(n):
    return (tuple(range(n)), tuple(range(n, n + n // 4)))


def add_terms(out, refs, terms):
    for j in range(out.shape[0]):
        total = refs[j * terms][...]
        for ref in refs[j * terms + 1 : (j + 1) * terms]:
            total = total + ref[...]
        out[j] = total


def pick_kernel(lengths, x, enc, x_long, e_long, *shorts):
    rows = x_long.shape[0]
    long = jnp.where(lengths[1] > lengths[0], 1, 0)
    x_long[...] = x[long]
    e_long[...] = enc[long]
    for root, ref in enumerate(shorts):
        share = (lax.axis_index("blk") == root).astype(jnp.int32).astype(WIDE)
        ref[:rows] = (x[1 - long].astype(WIDE) * share).astype(LOW)
        ref[rows:] = (enc[1 - long].astype(WIDE) * share).astype(LOW)


def self_kernel(n, terms, order, rank, x, *refs):
    xl, refs = refs[: n - 1], refs[n - 1 :]
    shorts, refs = refs[: terms * (n // 4)], refs[terms * (n // 4) :]
    (
        w_in, w_out, w_cq, gains, shifts,
        q, kept, mixed, inverse, after, cq, n1, xs, kv, p, sems,
    ) = refs
    pairs = q.shape[1] // PAIR
    kv_save, p_save = saves(kv, p, kept, sems)
    add_terms(xs, shorts, terms)
    rows, width = x.shape[1:]
    r = rank[0]

    def first_norm(v):
        return (standard(v.astype(WIDE))[0] * gains[0:1] + shifts[0:1]).astype(LOW)

    def keys(v, block):
        kv[block * rows : (block + 1) * rows, :] = nn(first_norm(v), w_in[:, width:]).astype(LOW)

    mine = jnp.concatenate([x[order[0]], x[order[1]]], axis=0)
    normed = first_norm(mine)
    kv[0:rows, :] = nn(normed[:rows], w_in[:, width:]).astype(LOW)
    for d in range(1, n):
        keys(xl[d - 1][...], d)
    for j in range(n // 4):
        keys(xs[j], n + j)
    kv_save.start()
    q[...] = nn(normed, w_in[:, :width]).astype(LOW) * HEAD ** (-0.5)

    def mask(block, s):
        if 0 < block < n:
            return s, jnp.where(r >= block, 0.0, FAR)
        key = lax.broadcasted_iota(jnp.int32, s.shape, 0)
        query = lax.broadcasted_iota(jnp.int32, s.shape, 1)
        query = jnp.where(query >= rows, query - rows, query)
        if block >= n:
            query = query + (r - (block - n)) * rows
        return jnp.where(key <= query, s, -FAR), 0.0

    attend(q, kv, p, mixed, inverse, plan_of(n), mask, lambda pair: p_save(pair).start())
    total = mine.astype(WIDE) + nn(mixed[...], w_out[...])
    after[...] = total
    second = (standard(total)[0] * gains[1:2] + shifts[1:2]).astype(LOW)
    n1[...] = second
    cq[...] = nn(second, w_cq[...]).astype(LOW) * HEAD ** (-0.5)
    kv_save.wait()
    for pair in range(pairs):
        p_save(pair).wait()


def cross_kernel(n, terms, order, rank, breaks, enc, *refs):
    el, refs = refs[: n - 1], refs[n - 1 :]
    shorts, refs = refs[: terms * (n // 4)], refs[terms * (n // 4) :]
    cq, after, w_cm, w_out, kept, mixed, inverse, crossed, es, kv, p, sems = refs
    pairs = cq.shape[1] // PAIR
    kv_save, p_save = saves(kv, p, kept, sems)
    add_terms(es, shorts, terms)
    rows, width = enc.shape[1:]
    r = rank[0]
    kv[0:rows, :] = nn(enc[order[0]], w_cm[...]).astype(LOW)
    for d in range(1, n):
        kv[d * rows : (d + 1) * rows, :] = nn(el[d - 1][...], w_cm[...]).astype(LOW)
    for j in range(n // 4):
        kv[(n + j) * rows : (n + j + 1) * rows, :] = nn(es[j], w_cm[...]).astype(LOW)

    kv_save.start()

    def mask(block, s):
        key = lax.broadcasted_iota(jnp.int32, s.shape, 0)
        if block < n:
            first = lax.rem(r - block + n, n) * rows
            which = order[0]
        else:
            first = (block - n) * rows
            which = order[1]
        shut = key == breaks[which, 0] - first
        for i in range(1, breaks.shape[1]):
            shut = shut | (key == breaks[which, i] - first)
        return jnp.where(shut, -FAR, s), 0.0

    attend(cq, kv, p, mixed, inverse, plan_of(n), mask, lambda pair: p_save(pair).start())
    crossed[...] = after[...] + nn(mixed[...], w_out[...])
    kv_save.wait()
    for pair in range(pairs):
        p_save(pair).wait()


def spread(sums, code, value, lane):
    tall = sums.shape[1]
    for k in range(sums.shape[0]):
        part = value[k * tall : (k + 1) * tall, :]
        sums[k ^ code, :, lane : lane + value.shape[1]] = part


def feed_kernel(
    order, codes, crossed, cot, w_up, b_up, w_down, b_down, gains, shifts,
    out, grad, near, far, g_bias, g_small, third, total, back, sums, sems,
):
    rows, width = cot.shape[1:]
    hidden = w_up.shape[1]
    half, tall = near.shape[:2]
    deep = hidden // (2 * half)
    third[...] = (standard(crossed[...])[0] * gains[2:3] + shifts[2:3]).astype(LOW)
    up_low = jnp.concatenate([cot[order[0]], cot[order[1]]], axis=0)
    total[...] = crossed[...] + b_down[...].astype(WIDE)
    back[...] = jnp.zeros_like(back)

    @pl.loop(0, hidden // width)
    def _(c):
        at = columns(c, width)
        rising = nn(third[...], w_up[:, at]) + b_up[:, at].astype(WIDE)
        active, slope = gelu_pair(rising)
        active = active.astype(LOW)
        total[...] += nn(active, w_down[at, :])
        rising_grad = nt(up_low, w_down[at, :]) * slope
        g_bias[:, at] = jnp.sum(rising_grad, axis=0, keepdims=True)
        rising_grad = rising_grad.astype(LOW)
        back[...] += nt(rising_grad, w_up[:, at])
        g_up = tn(third[...], rising_grad).astype(LOW)
        for k in range(2 * half):
            sums[k ^ codes[0], :, at] = g_up[k * tall : (k + 1) * tall]
        g_down = tn(active, up_low).astype(LOW)
        for k in range(width // deep):
            for i in range(deep // tall):
                first = k * deep + i * tall
                lanes = slice(hidden + i * width, hidden + (i + 1) * width)
                sums[(c * (width // deep) + k) ^ codes[1], :, lanes] = g_down[first : first + tall]

    saves = [
        pltpu.make_async_copy(sums.at[:half], near, sems.at[0]),
        pltpu.make_async_copy(sums.at[half:], far, sems.at[1]),
    ]
    for save in saves:
        save.start()
    low = total[...].astype(LOW)
    out[order[0]] = low[:rows]
    out[order[1]] = low[rows:]
    upward = up_low.astype(WIDE)
    inner, gain, shift = norm_back(crossed[...], gains[2:3], back[...])
    grad[...] = upward + inner
    g_small[0, :] = jnp.sum(upward, axis=0)
    g_small[1, :] = gain
    g_small[2, :] = shift
    for save in saves:
        save.wait()


def loads(kept, kv, p, sems):
    rows, width, wide = slice(0, kv.shape[0]), kv.shape[1], p.shape[2]
    pairs = width // (2 * PAIR)

    def p_copy(pair):
        at = pl.ds(pl.multiple_of(width + pair * wide, PAIR), wide)
        return pltpu.make_async_copy(kept.at[rows, at], p.at[lax.rem(pair, 2)], sems.at[pair])

    def kv_copies(pair):
        return [
            pltpu.make_async_copy(
                kept.at[rows, columns(i, PAIR)], kv.at[:, columns(i, PAIR)], sems.at[pairs + i]
            )
            for i in (pair, pairs + pair)
        ]

    for pair in range(pairs):
        if pair < 2:
            p_copy(pair).start()
        for copy in kv_copies(pair):
            copy.start()

    def ready(pair):
        for copy in (p_copy(pair), *kv_copies(pair)):
            copy.wait()

    def done(pair):
        @pl.when(pair + 2 < pairs)
        def _():
            p_copy(pair + 2).start()

    return ready, done


def put_part(parts, n, b, value):
    rows = value.shape[0]
    if b < len(parts):
        parts[b][:rows, :] = value
    else:
        parts[1][(b - n + 1) * rows : (b - n + 2) * rows, :] = value


def cross_back_kernel(n, grad, mixed, inverse, cq, kept, w_cm, w_cout, *refs):
    parts, (dq, dkv, low, up, kv, p, sems) = refs[:-7], refs[-7:]
    ready, done = loads(kept, kv, p, sems)
    rows = parts[0].shape[0]
    low[...] = grad[...].astype(LOW)
    up[...] = nt(low[...], w_cout[...]).astype(LOW)
    attend_back(up, mixed, inverse, cq, kv, p, dq, dkv, plan_of(n), ready, done)
    for b in range(n + n // 4):
        put_part(parts, n, b, nt(dkv[b * rows : (b + 1) * rows, :], w_cm[...]).astype(LOW))


def cross_sums_kernel(n, order, enc, *refs):
    el, es, refs = refs[: n - 1], refs[n - 1], refs[n:]
    grad, low, mixed, dq, dkv, after, n1, w_cq, gains, self_grad, g_cross, g_small = refs
    rows, width = enc.shape[1:]
    g_cross[:, 3 * width :] = tn(mixed[...], low[...]).astype(LOW)
    g_cross[:, 2 * width : 3 * width] = tn(n1[...], dq[...]).astype(LOW)
    total = tn(enc[order[0]], dkv[0:rows, :])
    for d in range(1, n):
        total = total + tn(el[d - 1][...], dkv[d * rows : (d + 1) * rows, :])
    for j in range(n // 4):
        total = total + tn(es[j], dkv[(n + j) * rows : (n + j + 1) * rows, :])
    g_cross[:, : 2 * width] = total.astype(LOW)
    inner, gain, shift = norm_back(after[...], gains[1:2], nt(dq[...], w_cq[...]))
    self_grad[...] = grad[...] + inner
    g_small[0, :] = gain
    g_small[1, :] = shift


def self_back_kernel(n, order, codes, x, *refs):
    xl, refs = refs[: n - 1], refs[n - 1 :]
    (
        xs, self_grad, mixed, inverse, q, kept, w_in, w_out, gains, shifts, small_feed, g_bias,
        small_cross, g_cross, _,
    ) = refs[:15]
    parts, (own, near, far, sums, dq, up, dkv, kv, p, sems) = refs[15:-10], refs[-10:]
    ready, done = loads(kept, kv, p, sems)
    rows, width = x.shape[1:]
    low = self_grad[...].astype(LOW)
    up[...] = nt(low, w_out[...]).astype(LOW)
    attend_back(up, mixed, inverse, q, kv, p, dq, dkv, plan_of(n), ready, done)
    mine = jnp.concatenate([x[order[0]], x[order[1]]], axis=0).astype(WIDE)
    unit = standard(mine)[0]
    normed = (unit * gains[0:1] + shifts[0:1]).astype(LOW)
    g_out = tn(mixed[...], low).astype(LOW)
    g_query = tn(normed, dq[...]).astype(LOW)
    mine = nt(dq[...], w_in[:, :width])
    own[...] = mine
    gain = jnp.sum(mine * unit, axis=0)
    shift = jnp.sum(mine, axis=0)
    total = None
    for b in range(n + n // 4):
        if b == 0:
            key_unit, key_low = unit[:rows], normed[:rows]
        else:
            v = xl[b - 1][...] if b < n else xs[b - n]
            key_unit = standard(v.astype(WIDE))[0]
            key_low = (key_unit * gains[0:1] + shifts[0:1]).astype(LOW)
        pairs = dkv[b * rows : (b + 1) * rows, :]
        term = tn(key_low, pairs)
        total = term if total is None else total + term
        back = nt(pairs, w_in[:, width:])
        put_part(parts, n, b, back.astype(LOW))
        gain = gain + jnp.sum(back * key_unit, axis=0)
        shift = shift + jnp.sum(back, axis=0)
    small = [gain[None], small_cross[0:1], small_feed[1:2], shift[None], small_cross[1:2],
             small_feed[2:3], small_feed[0:1], g_bias[...]]
    small = [v[:, i : i + 128] for v in small for i in range(0, v.shape[1], 128)]
    small.append(jnp.zeros((width - len(small), 128), WIDE))
    small = jnp.concatenate(small, axis=0).astype(LOW)
    spread(sums, codes[0], g_cross, 0)
    spread(sums, codes[1], g_query, 4 * width)
    spread(sums, codes[1], total.astype(LOW), 5 * width)
    spread(sums, codes[1], g_out, 7 * width)
    spread(sums, codes[1], small, 8 * width)
    half = sums.shape[0] // 2
    saves = [
        pltpu.make_async_copy(sums.at[:half], near, sems.at[0]),
        pltpu.make_async_copy(sums.at[half:], far, sems.at[1]),
    ]
    for save in saves:
        save.start()
    for save in saves:
        save.wait()


def unpack(plan, codes, pieces, outs):
    for out, (at, count, which, lane, side) in zip(outs, plan):
        wide = out.shape[1]
        depth, tall = pieces[at].shape[:2]
        for k in range(count * depth):
            first = (codes[which] ^ k) * (tall * side)
            for i in range(side):
                start = pl.multiple_of(first + i * tall, tall)
                lanes = slice(lane + i * wide, lane + (i + 1) * wide)
                out[pl.ds(start, tall), :] = pieces[at + k // depth][k % depth, :, lanes].astype(WIDE)


def unpack_feed_kernel(plan, codes, *refs):
    unpack(plan, codes, refs[: -len(plan)], refs[-len(plan) :])


def unpack_rest_kernel(plan, codes, *refs):
    *refs, up_bias, down_bias, gains, shifts, small = refs
    count = len(plan) - 1
    unpack(plan, codes, refs[:-count], refs[-count:] + [small])
    at = 0
    for out, count in ((gains, 3), (shifts, 3), (down_bias, 1), (up_bias, 1)):
        for i in range(count):
            across = out.shape[1] // 128
            row = [small[at + j : at + j + 1, :] for j in range(across)]
            out[i : i + 1, :] = jnp.concatenate(row, axis=1)
            at += across


def last_kernel(n, order, rank, x, self_grad, own, gains, part, part_got, e_long, *refs):
    shorts, e_shorts, (grad, e_grad) = refs[: n // 4], refs[n // 4 : n // 2], refs[-2:]
    rows = x.shape[1]

    def mine(helds):
        total = jnp.zeros(part.shape, WIDE)
        for root, held in enumerate(helds):
            total = jnp.where(rank[0] == root, held[...].astype(WIDE), total)
        return total

    long_up = own[:rows] + part[...].astype(WIDE) + part_got[...].astype(WIDE)
    short_up = own[rows:] + mine(shorts)
    for which, up, at in ((order[0], long_up, 0), (order[1], short_up, rows)):
        inner, _, _ = norm_back(x[which].astype(WIDE), gains[0:1], up)
        grad[which] = self_grad[at : at + rows] + inner
    e_grad[order[0]] = e_long[...]
    e_grad[order[1]] = mine(e_shorts)


def add_core(near, got, *outs):
    at = 0
    half = near.shape[0] // 2
    for keep, send in zip(outs[::2], outs[1::2]):
        lanes = slice(at, at + keep.shape[2])
        keep[...] = near[:half, :, lanes] + got[:half, :, lanes]
        send[...] = near[half:, :, lanes] + got[half:, :, lanes]
        at = lanes.stop


def add_returns(own, near, near_got, *refs):
    rows = own.shape[0]
    count = near.shape[0] // rows
    total = own[...].astype(WIDE) + near_got[:rows, :].astype(WIDE)
    for ref in refs[:-count]:
        total = total + ref[...].astype(WIDE)
    refs[-count][...] = total
    for k in range(1, count):
        at = slice(k * rows, (k + 1) * rows)
        refs[k - count][...] = near[at, :] + near_got[at, :]


def add_halves(keep, got, *outs):
    half = keep.shape[0] // 2
    outs[-2][...] = keep[:half] + got[:half]
    outs[-1][...] = keep[half:] + got[half:]


def add_to_pieces(a, got_a, b, got_b, *outs):
    wide = a.shape[2]
    for k, out in enumerate(outs[-a.shape[0] :]):
        out[:, :, :wide] = a[k : k + 1] + got_a[k : k + 1]
        out[:, :, wide:] = b[k : k + 1] + got_b[k : k + 1]


def note(*refs):
    pass


def add_all(_, *refs):
    *parts, out = refs
    total = parts[0][...].astype(WIDE)
    for part in parts[1:]:
        total = total + part[...].astype(WIDE)
    out[...] = total.astype(out.dtype)


def lay_whole(_, *refs):
    for k, ref in enumerate(refs[:-1]):
        refs[-1][k : k + 1] = ref[...]


def lay(*refs):
    *parts, a, b = refs
    wide = a.shape[2]
    for k, part in enumerate(parts):
        a[k : k + 1] = part[:, :, :wide]
        b[k : k + 1] = part[:, :, wide:]


def join(a, b, out):
    out[: a.shape[0]] = a[...]
    out[a.shape[0] :] = b[...]


def beside(a, got_a, b, got_b, out):
    half, _, wide = a.shape
    out[:half, :, :wide] = a[...]
    out[half:, :, :wide] = got_a[...]
    out[:half, :, wide:] = b[...]
    out[half:, :, wide:] = got_b[...]


def steps_kernel(steps, *refs):
    refs = list(refs)
    at_in, at_out = 0, sum(count for _, count, _ in steps)
    for kernel, ins, outs in steps:
        kernel(*refs[at_in : at_in + ins], *refs[at_out : at_out + outs])
        at_in += ins
        at_out += outs


def call(kernel, ins, outs, us, scratch=(), smem=0, room=62, far_ins=(), far_outs=(), sems=0):
    vmem = pl.BlockSpec(memory_space=pltpu.VMEM)
    far = pl.BlockSpec(memory_space=pltpu.HBM)
    in_specs = [vmem] * len(ins)
    in_specs[:smem] = [pl.BlockSpec(memory_space=pltpu.SMEM)] * smem
    for i in far_ins:
        in_specs[i] = far
    scratch_shapes = [pltpu.VMEM(s, t) for s, t in scratch]
    if sems:
        scratch_shapes.append(pltpu.SemaphoreType.DMA((sems,)))
    return pl.pallas_call(
        kernel,
        out_shape=[jax.ShapeDtypeStruct(s, t) for s, t in outs],
        in_specs=in_specs,
        out_specs=[far if i in far_outs else vmem for i in range(len(outs))],
        scratch_shapes=scratch_shapes,
        compiler_params=pltpu.CompilerParams(vmem_limit_bytes=room << 20),
        cost_estimate=pl.CostEstimate(flops=us * 10**9, bytes_accessed=0, transcendentals=0),
    )(*ins)


def small_steps(steps):
    outs = call(
        functools.partial(steps_kernel, [(k, len(i), len(o)) for k, i, o in steps]),
        [v for _, ins, _ in steps for v in ins],
        [o if isinstance(o[0], tuple) else (o, LOW) for _, _, outs in steps for o in outs],
        2,
        room=20,
    )
    got = []
    for _, _, shapes in steps:
        got.append(outs[: len(shapes)])
        outs = outs[len(shapes) :]
    return got


def send_long(block, n, wrap):
    got = []
    for d in range(1, n):
        pairs = [(i, (i + d) % n) for i in range(n) if wrap or i + d < n]
        got.append(lax.ppermute(block, "blk", pairs))
    return got


def return_long(block, n, distance, wrap):
    pairs = [(i, (i - distance) % n) for i in range(n) if wrap or i >= distance]
    return lax.ppermute(block, "blk", pairs)


def hand_down(held, n, distance):
    return lax.ppermute(held, "blk", [(i, i - 1) for i in range(distance, n)])


def return_short(held, n, root, distance):
    pairs = [((root + k + distance) % n, (root + k) % n) for k in range(0, n, 2 * distance)]
    return lax.ppermute(held, "blk", pairs)


def return_short_rest(helds, n):
    got = []
    for root, held in enumerate(helds):
        d = 4
        while d < n:
            held = held + return_short(held, n, root, d)
            d *= 2
        got.append(held)
    return got


def send_short_first(shorts, n):
    return [
        [held, lax.ppermute(held, "blk", [(root, (root + n // 2) % n)])]
        for root, held in enumerate(shorts)
    ]


def send_short_rest(terms, n):
    for root in range(n // 4):
        d = n // 4
        while d:
            pairs = [((root + k) % n, (root + k + d) % n) for k in range(0, n, 2 * d)]
            held = functools.reduce(jnp.add, terms[root])
            terms[root].append(lax.ppermute(held, "blk", pairs))
            d //= 2
    return [v for several in terms for v in several]


def tied(value, *others):
    return lax.optimization_barrier((value, others))[0]


def trade(v, axis, distance):
    return lax.ppermute(v, axis, [(i, i ^ distance) for i in range(lax.axis_size(axis))])


class Sharing:
    def __init__(self, batch, n):
        self.rest = [("batch", d) for d in (8, 16, 32) if d < batch]
        self.rest += [("blk", d) for d in (4, 8, 16, 32) if d < n]
        self.chunks = 32

    def codes(self):
        codes = []
        for first, second in ((2, 4), (4, 2)):
            code = jnp.int32(0)
            for axis, distance in (("batch", 1), ("batch", first), ("batch", second), ("blk", 2),
                                   ("blk", 1)):
                code = 2 * code + (lax.axis_index(axis) // distance) % 2
            codes.append(code.astype(jnp.int32))
        return jnp.stack(codes)

    def doubled(self, v):
        for axis, distance in self.rest:
            v = v + trade(v, axis, distance)
        return v


def to_tall(pieces):
    return [trade(v, "blk", j) for j, v in enumerate(pieces) if j]


def on_device(
    decoder_input, encoder_output, sequence_lengths, chain_breaks,
    self_inward, self_outward, cross_query, cross_memory, cross_outward,
    feed_up, feed_up_bias, feed_down, feed_down_bias, norm_gains, norm_shifts,
    output_cotangent,
):
    sequences, rows, width = decoder_input.shape
    hidden = feed_up.shape[1]
    n = lax.axis_size("blk")
    rank = lax.axis_index("blk")
    ranks = rank.astype(jnp.int32)[None]
    longest = (sequence_lengths[1] > sequence_lengths[0]).astype(jnp.int32)
    order = jnp.stack([longest, 1 - longest])
    both = 2 * rows
    nk = (n + n // 4) * rows
    pairs = width // PAIR

    sharing = Sharing(lax.axis_size("batch"), n)
    codes = sharing.codes()
    chunks = sharing.chunks
    tall = width // chunks
    blocks = nk // rows

    room = 62 if n > 4 else 22
    block = ((rows, width), LOW)
    x_long, e_long, *shorts = call(
        pick_kernel,
        (sequence_lengths, decoder_input, encoder_output),
        [block, block] + [((both, width), LOW)] * (n // 4),
        1,
        smem=1,
        room=60,
    )
    firsts = send_short_first(shorts, n)
    xl = send_long(x_long, n, False)
    xs = send_short_rest([[v[:rows] for v in terms] for terms in firsts], n)
    shorts = len(xs) // (n // 4)
    e_long = tied(e_long, *[terms[1] for terms in firsts])
    es = send_short_rest([[tied(v[rows:], *xl) for v in terms] for terms in firsts], n)
    el = send_long(e_long, n, True)

    pair_rows = ((nk, 2 * width), LOW)
    saved = [pair_rows, ((nk, pairs * both), LOW)]
    loaded = [pair_rows, ((2, nk, both), LOW)]
    kept_shape = ((nk * (9 if n == 4 else 1), 2 * width + pairs * both), LOW)
    inverses = ((2 * pairs, both), WIDE)
    low_rows, wide_rows = ((both, width), LOW), ((both, width), WIDE)
    q, kept, mixed, inverse, after, cq, n1, xs = call(
        functools.partial(self_kernel, n, shorts),
        (order, ranks, decoder_input, *xl, *xs, self_inward, self_outward, cross_query,
         norm_gains, norm_shifts),
        [low_rows, kept_shape, low_rows, inverses, wide_rows, low_rows, low_rows,
         ((n // 4, rows, width), LOW)],
        12,
        scratch=saved,
        smem=2,
        room=room,
        far_outs=(1,),
        sems=pairs + 1,
    )
    cross_kept, cmixed, cinverse, crossed, es = call(
        functools.partial(cross_kernel, n, shorts),
        (order, ranks, chain_breaks, encoder_output, *el, *es, cq, after, cross_memory,
         cross_outward),
        [kept_shape, low_rows, inverses, wide_rows, ((n // 4, rows, width), LOW)],
        11,
        scratch=saved,
        smem=3,
        room=room,
        far_outs=(0,),
        sems=pairs + 1,
    )
    half = chunks // 2
    layer_output, cross_grad, near, far, g_bias, small_feed = call(
        feed_kernel,
        (order, codes, crossed, output_cotangent, feed_up, feed_up_bias[None], feed_down,
         feed_down_bias[None], norm_gains, norm_shifts),
        [(decoder_input.shape, LOW), ((both, width), WIDE), ((half, tall, 2 * hidden), LOW),
         ((half, tall, 2 * hidden), LOW), ((1, hidden), WIDE), ((3, width), WIDE)],
        14,
        scratch=[low_rows, wide_rows, wide_rows, ((chunks, tall, 2 * hidden), LOW)],
        smem=2,
        room=room,
        far_outs=(2, 3),
        sems=2,
    )
    wide = [hidden, hidden]
    wide_rest = [hidden, hidden + 128]

    def shape(count, lanes):
        return (count, tall, lanes)

    roots = range(n // 4)
    part_shapes = [((rows, width), LOW)] * n
    part_shapes[1] = (((n // 4 + 1) * rows, width), LOW)
    feed_core = trade(far, "batch", 1)
    feed_near = near
    *e_parts, cross_dq, cross_dkv, cross_low = call(
        functools.partial(cross_back_kernel, n),
        (cross_grad, cmixed, cinverse, cq, cross_kept, cross_memory, cross_outward),
        part_shapes + [low_rows, pair_rows, low_rows],
        10,
        scratch=[low_rows, *loaded],
        room=room,
        far_ins=(4,),
        sems=3 * pairs,
    )
    self_grad, g_cross, small_cross = call(
        functools.partial(cross_sums_kernel, n),
        (order, encoder_output, *el, es, cross_grad, cross_low, cmixed, cross_dq, cross_dkv,
         after, n1, cross_query, norm_gains),
        [wide_rows, ((width, 4 * width), LOW), ((2, width), WIDE)],
        4,
        smem=1,
        room=room,
    )
    (a, a_send, b, b_send), _ = small_steps(
        [(add_core, (feed_near, feed_core), [shape(8, w) for w in wide for _ in "ks"]),
         (note, (small_cross,), [])]
    )
    a_got, b_got = trade(a_send, "batch", 2), trade(b_send, "batch", 4)
    e_got = [return_long(e_parts[d], n, d, True) for d in range(1, n)]
    *parts, own, near, far = call(
        functools.partial(self_back_kernel, n),
        (order, codes, decoder_input, *xl, xs, self_grad, mixed, inverse, q, kept, self_inward,
         self_outward, norm_gains, norm_shifts, small_feed, g_bias, small_cross, g_cross, a),
        [((rows, width), LOW)] * blocks
        + [((both, width), WIDE), (shape(half, sum(wide_rest)), LOW),
           (shape(half, sum(wide_rest)), LOW)],
        14,
        scratch=[(shape(chunks, sum(wide_rest)), LOW), low_rows, low_rows, pair_rows, *loaded],
        smem=2,
        room=room,
        far_ins=(n + 7,),
        far_outs=(blocks + 1, blocks + 2),
        sems=3 * pairs,
    )
    (a, a_send), (b, b_send) = small_steps(
        [(add_halves, (a, a_got, own), [shape(4, wide[0])] * 2),
         (add_halves, (b, b_got), [shape(4, wide[1])] * 2)]
    )
    a_got, b_got = trade(a_send, "batch", 4), trade(b_send, "batch", 2)
    ((e_long, *e_short),) = small_steps(
        [(add_returns, (tied(e_parts[0], a_send), e_parts[1], *e_got),
          [((rows, width), WIDE)] + [(rows, width)] * (n // 4))]
    )
    held = tied(parts[n - 1], e_short[0])
    for d in range(n - 2, 2, -1):
        held = parts[d] + hand_down(held, n, d + 1)
    long_got = hand_down(held, n, 3)
    feed, (a, a_send, b, b_send), (held,) = small_steps(
        [(add_to_pieces, (a, a_got, b, b_got), [shape(1, sum(wide))] * 4),
         (add_core, (near, trade(tied(far, e_short[0]), "batch", 1)),
          [shape(8, w) for w in wide_rest for _ in "ks"]),
         (add_all, (own, parts[2], long_got), [(rows, width)])]
    )
    a_got, b_got = trade(a_send, "batch", 2), trade(b_send, "batch", 4)
    ((feed,),) = small_steps(
        [(add_all, (own, feed[0], *to_tall(feed)), [shape(1, sum(wide))])]
    )
    (a, a_send), (b, b_send) = small_steps(
        [(add_halves, (tied(a, feed), a_got), [shape(4, wide_rest[0])] * 2),
         (add_halves, (b, b_got), [shape(4, wide_rest[1])] * 2)]
    )
    feed = sharing.doubled(feed)
    a_got, b_got = trade(a_send, "batch", 4), trade(b_send, "batch", 2)
    feed_got = to_tall([feed] * 4)
    (rest,) = small_steps([(add_to_pieces, (a, a_got, b, b_got), [shape(1, sum(wide_rest))] * 4)])
    ((fa, fb),) = small_steps(
        [(lay, (tied(feed, rest[0]), *feed_got), [shape(4, w) for w in wide])]
    )
    (rest,), (fa,), (fb,) = small_steps(
        [(add_all, (own, rest[0], *to_tall(rest)), [shape(1, sum(wide_rest))]),
         (join, (fa, trade(fa, "batch", 4)), [shape(8, wide[0])]),
         (join, (fb, trade(fb, "batch", 2)), [shape(8, wide[1])])]
    )
    rest = sharing.doubled(rest)
    (ra, rb), (feed,) = small_steps(
        [(lay, (rest, *to_tall([rest] * 4)), [shape(4, w) for w in wide_rest]),
         (beside, (fa, trade(fa, "batch", 2), fb, trade(fb, "batch", 4)),
          [shape(16, sum(wide))])]
    )
    ra_got, rb_got = trade(ra, "batch", 4), trade(rb, "batch", 2)
    held, *shorts = tied((held, *parts[n:]), ra)
    long_got = hand_down(held, n, 2)
    got = [return_short(shorts[k], n, k, 1) for k in roots]
    e_got = [return_short(tied(e_short[k], ra), n, k, 2) for k in roots]
    (ra,), (rb,), (held,), *shorts = small_steps(
        [(join, (ra, ra_got), [shape(8, wide_rest[0])]),
         (join, (rb, rb_got), [shape(8, wide_rest[1])]),
         (add_all, (own, parts[1], long_got), [(rows, width)])]
        + [(add_all, (own, parts[n + k], got[k]), [(rows, width)]) for k in roots]
        + [(add_all, (own, e_short[k], e_got[k]), [(rows, width)]) for k in roots]
    )
    shorts, e_short = shorts[: n // 4], return_short_rest([v for v, in shorts[n // 4 :]], n)
    ra_got, rb_got = trade(ra, "batch", 2), trade(rb, "batch", 4)
    feed_got = trade(tied(feed, ra), "batch", 1)
    long_got = hand_down(held, n, 1)
    got = [return_short(shorts[k][0], n, k, 2) for k in roots]
    s_up, s_down = call(
        functools.partial(unpack_feed_kernel, [(0, 2, 0, 0, 1), (0, 2, 1, hidden, hidden // width)]),
        (codes, feed, feed_got),
        [(feed_up.shape, WIDE), (feed_down.shape, WIDE)],
        6,
        smem=1,
        room=room,
    )
    (rest,), _, *shorts = small_steps(
        [(beside, (ra, ra_got, rb, rb_got), [shape(16, sum(wide_rest))]),
         (note, (s_down[:8, :128], long_got), [])]
        + [(add_all, (own, shorts[k][0], got[k]), [(rows, width)]) for k in roots]
    )
    shorts = return_short_rest([v for v, in shorts], n)
    rest_got = trade(rest, "batch", 1)
    input_gradient, encoder_gradient = call(
        functools.partial(last_kernel, n),
        (order, ranks, decoder_input, self_grad, own, norm_gains, parts[0], long_got, e_long,
         *shorts, *e_short),
        [(decoder_input.shape, WIDE), (decoder_input.shape, WIDE)],
        3,
        smem=2,
        room=room,
    )
    at = hidden
    places = [(0, 2, 0, 0, 1), (0, 2, 0, 2 * width, 1), (0, 2, 0, 3 * width, 1),
              (0, 2, 1, at, 1), (0, 2, 1, at + 3 * width, 1), (0, 2, 1, at + 4 * width, 1)]
    s_cm, s_cq, s_cout, s_in, s_out, up_bias, down_bias, gains, shifts = call(
        functools.partial(unpack_rest_kernel, places),
        (codes, rest, rest_got),
        [(s, WIDE) for s in (cross_memory.shape, cross_query.shape, cross_outward.shape,
                             self_inward.shape, self_outward.shape, (1, hidden), (1, width),
                             norm_gains.shape, norm_shifts.shape)],
        5,
        scratch=[((width, 128), WIDE)],
        smem=1,
        room=room,
    )
    return (
        layer_output, input_gradient, encoder_gradient, s_in, s_out, s_cq, s_cm, s_cout,
        s_up, up_bias[0], s_down, down_bias[0], gains, shifts,
    )


def solution(mesh):
    blocked = P("batch", "blk", None)
    placed = (blocked, blocked, P("batch"), P("batch", None)) + (P(),) * 11 + (blocked,)
    return jax.shard_map(
        on_device,
        mesh=mesh,
        in_specs=placed,
        out_specs=(blocked,) * 3 + (P(),) * 11,
        check_vma=False,
    )
```
